128 devices in a mesh: row: 8 (over z, core), col: 8 (over x_lo, y), wave: 2 (over x_hi).
Axes of the slice: x: 4 (x_hi: 2, x_lo: 2; x = x_hi * 2 + x_lo), y: 4, z: 4, core: 2. Of those that a mesh axis runs over, the one named last changes fastest.
Arguments:
- transmission: float32 [4096, 4096], P('row', 'col'), may hold values from 0 to 1
- dual_focal: float32 [512, 8, 512], P(('row', 'col'), 'wave'), may hold values from -12 to 12
- dual_curvature: float32 [4096, 4096], P('row', 'col'), may hold values from -6 to 6
- pupil_mask: int32 [4096, 4096], P('row', 'col'), may hold values 0 or 1
- lyot_mask: int32 [4096, 4096], P('row', 'col'), may hold values 0 or 1
- dark_mask: int32 [512, 8, 512], P(('row', 'col'), 'wave'), may hold values 0 or 1
- focal_rows: float32 [8, 512, 4096], P('wave', None, 'row'), may hold values from -0.09375 to 0.09375
- focal_cols: float32 [8, 512, 4096], P('wave', None, 'col'), may hold values from -0.09375 to 0.09375
Outputs:
- transmission_out: float32 [4096, 4096], P('row', 'col')
- dual_focal_out: float32 [512, 8, 512], P(('row', 'col'), 'wave')
- dual_curvature_out: float32 [4096, 4096], P('row', 'col')
The draws below stay inside these ranges and needn't reach their ends.
All inputs are finite; a program needn't handle non-finite values. No bound on the sum of `pupil_mask` or of `lyot_mask` or of `dark_mask` on one device may be relied on, other than what follows from the above.
Results may differ from the reference program's by a relative error of at most 0.0001.
Values sent between devices are 32-bit elements; how exact they have to be, the bound alone decides.
No kernel may reach another device: no remote copies, remote signals or barrier semaphores. Data moves between devices by JAX's collectives and lax.ppermute only.
A program may use at most 64 MiB of HBM per device.

```python
import jax
import jax.numpy as jnp
from jax import lax

N = 4096
Z = 512
NW = 8
ITERS = 2


def with_ends(drawn, stream_key, smallest, high):
    longest = drawn.shape.index(max(drawn.shape))
    spots = []
    for shift in (0, 1):
        where = [jax.random.randint(jax.random.fold_in(stream_key, axis), (), 0, length) for axis, length in enumerate(drawn.shape)]
        where[longest] = (where[longest] + shift) % drawn.shape[longest]
        spots.append(tuple(where))
    return drawn.at[spots[0]].set(smallest).at[spots[1]].set(high)


def steps_of(rng, extent, shards, smallest, high):
    loudness, own = 1.0, jax.random.fold_in(rng, 6)
    for dim, parts in shards:
        steps = jnp.exp(jax.random.uniform(jax.random.fold_in(own, dim), (parts,), jnp.float32, smallest / len(shards), high / len(shards)))
        loudness = loudness * jnp.repeat(steps, extent[dim] // parts).reshape([-1 if axis == dim else 1 for axis in range(len(extent))])
    return loudness


def centred(stream_key, dims, scale, most, pieces=(), held_as=jnp.bfloat16):
    drawn = jax.random.normal(stream_key, dims, jnp.float32) * scale
    if len(pieces) > 0:
        drawn = steps_of(stream_key, dims, pieces, -0.22, 0.18) * drawn
    return jnp.clip(drawn, min=-most, max=most).astype(held_as)


def setup_inputs(seed: int = 0) -> dict:
    splits = jax.random.split(jax.random.key(seed), 9)
    transmission = jnp.clip(1.0 * jax.random.uniform(splits[0], (N, N), jnp.float32) ** steps_of(splits[0], (N, N), ((0, 8), (1, 8)), -0.2, 0.2), 0.0, 1.0)
    dual_focal = centred(splits[1], (Z, NW, Z), 2.0, 12.0, ((0, 64), (1, 2)), jnp.float32)
    dual_curvature = centred(splits[2], (N, N), 1.0, 6.0, ((0, 8), (1, 8)), jnp.float32)
    pupil_mask = with_ends((jax.random.randint(splits[3], (N, N), 0, 8) < 7).astype(jnp.int32), jax.random.fold_in(splits[3], 1), 0, 1)
    lyot_mask = with_ends((jax.random.randint(splits[4], (N, N), 0, 8) < 7).astype(jnp.int32), jax.random.fold_in(splits[4], 1), 0, 1)
    dark_mask = with_ends((jax.random.randint(splits[5], (Z, NW, Z), 0, 2) < 1).astype(jnp.int32), jax.random.fold_in(splits[5], 1), 0, 1)
    focal_rows = centred(splits[6], (NW, Z, N), N ** -0.5, 0.09375, ((0, 2), (2, 8)), jnp.float32)
    focal_cols = centred(splits[7], (NW, Z, N), N ** -0.5, 0.09375, ((0, 2), (2, 8)), jnp.float32)
    return {"transmission": transmission, "dual_focal": dual_focal, "dual_curvature": dual_curvature, "pupil_mask": pupil_mask, "lyot_mask": lyot_mask, "dark_mask": dark_mask, "focal_rows": focal_rows, "focal_cols": focal_cols}


step_primal = 0.12
step_dual = 0.2
contrast = 0.5
curvature_limit = 0.1


def curvature(field):
    padded = jnp.pad(field, 1)
    beside_all = padded[2:, 1:-1] + padded[:-2, 1:-1] + padded[1:-1, 2:] + padded[1:-1, :-2]
    return 0.25 * beside_all - field


def reference(transmission, dual_focal, dual_curvature, pupil_mask, lyot_mask, dark_mask, focal_rows, focal_cols):
    highest = lax.Precision.HIGHEST
    pupil = pupil_mask.astype(jnp.float32)
    stop = pupil * lyot_mask.astype(jnp.float32)
    dark = dark_mask.astype(jnp.float32)
    primal = transmission
    dual_f = dual_focal * dark
    dual_c = dual_curvature

    def back_one(carry, items):
        rows_table, cols_table, field = items
        carried = jnp.dot(field, cols_table, precision=highest, preferred_element_type=jnp.float32)
        return carry + jnp.dot(rows_table.T, carried, precision=highest, preferred_element_type=jnp.float32), None

    def forward_one(carry, items):
        rows_table, cols_table = items
        left = jnp.dot(rows_table, carry, precision=highest, preferred_element_type=jnp.float32)
        return carry, jnp.dot(left, cols_table.T, precision=highest, preferred_element_type=jnp.float32)

    for iteration in range(ITERS):
        start = jnp.zeros((N, N), jnp.float32)
        backward, _ = lax.scan(back_one, start, (focal_rows, focal_cols, jnp.transpose(dual_f, (1, 0, 2))))
        gradient = -pupil + stop * backward + curvature(dual_c)
        primal_new = jnp.clip(primal - step_primal * gradient, 0.0, 1.0)
        extended = 2.0 * primal_new - primal
        _, fields = lax.scan(forward_one, stop * extended, (focal_rows, focal_cols))
        shifted = dual_f + step_dual * jnp.transpose(fields, (1, 0, 2))
        dual_f = dark * (shifted - step_dual * jnp.clip(shifted / step_dual, -contrast, contrast))
        moved = dual_c + step_dual * curvature(extended)
        dual_c = moved - step_dual * jnp.clip(moved / step_dual, -curvature_limit, curvature_limit)
        primal = primal_new
    return primal, dual_f, dual_c
```

```python
import jax
import jax.numpy as jnp
from jax import lax
from jax.sharding import Mesh, PartitionSpec as P

ITERS = 2

step_primal = 0.12
step_dual = 0.2
contrast = 0.5
curvature_limit = 0.1
high = lax.Precision.HIGH

ROW = ("z", "core")
COL = ("xl", "y")
ZS, CORES, COLS, WAVES = 4, 2, 8, 2
CHUNKS = 2


def swap_core(cells):
    return lax.ppermute(cells, "core", [(0, 1), (1, 0)])


def shift_z(cells, by):
    return lax.ppermute(cells, "z", [(i, (i + by) % ZS) for i in range(ZS)])


def halos(cells):
    edges = []
    for axes, count, dim in ((ROW, ZS * CORES, 0), (COL, COLS, 1)):
        head = lax.slice_in_dim(cells, 0, 1, axis=dim)
        tail = lax.slice_in_dim(cells, cells.shape[dim] - 1, cells.shape[dim], axis=dim)
        edges.append(lax.ppermute(tail, axes, [(i, i + 1) for i in range(count - 1)]))
        edges.append(lax.ppermute(head, axes, [(i + 1, i) for i in range(count - 1)]))
    return edges


def curvature(cells, edges):
    above, below, left, right = edges
    down = jnp.concatenate([above, cells[:-1]], axis=0)
    up = jnp.concatenate([cells[1:], below], axis=0)
    after = jnp.concatenate([left, cells[:, :-1]], axis=1)
    before = jnp.concatenate([cells[:, 1:], right], axis=1)
    return 0.25 * (down + up + after + before) - cells


def per_device(
    transmission,
    dual_focal,
    dual_curvature,
    pupil_mask,
    lyot_mask,
    dark_mask,
    focal_rows,
    focal_cols,
):
    z = lax.axis_index("z")
    core = lax.axis_index("core")
    first = core == 0
    waves, fields, rows = focal_rows.shape
    cols = focal_cols.shape[2]
    part = fields // (ZS * CORES)
    own = dual_focal.shape[0]
    half = cols // CORES
    wide = half // CHUNKS

    def halves(cells):
        a, b = cells[..., :half], cells[..., half:]
        return jnp.where(first, a, b), jnp.where(first, b, a)

    def to_half(cells):
        mine, other = halves(cells)
        return jnp.stack([mine, swap_core(other)])

    def from_half(cells):
        mine, other = cells[0], swap_core(cells[1])
        return jnp.concatenate([jnp.where(first, mine, other), jnp.where(first, other, mine)], axis=1)

    def ordered(table):
        blocks = table.reshape(waves, ZS, CORES, part, rows)
        steps = [lax.dynamic_index_in_dim(blocks, (z + step) % ZS, 1, keepdims=False) for step in range(ZS)]
        out = []
        for block in steps:
            a, b = block[:, 0], block[:, 1]
            out.append(jnp.stack([jnp.where(first, a, b), jnp.where(first, b, a)]))
        return jnp.stack(out).reshape(ZS, CORES * waves * part, rows)

    other_rows = swap_core(focal_rows)
    table = jnp.concatenate([ordered(focal_rows), ordered(other_rows)], axis=2)
    cols_mine, cols_other = halves(focal_cols)
    cols_rel = jnp.concatenate([cols_mine, cols_other], axis=2)

    pupil = pupil_mask.astype(jnp.float32)
    stop = pupil * lyot_mask.astype(jnp.float32)
    stop_half = to_half(stop)
    dark = jnp.transpose(dark_mask.astype(jnp.float32), (1, 0, 2))
    primal = transmission
    primal_half = to_half(primal)
    dual_f = jnp.transpose(dual_focal, (1, 0, 2)) * dark
    dual_c = dual_curvature
    for iteration in range(ITERS):
        known_half = to_half(curvature(dual_c, halos(dual_c)) - pupil)

        spread = jnp.broadcast_to(dual_f[None], (COLS,) + dual_f.shape)
        gathered = lax.all_to_all(spread, COL, 0, 0, tiled=True)
        gathered = jnp.transpose(gathered, (1, 0, 2, 3)).reshape(waves, part, fields)
        carried = jnp.einsum("wkv,wvc->wkc", gathered, cols_rel, precision=high)
        carried = carried.reshape(waves * part, cols)
        pair = jnp.concatenate([carried[:, :half], swap_core(carried[:, half:])], axis=0)

        new_half, masked = [], []
        for chunk in range(CHUNKS):
            at = slice(chunk * wide, (chunk + 1) * wide)
            block = pair[:, at]
            blocks = [block, shift_z(block, -1), shift_z(block, -2), shift_z(block, -3)]
            back = jnp.einsum("skr,skc->rc", table, jnp.stack(blocks), precision=high)
            back = back + lax.ppermute(back, "wave", [(0, 1), (1, 0)])
            back = back.reshape(CORES, rows, wide)
            before = primal_half[:, :, at]
            gradient = known_half[:, :, at] + stop_half[:, :, at] * back
            after = jnp.clip(before - step_primal * gradient, 0.0, 1.0)
            new_half.append(after)
            masked.append(stop_half[:, :, at] * (2.0 * after - before))
        sums = []
        for chunk in range(CHUNKS):
            left = jnp.einsum("skr,rc->skc", table, masked[chunk].reshape(CORES * rows, wide), precision=high)
            sums.append(left[0] + shift_z(left[1], 1) + shift_z(left[2], 2) + shift_z(left[3], 3))
        total = jnp.concatenate(sums, axis=1)
        count = waves * part
        total = jnp.concatenate([total[:count], swap_core(total[count:])], axis=1)
        found = jnp.einsum("wkc,wvc->wkv", total.reshape(waves, part, cols), cols_rel, precision=high)
        found = jnp.transpose(found.reshape(waves, COLS, own, fields), (1, 0, 2, 3))
        found = jnp.sum(lax.all_to_all(found, COL, 0, 0, tiled=True), axis=0)
        shifted = dual_f + step_dual * found
        dual_f = dark * (shifted - step_dual * jnp.clip(shifted / step_dual, -contrast, contrast))

        primal_half = jnp.concatenate(new_half, axis=2)
        primal_new = from_half(primal_half)
        extended = 2.0 * primal_new - primal
        moved = dual_c + step_dual * curvature(extended, halos(extended))
        dual_c = moved - step_dual * jnp.clip(moved / step_dual, -curvature_limit, curvature_limit)
        primal = primal_new
    return (primal, jnp.transpose(dual_f, (1, 0, 2)), dual_c)


def solution(mesh):
    parts = Mesh(
        mesh.devices.reshape(ZS, CORES, 2, COLS // 2, WAVES),
        ("z", "core", "xl", "y", "wave"),
    )
    return jax.shard_map(
        per_device,
        mesh=parts,
        in_specs=(
            P(ROW, COL),
            P(ROW + COL, "wave", None),
            P(ROW, COL),
            P(ROW, COL),
            P(ROW, COL),
            P(ROW + COL, "wave", None),
            P("wave", None, ROW),
            P("wave", None, COL),
        ),
        out_specs=(P(ROW, COL), P(ROW + COL, "wave", None), P(ROW, COL)),
        check_vma=False,
    )
```

```python
import functools

import jax
import jax.numpy as jnp
from jax import lax
from jax.experimental import pallas as pl
from jax.experimental.pallas import tpu as pltpu
from jax.sharding import Mesh, PartitionSpec as P

ITERS = 2

step_primal = 0.12
step_dual = 0.2
contrast = 0.5
curvature_limit = 0.1
high = lax.Precision.HIGH

ROW = ("z", "core")
COL = ("xl", "y")
ZS, CORES, COLS, WAVES = 4, 2, 8, 2
CHUNKS = 2
LIMIT = 40 * 1024 * 1024
f32 = jnp.float32
tie = lax.optimization_barrier
in_vmem = pl.BlockSpec(memory_space=pltpu.VMEM)
in_smem = pl.BlockSpec(memory_space=pltpu.SMEM)


def swap_core(cells):
    return lax.ppermute(cells, "core", [(0, 1), (1, 0)])


def shift_z(cells, by):
    return lax.ppermute(cells, "z", [(i, (i + by) % ZS) for i in range(ZS)])


def split(values):
    top = values.astype(jnp.bfloat16)
    return top, (values - top.astype(f32)).astype(jnp.bfloat16)


def dot3(a, b, dims):
    (a1, a2), (b1, b2) = split(a), split(b)
    mul = functools.partial(lax.dot_general, dimension_numbers=(dims, ((), ())), preferred_element_type=f32)
    return mul(a1, b1) + (mul(a1, b2) + mul(a2, b1))


def exchange(edges):
    near, far, head, tail = edges
    pairs = [(i, i + 1) for i in range(1, ZS * CORES - 1, 2)]
    return (
        swap_core(near),
        lax.ppermute(far, ROW, pairs + [(b, a) for a, b in pairs]),
        lax.ppermute(tail, COL, [(i, i + 1) for i in range(COLS - 1)]),
        lax.ppermute(head, COL, [(i + 1, i) for i in range(COLS - 1)]),
    )


def put_edges(first, cells, near_ref, far_ref, head_ref, tail_ref):
    rows, cols = cells.shape
    top, bottom = cells[0:1, :], cells[rows - 1 : rows, :]
    near_ref[...] = jnp.where(first, bottom, top)
    far_ref[...] = jnp.where(first, top, bottom)
    head_ref[...] = jnp.transpose(cells[:, :128])[0:1, :]
    tail_ref[...] = jnp.transpose(cells[:, cols - 128 :])[127:128, :]


def stencil(first, cells, near, far, left, right):
    rows, cols = cells.shape
    above, below = jnp.where(first, far, near), jnp.where(first, near, far)
    row = lax.broadcasted_iota(jnp.int32, cells.shape, 0)
    col = lax.broadcasted_iota(jnp.int32, cells.shape, 1)
    left = jnp.transpose(jnp.broadcast_to(left, (128, rows)))[:, 0:1]
    right = jnp.transpose(jnp.broadcast_to(right, (128, rows)))[:, 0:1]
    down = jnp.where(row == 0, above, pltpu.roll(cells, 1, 0))
    up = jnp.where(row == rows - 1, below, pltpu.roll(cells, rows - 1, 0))
    after = jnp.where(col == 0, left, pltpu.roll(cells, 1, 1))
    before = jnp.where(col == cols - 1, right, pltpu.roll(cells, cols - 1, 1))
    return 0.25 * (down + up + after + before) - cells


def halves(first, cells, mine_ref, other_ref):
    half = cells.shape[1] // 2
    a, b = cells[:, :half], cells[:, half:]
    mine_ref[...] = jnp.where(first, a, b)
    other_ref[...] = jnp.where(first, b, a)


def start_kernel(core, x, yc, pupil_mask, lyot_mask, near, far, head, tail, x_mine, x_other, stop_mine, stop_other):
    first = core[0] == 0
    put_edges(first, yc[...], near, far, head, tail)
    halves(first, x[...], x_mine, x_other)
    halves(first, (pupil_mask[...] * lyot_mask[...]).astype(f32), stop_mine, stop_other)


def known_kernel(core, yc, pupil_mask, near, far, left, right, mine, other):
    first = core[0] == 0
    curved = stencil(first, yc[...], near[...], far[...], left[...], right[...])
    halves(first, curved - pupil_mask[...].astype(f32), mine, other)


def primal_kernel(core, new_a, new_b, far_a, far_b, x, out, near, far, head, tail):
    first = core[0] == 0
    mine = jnp.concatenate([new_a[...], new_b[...]], axis=1)
    other = jnp.concatenate([far_a[...], far_b[...]], axis=1)
    new = jnp.concatenate([jnp.where(first, mine, other), jnp.where(first, other, mine)], axis=1)
    out[...] = new
    put_edges(first, 2.0 * new - x[...], near, far, head, tail)


def dual_kernel(core, new, x, yc, near, far, left, right, out, *edges):
    first = core[0] == 0
    extended = 2.0 * new[...] - x[...]
    curved = stencil(first, extended, near[...], far[...], left[...], right[...])
    moved = yc[...] + step_dual * curved
    result = moved - step_dual * jnp.clip(moved / step_dual, -curvature_limit, curvature_limit)
    out[...] = result
    if edges:
        put_edges(first, result, *edges)


def focal_kernel(parts, yf, dark, out, *spread):
    fields = parts[0]
    for other in range(1, COLS):
        fields = fields + parts[other]
    shifted = yf[...] + step_dual * fields
    result = dark[...] * (shifted - step_dual * jnp.clip(shifted / step_dual, -contrast, contrast))
    out[...] = result
    if spread:
        for other in range(COLS):
            spread[0][other] = result


def carry_kernel(core, y, table, mine, other):
    rows = y.shape[0] * y.shape[2]
    carried = dot3(y[:, 0].reshape(rows, y.shape[3]), table[0], ((1,), (0,)))
    halves(core[0] == 0, carried, mine, other)


def found_kernel(core, own_a, own_b, far_a, far_b, table, out):
    first = core[0] == 0
    own = jnp.concatenate([own_a[...], own_b[...]], axis=1)
    far = jnp.concatenate([far_a[...], far_b[...]], axis=1)
    left = jnp.concatenate([jnp.where(first, own, far), jnp.where(first, far, own)], axis=1)
    found = dot3(left, table[0], ((1,), (1,)))
    out[:, 0] = found.reshape(out.shape[0], out.shape[2], out.shape[3])


def table_kernel(where, mine, other, out):
    rows = mine.shape[3]
    out[0, :, :rows] = mine[:, 0].reshape(out.shape[1], rows)
    out[0, :, rows:] = other[:, 0].reshape(out.shape[1], rows)


def whole(kernel, core, args, shapes):
    return pl.pallas_call(
        kernel,
        out_shape=[jax.ShapeDtypeStruct(shape, f32) for shape in shapes],
        in_specs=[in_smem] + [in_vmem] * len(args) if core is not None else [in_vmem] * len(args),
        out_specs=[in_vmem] * len(shapes),
        compiler_params=pltpu.CompilerParams(vmem_limit_bytes=LIMIT),
    )(*(([core] if core is not None else []) + list(args)))


def per_device(
    transmission,
    dual_focal,
    dual_curvature,
    pupil_mask,
    lyot_mask,
    dark_mask,
    focal_rows,
    focal_cols,
):
    z = lax.axis_index("z").astype(jnp.int32)
    core = lax.axis_index("core").astype(jnp.int32)
    where, core = jnp.stack([z, core]), core[None]
    waves, fields, rows = focal_rows.shape
    cols = focal_cols.shape[2]
    part = fields // (ZS * CORES)
    own = dual_focal.shape[0]
    count = waves * part
    half = cols // CORES
    wide = half // CHUNKS
    tile, line = (rows, cols), [(1, cols)] * 4
    piece = (rows, half)

    dark = jnp.transpose(dark_mask.astype(f32), (1, 0, 2))
    dual_f = jnp.transpose(dual_focal, (1, 0, 2)) * dark
    spread = jnp.broadcast_to(dual_f[None], (COLS,) + dual_f.shape)

    other_rows = swap_core(focal_rows)
    started = whole(
        start_kernel, core, (transmission, dual_curvature, pupil_mask, lyot_mask), line + [piece] * 4
    )
    edges, x_mine, x_other, stop_mine, stop_other = started[:4], *started[4:]

    def block_of(b, where):
        return (0, (where[0] + b // CORES) % ZS * CORES + (where[1] + b) % CORES, 0, 0)

    def table_of(mine, other):
        return pl.pallas_call(
            table_kernel,
            grid_spec=pltpu.PrefetchScalarGridSpec(
                num_scalar_prefetch=1,
                grid=(ZS * CORES,),
                in_specs=[pl.BlockSpec((waves, 1, part, rows), block_of)] * 2,
                out_specs=pl.BlockSpec((1, count, 2 * rows), lambda b, where: (b, 0, 0)),
            ),
            out_shape=jax.ShapeDtypeStruct((ZS * CORES, count, 2 * rows), f32),
            compiler_params=pltpu.CompilerParams(vmem_limit_bytes=LIMIT),
        )(where, mine.reshape(waves, ZS * CORES, part, rows), other.reshape(waves, ZS * CORES, part, rows))

    table = table_of(focal_rows, other_rows).reshape(ZS, CORES * count, CORES * rows)
    primal_half = jnp.concatenate([x_mine, swap_core(x_other)], axis=0)
    stop_half = jnp.concatenate([stop_mine, swap_core(stop_other)], axis=0)

    def known(yc, edges):
        mine, other = whole(known_kernel, core, (yc, pupil_mask, *exchange(edges)), [piece] * 2)
        return jnp.concatenate([mine, swap_core(other)], axis=0)

    def carry(gathered):
        return pl.pallas_call(
            carry_kernel,
            grid=(waves,),
            in_specs=[
                in_smem,
                pl.BlockSpec((COLS, 1, own, fields), lambda w: (0, w, 0, 0)),
                pl.BlockSpec((1, fields, cols), lambda w: (w, 0, 0)),
            ],
            out_specs=[pl.BlockSpec((part, half), lambda w: (w, 0))] * 2,
            out_shape=[jax.ShapeDtypeStruct((count, half), f32)] * 2,
            compiler_params=pltpu.CompilerParams(vmem_limit_bytes=LIMIT),
        )(core, gathered, focal_cols)

    def find(sums, fars):
        return pl.pallas_call(
            found_kernel,
            grid=(waves,),
            in_specs=[in_smem]
            + [pl.BlockSpec((part, wide), lambda w: (w, 0))] * 4
            + [pl.BlockSpec((1, fields, cols), lambda w: (w, 0, 0))],
            out_specs=pl.BlockSpec((COLS, 1, own, fields), lambda w: (0, w, 0, 0)),
            out_shape=jax.ShapeDtypeStruct((COLS, waves, own, fields), f32),
            compiler_params=pltpu.CompilerParams(vmem_limit_bytes=LIMIT),
        )(core, *sums, *fars, focal_cols)

    def gather(block):
        return jnp.stack([block, shift_z(block, -1), shift_z(block, -2), shift_z(block, -3)])

    def backward(full):
        back = jnp.einsum("skr,skc->rc", table, full, precision=high)
        return back, lax.ppermute(back, "wave", [(0, 1), (1, 0)])

    def update(chunk, known_half, back, far):
        at = slice(chunk * wide, (chunk + 1) * wide)
        before = primal_half[:, at]
        after = jnp.clip(before - step_primal * (known_half[:, at] + stop_half[:, at] * (back + far)), 0.0, 1.0)
        return after, stop_half[:, at] * (2.0 * after - before)

    def scatter(masked):
        left = jnp.einsum("skr,rc->skc", table, masked, precision=high)
        return left[0] + shift_z(left[1], 1) + shift_z(left[2], 2) + shift_z(left[3], 3)

    primal, dual_c = transmission, dual_curvature
    for iteration in range(ITERS):
        last = iteration == ITERS - 1
        known_half = known(dual_c, edges)
        mine, other = carry(lax.all_to_all(spread, COL, 0, 0, tiled=True))
        received = swap_core(other)
        pair = jnp.concatenate([mine, received], axis=0)
        full_a, full_b = gather(pair[:, :wide]), gather(pair[:, wide:])
        back_a, far_a = backward(full_a)
        back_b, far_b = backward(full_b)
        far_a, back_b = tie((far_a, back_b))
        new_a, masked_a = tie(update(0, known_half, back_a, far_a))
        sum_a = scatter(masked_a)
        far_b, masked_a = tie((far_b, masked_a))
        new_b, masked_b = tie(update(1, known_half, back_b, far_b))
        sum_b = scatter(masked_b)
        sums = (sum_a[:count], sum_b[:count])
        fars = swap_core(sum_a[count:]), swap_core(sum_b[count:])
        found = find(sums, fars)
        parts = lax.all_to_all(found, COL, 0, 0, tiled=True)
        shapes = [dual_f.shape] + ([] if last else [spread.shape])
        focal = whole(focal_kernel, None, (parts, dual_f, dark), shapes)
        dual_f = focal[0]
        if not last:
            spread = focal[1]

        args = (new_a[:rows], new_b[:rows], swap_core(new_a[rows:]), swap_core(new_b[rows:]), primal)
        primal_new, *edges = whole(primal_kernel, core, args, [tile] + line)
        args = (primal_new, primal, dual_c, *exchange(edges))
        dual_c, *edges = whole(dual_kernel, core, args, [tile] + ([] if last else line))
        primal_half = jnp.concatenate([new_a, new_b], axis=1)
        primal = primal_new
    return (primal, jnp.transpose(dual_f, (1, 0, 2)), dual_c)


def solution(mesh):
    parts = Mesh(
        mesh.devices.reshape(ZS, CORES, 2, COLS // 2, WAVES),
        ("z", "core", "xl", "y", "wave"),
    )
    return jax.shard_map(
        per_device,
        mesh=parts,
        in_specs=(
            P(ROW, COL),
            P(ROW + COL, "wave", None),
            P(ROW, COL),
            P(ROW, COL),
            P(ROW, COL),
            P(ROW + COL, "wave", None),
            P("wave", None, ROW),
            P("wave", None, COL),
        ),
        out_specs=(P(ROW, COL), P(ROW + COL, "wave", None), P(ROW, COL)),
        check_vma=False,
    )
```

```python
import functools

import jax
import jax.numpy as jnp
from jax import lax
from jax.experimental import pallas as pl
from jax.experimental.pallas import tpu as pltpu
from jax.sharding import Mesh, PartitionSpec as P

ITERS = 2

step_primal = 0.12
step_dual = 0.2
contrast = 0.5
curvature_limit = 0.1
high = lax.Precision.HIGH

ROW = ("z", "core")
COL = ("xl", "y")
ZS, CORES, COLS, WAVES = 4, 2, 8, 2
CHUNKS = 2
LIMIT = 40 * 1024 * 1024
f32 = jnp.float32
tie = lax.optimization_barrier
in_vmem = pl.BlockSpec(memory_space=pltpu.VMEM)
in_smem = pl.BlockSpec(memory_space=pltpu.SMEM)


def swap_core(cells):
    return lax.ppermute(cells, "core", [(0, 1), (1, 0)])


def shift_z(cells, by):
    return lax.ppermute(cells, "z", [(i, (i + by) % ZS) for i in range(ZS)])


def split(values):
    top = values.astype(jnp.bfloat16)
    return top, (values - top.astype(f32)).astype(jnp.bfloat16)


def dot3(a, b, dims):
    (a1, a2), (b1, b2) = split(a), split(b)
    mul = functools.partial(lax.dot_general, dimension_numbers=(dims, ((), ())), preferred_element_type=f32)
    return mul(a1, b1) + (mul(a1, b2) + mul(a2, b1))


def exchange(edges):
    near, far, head, tail = edges
    pairs = [(i, i + 1) for i in range(1, ZS * CORES - 1, 2)]
    return (
        swap_core(near),
        lax.ppermute(far, ROW, pairs + [(b, a) for a, b in pairs]),
        lax.ppermute(tail, COL, [(i, i + 1) for i in range(COLS - 1)]),
        lax.ppermute(head, COL, [(i + 1, i) for i in range(COLS - 1)]),
    )


def put_edges(first, cells, near_ref, far_ref, head_ref, tail_ref):
    rows, cols = cells.shape
    top, bottom = cells[0:1, :], cells[rows - 1 : rows, :]
    near_ref[...] = jnp.where(first, bottom, top)
    far_ref[...] = jnp.where(first, top, bottom)
    head_ref[...] = jnp.transpose(cells[:, :128])[0:1, :]
    tail_ref[...] = jnp.transpose(cells[:, cols - 128 :])[127:128, :]


def stencil(first, cells, near, far, left, right):
    rows, cols = cells.shape
    above, below = jnp.where(first, far, near), jnp.where(first, near, far)
    row = lax.broadcasted_iota(jnp.int32, cells.shape, 0)
    col = lax.broadcasted_iota(jnp.int32, cells.shape, 1)
    left = jnp.transpose(jnp.broadcast_to(left, (128, rows)))[:, 0:1]
    right = jnp.transpose(jnp.broadcast_to(right, (128, rows)))[:, 0:1]
    down = jnp.where(row == 0, above, pltpu.roll(cells, 1, 0))
    up = jnp.where(row == rows - 1, below, pltpu.roll(cells, rows - 1, 0))
    after = jnp.where(col == 0, left, pltpu.roll(cells, 1, 1))
    before = jnp.where(col == cols - 1, right, pltpu.roll(cells, cols - 1, 1))
    return 0.25 * (down + up + after + before) - cells


def halves(first, cells, mine_ref, other_ref):
    half = cells.shape[1] // 2
    a, b = cells[:, :half], cells[:, half:]
    mine_ref[...] = jnp.where(first, a, b)
    other_ref[...] = jnp.where(first, b, a)


def start_kernel(core, x, yc, pupil_mask, lyot_mask, near, far, head, tail, x_mine, x_other, stop_mine, stop_other):
    first = core[0] == 0
    put_edges(first, yc[...], near, far, head, tail)
    halves(first, x[...], x_mine, x_other)
    halves(first, (pupil_mask[...] * lyot_mask[...]).astype(f32), stop_mine, stop_other)


def known_kernel(core, yc, pupil_mask, near, far, left, right, mine, other):
    first = core[0] == 0
    curved = stencil(first, yc[...], near[...], far[...], left[...], right[...])
    halves(first, curved - pupil_mask[...].astype(f32), mine, other)


def primal_kernel(core, new_a, new_b, far_a, far_b, x, out, near, far, head, tail):
    first = core[0] == 0
    mine = jnp.concatenate([new_a[...], new_b[...]], axis=1)
    other = jnp.concatenate([far_a[...], far_b[...]], axis=1)
    new = jnp.concatenate([jnp.where(first, mine, other), jnp.where(first, other, mine)], axis=1)
    out[...] = new
    put_edges(first, 2.0 * new - x[...], near, far, head, tail)


def dual_kernel(core, new, x, yc, near, far, left, right, out, *edges):
    first = core[0] == 0
    extended = 2.0 * new[...] - x[...]
    curved = stencil(first, extended, near[...], far[...], left[...], right[...])
    moved = yc[...] + step_dual * curved
    result = moved - step_dual * jnp.clip(moved / step_dual, -curvature_limit, curvature_limit)
    out[...] = result
    if edges:
        put_edges(first, result, *edges)


def focal_kernel(parts, yf, dark, out, *spread):
    fields = parts[0]
    for other in range(1, COLS):
        fields = fields + parts[other]
    shifted = yf[...] + step_dual * fields
    result = dark[...] * (shifted - step_dual * jnp.clip(shifted / step_dual, -contrast, contrast))
    out[...] = result
    if spread:
        for other in range(COLS):
            spread[0][other] = result


def carry_kernel(core, y, table, mine, other):
    rows = y.shape[0] * y.shape[2]
    carried = dot3(y[:, 0].reshape(rows, y.shape[3]), table[0], ((1,), (0,)))
    halves(core[0] == 0, carried, mine, other)


def found_kernel(core, own_a, own_b, far_a, far_b, table, out):
    first = core[0] == 0
    own = jnp.concatenate([own_a[...], own_b[...]], axis=1)
    far = jnp.concatenate([far_a[...], far_b[...]], axis=1)
    left = jnp.concatenate([jnp.where(first, own, far), jnp.where(first, far, own)], axis=1)
    found = dot3(left, table[0], ((1,), (1,)))
    out[:, 0] = found.reshape(out.shape[0], out.shape[2], out.shape[3])


def table_kernel(where, mine, other, out):
    rows = mine.shape[3]
    out[0, :, :rows] = mine[:, 0].reshape(out.shape[1], rows)
    out[0, :, rows:] = other[:, 0].reshape(out.shape[1], rows)


def whole(kernel, core, args, shapes):
    return pl.pallas_call(
        kernel,
        out_shape=[jax.ShapeDtypeStruct(shape, f32) for shape in shapes],
        in_specs=[in_smem] + [in_vmem] * len(args) if core is not None else [in_vmem] * len(args),
        out_specs=[in_vmem] * len(shapes),
        compiler_params=pltpu.CompilerParams(vmem_limit_bytes=LIMIT),
    )(*(([core] if core is not None else []) + list(args)))


def per_device(
    transmission,
    dual_focal,
    dual_curvature,
    pupil_mask,
    lyot_mask,
    dark_mask,
    focal_rows,
    focal_cols,
):
    z = lax.axis_index("z").astype(jnp.int32)
    core = lax.axis_index("core").astype(jnp.int32)
    where, core = jnp.stack([z, core]), core[None]
    waves, fields, rows = focal_rows.shape
    cols = focal_cols.shape[2]
    part = fields // (ZS * CORES)
    own = dual_focal.shape[0]
    count = waves * part
    half = cols // CORES
    wide = half // CHUNKS
    tile, line = (rows, cols), [(1, cols)] * 4
    piece = (rows, half)

    dark = jnp.transpose(dark_mask.astype(f32), (1, 0, 2))
    dual_f = jnp.transpose(dual_focal, (1, 0, 2)) * dark
    spread = jnp.broadcast_to(dual_f[None], (COLS,) + dual_f.shape)

    other_rows = swap_core(focal_rows)
    started = whole(
        start_kernel, core, (transmission, dual_curvature, pupil_mask, lyot_mask), line + [piece] * 4
    )
    edges, x_mine, x_other, stop_mine, stop_other = started[:4], *started[4:]

    def block_of(b, where):
        return (0, (where[0] + b // CORES) % ZS * CORES + (where[1] + b) % CORES, 0, 0)

    def table_of(mine, other):
        return pl.pallas_call(
            table_kernel,
            grid_spec=pltpu.PrefetchScalarGridSpec(
                num_scalar_prefetch=1,
                grid=(ZS * CORES,),
                in_specs=[pl.BlockSpec((waves, 1, part, rows), block_of)] * 2,
                out_specs=pl.BlockSpec((1, count, 2 * rows), lambda b, where: (b, 0, 0)),
            ),
            out_shape=jax.ShapeDtypeStruct((ZS * CORES, count, 2 * rows), f32),
            compiler_params=pltpu.CompilerParams(vmem_limit_bytes=LIMIT),
        )(where, mine.reshape(waves, ZS * CORES, part, rows), other.reshape(waves, ZS * CORES, part, rows))

    table = table_of(focal_rows, other_rows).reshape(ZS, CORES * count, CORES * rows)
    primal_half = jnp.concatenate([x_mine, swap_core(x_other)], axis=0)
    stop_half = jnp.concatenate([stop_mine, swap_core(stop_other)], axis=0)

    def known(yc, around):
        mine, other = whole(known_kernel, core, (yc, pupil_mask, *around), [piece] * 2)
        return jnp.concatenate([mine, swap_core(other)], axis=0)

    def carry(gathered):
        return pl.pallas_call(
            carry_kernel,
            grid=(waves,),
            in_specs=[
                in_smem,
                pl.BlockSpec((COLS, 1, own, fields), lambda w: (0, w, 0, 0)),
                pl.BlockSpec((1, fields, cols), lambda w: (w, 0, 0)),
            ],
            out_specs=[pl.BlockSpec((part, half), lambda w: (w, 0))] * 2,
            out_shape=[jax.ShapeDtypeStruct((count, half), f32)] * 2,
            compiler_params=pltpu.CompilerParams(vmem_limit_bytes=LIMIT),
        )(core, gathered, focal_cols)

    def find(sums, fars):
        return pl.pallas_call(
            found_kernel,
            grid=(waves,),
            in_specs=[in_smem]
            + [pl.BlockSpec((part, wide), lambda w: (w, 0))] * 4
            + [pl.BlockSpec((1, fields, cols), lambda w: (w, 0, 0))],
            out_specs=pl.BlockSpec((COLS, 1, own, fields), lambda w: (0, w, 0, 0)),
            out_shape=jax.ShapeDtypeStruct((COLS, waves, own, fields), f32),
            compiler_params=pltpu.CompilerParams(vmem_limit_bytes=LIMIT),
        )(core, *sums, *fars, focal_cols)

    def gather(block):
        return jnp.stack([block, shift_z(block, -1), shift_z(block, -2), shift_z(block, -3)])

    def backward(full):
        back = jnp.einsum("skr,skc->rc", table, full, precision=high)
        return back, lax.ppermute(back, "wave", [(0, 1), (1, 0)])

    def update(chunk, known_half, back, far):
        at = slice(chunk * wide, (chunk + 1) * wide)
        before = primal_half[:, at]
        after = jnp.clip(before - step_primal * (known_half[:, at] + stop_half[:, at] * (back + far)), 0.0, 1.0)
        return after, stop_half[:, at] * (2.0 * after - before)

    def scatter(masked):
        left = jnp.einsum("skr,rc->skc", table, masked, precision=high)
        return left[0] + shift_z(left[1], 1) + shift_z(left[2], 2) + shift_z(left[3], 3)

    primal, dual_c = transmission, dual_curvature
    gathered = lax.all_to_all(spread, COL, 0, 0, tiled=True)
    known_half = known(dual_c, exchange(edges))
    gathered, known_half, primal_half, stop_half = tie((gathered, known_half, primal_half, stop_half))
    for iteration in range(ITERS):
        last = iteration == ITERS - 1
        mine, other = carry(gathered)
        received = swap_core(other)
        pair = jnp.concatenate([mine, received], axis=0)
        full_a, full_b = gather(pair[:, :wide]), gather(pair[:, wide:])
        back_a, far_a = backward(full_a)
        back_b, far_b = backward(full_b)
        far_a, back_b = tie((far_a, back_b))
        new_a, masked_a = tie(update(0, known_half, back_a, far_a))
        sum_a = scatter(masked_a)
        far_b, masked_a = tie((far_b, masked_a))
        new_b, masked_b = tie(update(1, known_half, back_b, far_b))
        sum_b = scatter(masked_b)

        args = (new_a[:rows], new_b[:rows], swap_core(new_a[rows:]), swap_core(new_b[rows:]), primal)
        primal_new, *edges = whole(primal_kernel, core, args, [tile] + line)
        args = (primal_new, primal, dual_c, *exchange(edges))
        dual_c, *edges = whole(dual_kernel, core, args, [tile] + ([] if last else line))
        primal = primal_new
        sum_a, sum_b, primal, dual_c, *edges = tie((sum_a, sum_b, primal, dual_c, *edges))

        fars = swap_core(sum_a[count:]), swap_core(sum_b[count:])
        parts = lax.all_to_all(find((sum_a[:count], sum_b[:count]), fars), COL, 0, 0, tiled=True)
        if last:
            dual_f = whole(focal_kernel, None, (parts, dual_f, dark), [dual_f.shape])[0]
            break
        primal_half = jnp.concatenate([new_a, new_b], axis=1)
        parts, *around = tie((parts, *exchange(edges)))
        dual_f, spread = whole(focal_kernel, None, (parts, dual_f, dark), [dual_f.shape, spread.shape])
        gathered = lax.all_to_all(spread, COL, 0, 0, tiled=True)
        gathered, known_half = tie((gathered, known(dual_c, around)))
    return (primal, jnp.transpose(dual_f, (1, 0, 2)), dual_c)


def solution(mesh):
    parts = Mesh(
        mesh.devices.reshape(ZS, CORES, 2, COLS // 2, WAVES),
        ("z", "core", "xl", "y", "wave"),
    )
    return jax.shard_map(
        per_device,
        mesh=parts,
        in_specs=(
            P(ROW, COL),
            P(ROW + COL, "wave", None),
            P(ROW, COL),
            P(ROW, COL),
            P(ROW, COL),
            P(ROW + COL, "wave", None),
            P("wave", None, ROW),
            P("wave", None, COL),
        ),
        out_specs=(P(ROW, COL), P(ROW + COL, "wave", None), P(ROW, COL)),
        check_vma=False,
    )
```

```python
import functools

import jax
import jax.numpy as jnp
from jax import lax
from jax.experimental import pallas as pl
from jax.experimental.pallas import tpu as pltpu
from jax.sharding import Mesh, PartitionSpec as P

ITERS = 2

step_primal = 0.12
step_dual = 0.2
contrast = 0.5
curvature_limit = 0.1
high = lax.Precision.HIGH

ROW = ("z", "core")
COL = ("xl", "y")
ZS, CORES, COLS, WAVES = 4, 2, 8, 2
CHUNKS = 2
LIMIT = 16 * 1024 * 1024
f32 = jnp.float32
tie = lax.optimization_barrier
in_vmem = pl.BlockSpec(memory_space=pltpu.VMEM)
in_smem = pl.BlockSpec(memory_space=pltpu.SMEM)


def swap_core(cells):
    return lax.ppermute(cells, "core", [(0, 1), (1, 0)])


def shift_z(cells, by):
    return lax.ppermute(cells, "z", [(i, (i + by) % ZS) for i in range(ZS)])


def split(values):
    top = values.astype(jnp.bfloat16)
    return top, (values - top.astype(f32)).astype(jnp.bfloat16)


def dot3(a, b, dims):
    (a1, a2), (b1, b2) = split(a), split(b)
    mul = functools.partial(lax.dot_general, dimension_numbers=(dims, ((), ())), preferred_element_type=f32)
    return mul(a1, b1) + (mul(a1, b2) + mul(a2, b1))


def exchange(edges):
    near, far, head, tail = edges
    pairs = [(i, i + 1) for i in range(1, ZS * CORES - 1, 2)]
    return (
        swap_core(near),
        lax.ppermute(far, ROW, pairs + [(b, a) for a, b in pairs]),
        lax.ppermute(tail, COL, [(i, i + 1) for i in range(COLS - 1)]),
        lax.ppermute(head, COL, [(i + 1, i) for i in range(COLS - 1)]),
    )


def put_edges(first, cells, near_ref, far_ref, head_ref, tail_ref):
    rows, cols = cells.shape
    top, bottom = cells[0:1, :], cells[rows - 1 : rows, :]
    near_ref[...] = jnp.where(first, bottom, top)
    far_ref[...] = jnp.where(first, top, bottom)
    head_ref[...] = jnp.transpose(cells[:, :128])[0:1, :]
    tail_ref[...] = jnp.transpose(cells[:, cols - 128 :])[127:128, :]


def stencil(first, cells, near, far, left, right):
    rows, cols = cells.shape
    above, below = jnp.where(first, far, near), jnp.where(first, near, far)
    row = lax.broadcasted_iota(jnp.int32, cells.shape, 0)
    col = lax.broadcasted_iota(jnp.int32, cells.shape, 1)
    left = jnp.transpose(jnp.broadcast_to(left, (128, rows)))[:, 0:1]
    right = jnp.transpose(jnp.broadcast_to(right, (128, rows)))[:, 0:1]
    down = jnp.where(row == 0, above, pltpu.roll(cells, 1, 0))
    up = jnp.where(row == rows - 1, below, pltpu.roll(cells, rows - 1, 0))
    after = jnp.where(col == 0, left, pltpu.roll(cells, 1, 1))
    before = jnp.where(col == cols - 1, right, pltpu.roll(cells, cols - 1, 1))
    return 0.25 * (down + up + after + before) - cells


def halves(first, cells, mine_ref, other_ref):
    half = cells.shape[1] // 2
    a, b = cells[:, :half], cells[:, half:]
    mine_ref[...] = jnp.where(first, a, b)
    other_ref[...] = jnp.where(first, b, a)


def start_kernel(core, x, yc, pupil_mask, lyot_mask, near, far, head, tail, x_mine, x_other, stop_mine, stop_other):
    first = core[0] == 0
    put_edges(first, yc[...], near, far, head, tail)
    halves(first, x[...], x_mine, x_other)
    halves(first, (pupil_mask[...] * lyot_mask[...]).astype(f32), stop_mine, stop_other)


def known_kernel(core, yc, pupil_mask, near, far, left, right, mine, other):
    first = core[0] == 0
    curved = stencil(first, yc[...], near[...], far[...], left[...], right[...])
    halves(first, curved - pupil_mask[...].astype(f32), mine, other)


def primal_kernel(core, new_a, new_b, far_a, far_b, x, out, near, far, head, tail):
    first = core[0] == 0
    mine = jnp.concatenate([new_a[...], new_b[...]], axis=1)
    other = jnp.concatenate([far_a[...], far_b[...]], axis=1)
    new = jnp.concatenate([jnp.where(first, mine, other), jnp.where(first, other, mine)], axis=1)
    out[...] = new
    put_edges(first, 2.0 * new - x[...], near, far, head, tail)


def dual_kernel(core, new, x, yc, near, far, left, right, out, *edges):
    first = core[0] == 0
    extended = 2.0 * new[...] - x[...]
    curved = stencil(first, extended, near[...], far[...], left[...], right[...])
    moved = yc[...] + step_dual * curved
    result = moved - step_dual * jnp.clip(moved / step_dual, -curvature_limit, curvature_limit)
    out[...] = result
    if edges:
        put_edges(first, result, *edges)


def focal_kernel(parts, yf, dark, out, *spread):
    fields = parts[0]
    for other in range(1, COLS):
        fields = fields + parts[other]
    shifted = yf[...] + step_dual * fields
    result = dark[...] * (shifted - step_dual * jnp.clip(shifted / step_dual, -contrast, contrast))
    out[...] = result
    if spread:
        for other in range(COLS):
            spread[0][other] = result


def carry_kernel(core, y, table, mine, other):
    rows = y.shape[0] * y.shape[2]
    carried = dot3(y[:, 0].reshape(rows, y.shape[3]), table[0], ((1,), (0,)))
    halves(core[0] == 0, carried, mine, other)


def found_kernel(core, own_a, own_b, far_a, far_b, table, out):
    first = core[0] == 0
    own = jnp.concatenate([own_a[...], own_b[...]], axis=1)
    far = jnp.concatenate([far_a[...], far_b[...]], axis=1)
    left = jnp.concatenate([jnp.where(first, own, far), jnp.where(first, far, own)], axis=1)
    found = dot3(left, table[0], ((1,), (1,)))
    out[:, 0] = found.reshape(out.shape[0], out.shape[2], out.shape[3])


def table_kernel(where, mine, other, out):
    rows = mine.shape[3]
    out[0, :, :rows] = mine[:, 0].reshape(out.shape[1], rows)
    out[0, :, rows:] = other[:, 0].reshape(out.shape[1], rows)


def whole(kernel, core, args, shapes):
    return pl.pallas_call(
        kernel,
        out_shape=[jax.ShapeDtypeStruct(shape, f32) for shape in shapes],
        in_specs=[in_smem] + [in_vmem] * len(args) if core is not None else [in_vmem] * len(args),
        out_specs=[in_vmem] * len(shapes),
        compiler_params=pltpu.CompilerParams(vmem_limit_bytes=LIMIT),
    )(*(([core] if core is not None else []) + list(args)))


def per_device(
    transmission,
    dual_focal,
    dual_curvature,
    pupil_mask,
    lyot_mask,
    dark_mask,
    focal_rows,
    focal_cols,
):
    z = lax.axis_index("z").astype(jnp.int32)
    core = lax.axis_index("core").astype(jnp.int32)
    where, core = jnp.stack([z, core]), core[None]
    waves, fields, rows = focal_rows.shape
    cols = focal_cols.shape[2]
    part = fields // (ZS * CORES)
    own = dual_focal.shape[0]
    count = waves * part
    half = cols // CORES
    wide = half // CHUNKS
    tile, line = (rows, cols), [(1, cols)] * 4
    piece = (rows, half)

    dark = jnp.transpose(dark_mask.astype(f32), (1, 0, 2))
    dual_f = jnp.transpose(dual_focal, (1, 0, 2)) * dark
    spread = jnp.broadcast_to(dual_f[None], (COLS,) + dual_f.shape)

    other_rows = swap_core(focal_rows)
    started = whole(
        start_kernel, core, (transmission, dual_curvature, pupil_mask, lyot_mask), line + [piece] * 4
    )
    edges, x_mine, x_other, stop_mine, stop_other = started[:4], *started[4:]

    def block_of(b, where):
        return (0, (where[0] + b // CORES) % ZS * CORES + (where[1] + b) % CORES, 0, 0)

    def table_of(mine, other):
        return pl.pallas_call(
            table_kernel,
            grid_spec=pltpu.PrefetchScalarGridSpec(
                num_scalar_prefetch=1,
                grid=(ZS * CORES,),
                in_specs=[pl.BlockSpec((waves, 1, part, rows), block_of)] * 2,
                out_specs=pl.BlockSpec((1, count, 2 * rows), lambda b, where: (b, 0, 0)),
            ),
            out_shape=jax.ShapeDtypeStruct((ZS * CORES, count, 2 * rows), f32),
            compiler_params=pltpu.CompilerParams(vmem_limit_bytes=LIMIT),
        )(where, mine.reshape(waves, ZS * CORES, part, rows), other.reshape(waves, ZS * CORES, part, rows))

    table = table_of(focal_rows, other_rows).reshape(ZS, CORES * count, CORES * rows)
    primal_half = jnp.concatenate([x_mine, swap_core(x_other)], axis=0)
    stop_half = jnp.concatenate([stop_mine, swap_core(stop_other)], axis=0)

    def known(yc, around):
        mine, other = whole(known_kernel, core, (yc, pupil_mask, *around), [piece] * 2)
        return jnp.concatenate([mine, swap_core(other)], axis=0)

    def carry(gathered):
        return pl.pallas_call(
            carry_kernel,
            grid=(waves,),
            in_specs=[
                in_smem,
                pl.BlockSpec((COLS, 1, own, fields), lambda w: (0, w, 0, 0)),
                pl.BlockSpec((1, fields, cols), lambda w: (w, 0, 0)),
            ],
            out_specs=[pl.BlockSpec((part, half), lambda w: (w, 0))] * 2,
            out_shape=[jax.ShapeDtypeStruct((count, half), f32)] * 2,
            compiler_params=pltpu.CompilerParams(vmem_limit_bytes=LIMIT),
        )(core, gathered, focal_cols)

    def find(sums, fars):
        return pl.pallas_call(
            found_kernel,
            grid=(waves,),
            in_specs=[in_smem]
            + [pl.BlockSpec((part, wide), lambda w: (w, 0))] * 4
            + [pl.BlockSpec((1, fields, cols), lambda w: (w, 0, 0))],
            out_specs=pl.BlockSpec((COLS, 1, own, fields), lambda w: (0, w, 0, 0)),
            out_shape=jax.ShapeDtypeStruct((COLS, waves, own, fields), f32),
            compiler_params=pltpu.CompilerParams(vmem_limit_bytes=LIMIT),
        )(core, *sums, *fars, focal_cols)

    def gather(block):
        return jnp.stack([block, shift_z(block, -1), shift_z(block, -2), shift_z(block, -3)])

    def backward(full):
        back = jnp.einsum("skr,skc->rc", table, full, precision=high)
        return back, lax.ppermute(back, "wave", [(0, 1), (1, 0)])

    def update(chunk, known_half, back, far):
        at = slice(chunk * wide, (chunk + 1) * wide)
        before = primal_half[:, at]
        after = jnp.clip(before - step_primal * (known_half[:, at] + stop_half[:, at] * (back + far)), 0.0, 1.0)
        return after, stop_half[:, at] * (2.0 * after - before)

    def scatter(masked):
        left = jnp.einsum("skr,rc->skc", table, masked, precision=high)
        return left[0] + shift_z(left[1], 1) + shift_z(left[2], 2) + shift_z(left[3], 3)

    primal, dual_c = transmission, dual_curvature
    gathered = lax.all_to_all(spread, COL, 0, 0, tiled=True)
    known_half = known(dual_c, exchange(edges))
    gathered, known_half, primal_half, stop_half = tie((gathered, known_half, primal_half, stop_half))
    for iteration in range(ITERS):
        last = iteration == ITERS - 1
        mine, other = carry(gathered)
        received = swap_core(other)
        pair = jnp.concatenate([mine, received], axis=0)
        full_a, full_b = gather(pair[:, :wide]), gather(pair[:, wide:])
        back_a, far_a = backward(full_a)
        back_b, far_b = backward(full_b)
        far_a, back_b = tie((far_a, back_b))
        new_a, masked_a = tie(update(0, known_half, back_a, far_a))
        sum_a = scatter(masked_a)
        far_b, masked_a = tie((far_b, masked_a))
        new_b, masked_b = tie(update(1, known_half, back_b, far_b))
        sum_b = scatter(masked_b)

        args = (new_a[:rows], new_b[:rows], swap_core(new_a[rows:]), swap_core(new_b[rows:]), primal)
        primal_new, *edges = whole(primal_kernel, core, args, [tile] + line)
        args = (primal_new, primal, dual_c, *exchange(edges))
        dual_c, *edges = whole(dual_kernel, core, args, [tile] + ([] if last else line))
        primal = primal_new
        sum_a, sum_b, primal, dual_c, *edges = tie((sum_a, sum_b, primal, dual_c, *edges))

        fars = swap_core(sum_a[count:]), swap_core(sum_b[count:])
        parts = lax.all_to_all(find((sum_a[:count], sum_b[:count]), fars), COL, 0, 0, tiled=True)
        if last:
            dual_f = whole(focal_kernel, None, (parts, dual_f, dark), [dual_f.shape])[0]
            break
        primal_half = jnp.concatenate([new_a, new_b], axis=1)
        parts, *around = tie((parts, *exchange(edges)))
        dual_f, spread = whole(focal_kernel, None, (parts, dual_f, dark), [dual_f.shape, spread.shape])
        gathered = lax.all_to_all(spread, COL, 0, 0, tiled=True)
        gathered, known_half = tie((gathered, known(dual_c, around)))
    return (primal, jnp.transpose(dual_f, (1, 0, 2)), dual_c)


def solution(mesh):
    parts = Mesh(
        mesh.devices.reshape(ZS, CORES, 2, COLS // 2, WAVES),
        ("z", "core", "xl", "y", "wave"),
    )
    return jax.shard_map(
        per_device,
        mesh=parts,
        in_specs=(
            P(ROW, COL),
            P(ROW + COL, "wave", None),
            P(ROW, COL),
            P(ROW, COL),
            P(ROW, COL),
            P(ROW + COL, "wave", None),
            P("wave", None, ROW),
            P("wave", None, COL),
        ),
        out_specs=(P(ROW, COL), P(ROW + COL, "wave", None), P(ROW, COL)),
        check_vma=False,
    )
```

```python
import functools

import jax
import jax.numpy as jnp
from jax import lax
from jax.experimental import pallas as pl
from jax.experimental.pallas import tpu as pltpu
from jax.sharding import Mesh, PartitionSpec as P

ITERS = 2

step_primal = 0.12
step_dual = 0.2
contrast = 0.5
curvature_limit = 0.1

ROW = ("z", "core")
COL = ("xl", "y")
ZS, CORES, COLS, WAVES = 4, 2, 8, 2
CHUNKS = 2
LIMIT = 24 * 1024 * 1024
f32 = jnp.float32
tie = lax.optimization_barrier
in_vmem = pl.BlockSpec(memory_space=pltpu.VMEM)
in_smem = pl.BlockSpec(memory_space=pltpu.SMEM)
in_hbm = pl.BlockSpec(memory_space=pltpu.HBM)
bf16 = jnp.bfloat16


def swap_core(cells):
    return lax.ppermute(cells, "core", [(0, 1), (1, 0)])


def shift_z(cells, by):
    return lax.ppermute(cells, "z", [(i, (i + by) % ZS) for i in range(ZS)])


def split(values):
    top = values.astype(jnp.bfloat16)
    return top, (values - top.astype(f32)).astype(jnp.bfloat16)


def dot3(a, b, dims):
    (a1, a2), (b1, b2) = split(a), split(b)
    mul = functools.partial(lax.dot_general, dimension_numbers=(dims, ((), ())), preferred_element_type=f32)
    return mul(a1, b1) + (mul(a1, b2) + mul(a2, b1))


def exchange(edges):
    near, far, head, tail = edges
    pairs = [(i, i + 1) for i in range(1, ZS * CORES - 1, 2)]
    return (
        swap_core(near),
        lax.ppermute(far, ROW, pairs + [(b, a) for a, b in pairs]),
        lax.ppermute(tail, COL, [(i, i + 1) for i in range(COLS - 1)]),
        lax.ppermute(head, COL, [(i + 1, i) for i in range(COLS - 1)]),
    )


def put_edges(first, cells, near_ref, far_ref, head_ref, tail_ref):
    rows, cols = cells.shape
    top, bottom = cells[0:1, :], cells[rows - 1 : rows, :]
    near_ref[...] = jnp.where(first, bottom, top)
    far_ref[...] = jnp.where(first, top, bottom)
    head_ref[...] = jnp.transpose(cells[:, :128])[0:1, :]
    tail_ref[...] = jnp.transpose(cells[:, cols - 128 :])[127:128, :]


def stencil(first, cells, near, far, left, right):
    rows, cols = cells.shape
    above, below = jnp.where(first, far, near), jnp.where(first, near, far)
    row = lax.broadcasted_iota(jnp.int32, cells.shape, 0)
    col = lax.broadcasted_iota(jnp.int32, cells.shape, 1)
    left = jnp.transpose(jnp.broadcast_to(left, (128, rows)))[:, 0:1]
    right = jnp.transpose(jnp.broadcast_to(right, (128, rows)))[:, 0:1]
    down = jnp.where(row == 0, above, pltpu.roll(cells, 1, 0))
    up = jnp.where(row == rows - 1, below, pltpu.roll(cells, rows - 1, 0))
    after = jnp.where(col == 0, left, pltpu.roll(cells, 1, 1))
    before = jnp.where(col == cols - 1, right, pltpu.roll(cells, cols - 1, 1))
    return 0.25 * (down + up + after + before) - cells


def halves(first, cells, mine_ref, other_ref, turn=True):
    half = cells.shape[1] // 2
    a, b = cells[:, :half], cells[:, half:]
    mine, other = jnp.where(first, a, b), jnp.where(first, b, a)
    mine_ref[...] = jnp.transpose(mine) if turn else mine
    other_ref[...] = jnp.transpose(other) if turn else other


def start_kernel(core, x, yc, pupil_mask, lyot_mask, near, far, head, tail, x_mine, x_other, stop_mine, stop_other):
    first = core[0] == 0
    put_edges(first, yc[...], near, far, head, tail)
    halves(first, x[...], x_mine, x_other)
    halves(first, (pupil_mask[...] * lyot_mask[...]).astype(f32), stop_mine, stop_other)


def known_kernel(core, yc, pupil_mask, near, far, left, right, mine, other):
    first = core[0] == 0
    curved = stencil(first, yc[...], near[...], far[...], left[...], right[...])
    halves(first, curved - pupil_mask[...].astype(f32), mine, other)


def primal_kernel(core, new_a, new_b, far_a, far_b, x, out, near, far, head, tail):
    first = core[0] == 0
    mine = jnp.transpose(jnp.concatenate([new_a[...], new_b[...]], axis=0))
    other = jnp.transpose(jnp.concatenate([far_a[...], far_b[...]], axis=0))
    new = jnp.concatenate([jnp.where(first, mine, other), jnp.where(first, other, mine)], axis=1)
    out[...] = new
    put_edges(first, 2.0 * new - x[...], near, far, head, tail)


def dual_kernel(core, new, x, yc, near, far, left, right, out, *edges):
    first = core[0] == 0
    extended = 2.0 * new[...] - x[...]
    curved = stencil(first, extended, near[...], far[...], left[...], right[...])
    moved = yc[...] + step_dual * curved
    result = moved - step_dual * jnp.clip(moved / step_dual, -curvature_limit, curvature_limit)
    out[...] = result
    if edges:
        put_edges(first, result, *edges)


def focal_kernel(parts, yf, dark, out, *spread):
    fields = parts[0]
    for other in range(1, COLS):
        fields = fields + parts[other]
    shifted = yf[...] + step_dual * fields
    result = dark[...] * (shifted - step_dual * jnp.clip(shifted / step_dual, -contrast, contrast))
    out[...] = result
    if spread:
        for other in range(COLS):
            spread[0][other] = result


def fetch(pairs, sems):
    copies = [pltpu.make_async_copy(src, dst, sems.at[i]) for i, (src, dst) in enumerate(pairs)]
    for copy in copies:
        copy.start()
    return copies


def carry_kernel(core, y, table, mine, other, held, sems):
    waves, rows = y.shape[1], y.shape[0] * y.shape[2]
    copies = fetch([(table.at[w], held.at[w]) for w in range(waves)], sems)
    for w in range(waves):
        copies[w].wait()
        carried = dot3(y[:, w].reshape(rows, y.shape[3]), held[w], ((1,), (0,)))
        at = pl.ds(w * rows, rows)
        halves(core[0] == 0, carried, mine.at[at], other.at[at], turn=False)


def found_kernel(core, own_a, own_b, far_a, far_b, table, out, held, sems):
    first = core[0] == 0
    waves, rows = out.shape[1], out.shape[0] * out.shape[2]
    copies = fetch([(table.at[w], held.at[w]) for w in range(waves)], sems)
    for w in range(waves):
        at = pl.ds(w * rows, rows)
        own = jnp.concatenate([own_a[at, :], own_b[at, :]], axis=1)
        far = jnp.concatenate([far_a[at, :], far_b[at, :]], axis=1)
        left = jnp.concatenate([jnp.where(first, own, far), jnp.where(first, far, own)], axis=1)
        copies[w].wait()
        found = dot3(left, held[w], ((1,), (1,)))
        out[:, w] = found.reshape(out.shape[0], out.shape[2], out.shape[3])


def table_kernel(where, mine, other, top, rest):
    rows = mine.shape[3]
    for at, block in ((0, mine), (rows, other)):
        a, b = split(block[:, 0].reshape(top.shape[1], rows))
        top[0, :, at : at + rows] = a
        rest[0, :, at : at + rows] = b


def fetch_table(top, rest, held_top, held_rest, sems):
    pairs = []
    for b in range(top.shape[0]):
        pairs += [(top.at[b], held_top.at[b]), (rest.at[b], held_rest.at[b])]
    return fetch(pairs, sems)


def back_kernel(t0, t1, t2, t3, top, rest, out, held_top, held_rest, sems):
    copies = fetch_table(top, rest, held_top, held_rest, sems)
    for step, t in enumerate((t0, t1, t2, t3)):
        depth, wide = t.shape
        a, b = split(jnp.transpose(t[...]))
        for copy in copies[4 * step : 4 * step + 4]:
            copy.wait()
        blocks = slice(2 * step, 2 * step + 2)
        both = jnp.dot(
            jnp.concatenate([a, b], axis=0),
            held_top[blocks].reshape(depth, out.shape[1]),
            preferred_element_type=f32,
        )
        more = jnp.dot(a, held_rest[blocks].reshape(depth, out.shape[1]), preferred_element_type=f32)
        part = both[:wide] + (both[wide:] + more)
        out[...] = part if step == 0 else out[...] + part


def update_kernel(
    back, far, x0, x1, s0, s1, k0, k1, top, rest, new0, new1, l0, l1, l2, l3, held_top, held_rest, sems
):
    copies = fetch_table(top, rest, held_top, held_rest, sems)
    rows = x0.shape[1]
    masked = []
    for i, (x, stop, known, new) in enumerate(((x0, s0, k0, new0), (x1, s1, k1, new1))):
        at = slice(i * rows, (i + 1) * rows)
        before = x[...]
        gradient = known[...] + stop[...] * (back[:, at] + far[:, at])
        after = jnp.clip(before - step_primal * gradient, 0.0, 1.0)
        new[...] = after
        masked.append(stop[...] * (2.0 * after - before))
    a, b = split(jnp.concatenate(masked, axis=1))
    both, wide = jnp.concatenate([a, b], axis=0), a.shape[0]
    dims = (((1,), (1,)), ((), ()))
    for step, left in enumerate((l0, l1, l2, l3)):
        for copy in copies[4 * step : 4 * step + 4]:
            copy.wait()
        depth = left.shape[0]
        blocks = slice(2 * step, 2 * step + 2)
        large = held_top[blocks].reshape(depth, both.shape[1])
        small = held_rest[blocks].reshape(depth, both.shape[1])
        one = lax.dot_general(large, both, dims, preferred_element_type=f32)
        two = lax.dot_general(small, a, dims, preferred_element_type=f32)
        left[...] = one[:, :wide] + (one[:, wide:] + two)


def whole(kernel, core, args, shapes):
    return pl.pallas_call(
        kernel,
        out_shape=[jax.ShapeDtypeStruct(shape, f32) for shape in shapes],
        in_specs=[in_smem] + [in_vmem] * len(args) if core is not None else [in_vmem] * len(args),
        out_specs=[in_vmem] * len(shapes),
        compiler_params=pltpu.CompilerParams(vmem_limit_bytes=LIMIT),
    )(*(([core] if core is not None else []) + list(args)))


def per_device(
    transmission,
    dual_focal,
    dual_curvature,
    pupil_mask,
    lyot_mask,
    dark_mask,
    focal_rows,
    focal_cols,
):
    z = lax.axis_index("z").astype(jnp.int32)
    core = lax.axis_index("core").astype(jnp.int32)
    where, core = jnp.stack([z, core]), core[None]
    waves, fields, rows = focal_rows.shape
    cols = focal_cols.shape[2]
    part = fields // (ZS * CORES)
    own = dual_focal.shape[0]
    count = waves * part
    half = cols // CORES
    wide = half // CHUNKS
    tile, line = (rows, cols), [(1, cols)] * 4
    piece = (half, rows)

    dark = jnp.transpose(dark_mask.astype(f32), (1, 0, 2))
    dual_f = jnp.transpose(dual_focal, (1, 0, 2)) * dark
    spread = jnp.broadcast_to(dual_f[None], (COLS,) + dual_f.shape)

    other_rows = swap_core(focal_rows)
    started = whole(
        start_kernel, core, (transmission, dual_curvature, pupil_mask, lyot_mask), line + [piece] * 4
    )
    edges, x_mine, x_other, stop_mine, stop_other = started[:4], *started[4:]

    def block_of(b, where):
        return (0, (where[0] + b // CORES) % ZS * CORES + (where[1] + b) % CORES, 0, 0)

    def table_of(mine, other):
        return pl.pallas_call(
            table_kernel,
            grid_spec=pltpu.PrefetchScalarGridSpec(
                num_scalar_prefetch=1,
                grid=(ZS * CORES,),
                in_specs=[pl.BlockSpec((waves, 1, part, rows), block_of)] * 2,
                out_specs=[pl.BlockSpec((1, count, 2 * rows), lambda b, where: (b, 0, 0))] * 2,
            ),
            out_shape=[jax.ShapeDtypeStruct((ZS * CORES, count, 2 * rows), bf16)] * 2,
            compiler_params=pltpu.CompilerParams(vmem_limit_bytes=LIMIT),
        )(where, mine.reshape(waves, ZS * CORES, part, rows), other.reshape(waves, ZS * CORES, part, rows))

    table = table_of(focal_rows, other_rows)
    primal_half = (x_mine, swap_core(x_other))
    stop_half = (stop_mine, swap_core(stop_other))
    held_table = [pltpu.VMEM((ZS * CORES, count, 2 * rows), bf16)] * 2 + [
        pltpu.SemaphoreType.DMA((2 * ZS * CORES,))
    ]
    held_cols = [pltpu.VMEM((waves, fields, cols), f32), pltpu.SemaphoreType.DMA((waves,))]

    def known(yc, around):
        mine, other = whole(known_kernel, core, (yc, pupil_mask, *around), [piece] * 2)
        return mine, swap_core(other)

    def streamed(kernel, args, shapes, scratch, specs):
        return pl.pallas_call(
            kernel,
            grid=(1,),
            in_specs=specs,
            out_specs=[in_vmem] * len(shapes),
            out_shape=[jax.ShapeDtypeStruct(shape, f32) for shape in shapes],
            scratch_shapes=scratch,
            compiler_params=pltpu.CompilerParams(vmem_limit_bytes=LIMIT),
        )(*args)

    def carry(gathered):
        specs = [in_smem, in_vmem, in_hbm]
        return streamed(carry_kernel, (core, gathered, focal_cols), [(count, half)] * 2, held_cols, specs)

    def find(sums, fars):
        specs = [in_smem, in_vmem, in_vmem, in_vmem, in_vmem, in_hbm]
        args = (core, *sums, *fars, focal_cols)
        return streamed(found_kernel, args, [(COLS, waves, own, fields)], held_cols, specs)[0]

    def gather(block):
        return block, shift_z(block, -1), shift_z(block, -2), shift_z(block, -3)

    def backward(full):
        specs = [in_vmem] * 4 + [in_hbm] * 2
        back = streamed(back_kernel, (*full, *table), [(wide, CORES * rows)], held_table, specs)[0]
        return back, lax.ppermute(back, "wave", [(0, 1), (1, 0)])

    def update(chunk, known_half, back, far):
        cut = pl.BlockSpec((wide, rows), lambda i: (chunk, 0))
        specs = [in_vmem] * 2 + [cut] * 6 + [in_hbm] * 2
        args = (back, far, *primal_half, *stop_half, *known_half, *table)
        shapes = [(wide, rows)] * 2 + [(CORES * count, wide)] * ZS
        new0, new1, *left = streamed(update_kernel, args, shapes, held_table, specs)
        return (new0, new1), left

    def scatter(left):
        return left[0] + shift_z(left[1], 1) + shift_z(left[2], 2) + shift_z(left[3], 3)

    primal, dual_c = transmission, dual_curvature
    gathered = lax.all_to_all(spread, COL, 0, 0, tiled=True)
    gathered, *around = tie((gathered, *exchange(edges)))
    known_half = known(dual_c, around)
    for iteration in range(ITERS):
        last = iteration == ITERS - 1
        mine, other = carry(gathered)
        received = swap_core(other)
        pair = jnp.concatenate([mine, received], axis=0)
        full_a, full_b = gather(pair[:, :wide]), gather(pair[:, wide:])
        back_a, far_a = backward(full_a)
        back_b, far_b = backward(full_b)
        far_a, back_b = tie((far_a, back_b))
        new_a, left_a = update(0, known_half, back_a, far_a)
        sum_a = scatter(left_a)
        far_b, new_a = tie((far_b, new_a))
        new_b, left_b = update(1, known_half, back_b, far_b)
        sum_b = scatter(left_b)

        args = (new_a[0], new_b[0], swap_core(new_a[1]), swap_core(new_b[1]), primal)
        primal_new, *edges = whole(primal_kernel, core, args, [tile] + line)
        args = (primal_new, primal, dual_c, *exchange(edges))
        dual_c, *edges = whole(dual_kernel, core, args, [tile] + ([] if last else line))
        primal = primal_new
        sum_a, sum_b, primal, dual_c, *edges = tie((sum_a, sum_b, primal, dual_c, *edges))

        fars = swap_core(sum_a[count:]), swap_core(sum_b[count:])
        parts = lax.all_to_all(find((sum_a[:count], sum_b[:count]), fars), COL, 0, 0, tiled=True)
        if last:
            dual_f = whole(focal_kernel, None, (parts, dual_f, dark), [dual_f.shape])[0]
            break
        primal_half = tuple(jnp.concatenate(pieces, axis=0) for pieces in zip(new_a, new_b))
        parts, *around = tie((parts, *exchange(edges)))
        dual_f, spread = whole(focal_kernel, None, (parts, dual_f, dark), [dual_f.shape, spread.shape])
        gathered = lax.all_to_all(spread, COL, 0, 0, tiled=True)
        gathered, known_half = tie((gathered, known(dual_c, around)))
    return (primal, jnp.transpose(dual_f, (1, 0, 2)), dual_c)


def solution(mesh):
    parts = Mesh(
        mesh.devices.reshape(ZS, CORES, 2, COLS // 2, WAVES),
        ("z", "core", "xl", "y", "wave"),
    )
    return jax.shard_map(
        per_device,
        mesh=parts,
        in_specs=(
            P(ROW, COL),
            P(ROW + COL, "wave", None),
            P(ROW, COL),
            P(ROW, COL),
            P(ROW, COL),
            P(ROW + COL, "wave", None),
            P("wave", None, ROW),
            P("wave", None, COL),
        ),
        out_specs=(P(ROW, COL), P(ROW + COL, "wave", None), P(ROW, COL)),
        check_vma=False,
    )
```

```python
import functools

import jax
import jax.numpy as jnp
from jax import lax
from jax.experimental import pallas as pl
from jax.experimental.pallas import tpu as pltpu
from jax.sharding import Mesh, PartitionSpec as P

ITERS = 2

step_primal = 0.12
step_dual = 0.2
contrast = 0.5
curvature_limit = 0.1

ROW = ("z", "core")
COL = ("xl", "y")
ZS, CORES, COLS, WAVES = 4, 2, 8, 2
CHUNKS = 2
LIMIT = 24 * 1024 * 1024
f32 = jnp.float32
tie = lax.optimization_barrier
in_vmem = pl.BlockSpec(memory_space=pltpu.VMEM)
in_smem = pl.BlockSpec(memory_space=pltpu.SMEM)
in_hbm = pl.BlockSpec(memory_space=pltpu.HBM)
bf16 = jnp.bfloat16


def stay(cells):
    return pltpu.with_memory_space_constraint(cells, pltpu.HBM)


def cost(moved):
    return pl.CostEstimate(flops=0, bytes_accessed=moved, transcendentals=0)


def swap_core(cells):
    return lax.ppermute(cells, "core", [(0, 1), (1, 0)])


def shift_z(cells, by):
    return lax.ppermute(cells, "z", [(i, (i + by) % ZS) for i in range(ZS)])


def split(values):
    top = values.astype(jnp.bfloat16)
    return top, (values - top.astype(f32)).astype(jnp.bfloat16)


def dot3(a, b, dims):
    (a1, a2), (b1, b2) = split(a), split(b)
    mul = functools.partial(lax.dot_general, dimension_numbers=(dims, ((), ())), preferred_element_type=f32)
    return mul(a1, b1) + (mul(a1, b2) + mul(a2, b1))


def exchange(edges):
    near, far, head, tail = edges
    pairs = [(i, i + 1) for i in range(1, ZS * CORES - 1, 2)]
    return (
        swap_core(near),
        lax.ppermute(far, ROW, pairs + [(b, a) for a, b in pairs]),
        lax.ppermute(tail, COL, [(i, i + 1) for i in range(COLS - 1)]),
        lax.ppermute(head, COL, [(i + 1, i) for i in range(COLS - 1)]),
    )


def put_edges(first, cells, near_ref, far_ref, head_ref, tail_ref):
    rows, cols = cells.shape
    top, bottom = cells[0:1, :], cells[rows - 1 : rows, :]
    near_ref[...] = jnp.where(first, bottom, top)
    far_ref[...] = jnp.where(first, top, bottom)
    head_ref[...] = jnp.transpose(cells[:, :128])[0:1, :]
    tail_ref[...] = jnp.transpose(cells[:, cols - 128 :])[127:128, :]


def stencil(first, cells, near, far, left, right):
    rows, cols = cells.shape
    above, below = jnp.where(first, far, near), jnp.where(first, near, far)
    row = lax.broadcasted_iota(jnp.int32, cells.shape, 0)
    col = lax.broadcasted_iota(jnp.int32, cells.shape, 1)
    left = jnp.transpose(jnp.broadcast_to(left, (128, rows)))[:, 0:1]
    right = jnp.transpose(jnp.broadcast_to(right, (128, rows)))[:, 0:1]
    down = jnp.where(row == 0, above, pltpu.roll(cells, 1, 0))
    up = jnp.where(row == rows - 1, below, pltpu.roll(cells, rows - 1, 0))
    after = jnp.where(col == 0, left, pltpu.roll(cells, 1, 1))
    before = jnp.where(col == cols - 1, right, pltpu.roll(cells, cols - 1, 1))
    return 0.25 * (down + up + after + before) - cells


def halves(first, cells, mine_ref, other_ref, turn=True):
    half = cells.shape[1] // 2
    a, b = cells[:, :half], cells[:, half:]
    mine, other = jnp.where(first, a, b), jnp.where(first, b, a)
    mine_ref[...] = jnp.transpose(mine) if turn else mine
    other_ref[...] = jnp.transpose(other) if turn else other


def start_kernel(core, yc, x, pupil_mask, lyot_mask, *refs):
    near, far, head, tail, x_mine, x_other, stop_mine, stop_other, *held, sems = refs
    first = core[0] == 0
    copies = fetch(list(zip((yc, x, pupil_mask, lyot_mask), held)), sems)
    copies[0].wait()
    put_edges(first, held[0][...], near, far, head, tail)
    copies[1].wait()
    halves(first, held[1][...], x_mine, x_other)
    copies[2].wait()
    copies[3].wait()
    halves(first, (held[2][...] * held[3][...]).astype(f32), stop_mine, stop_other)


def known_kernel(core, yc, pupil_mask, near, far, left, right, mine, other):
    first = core[0] == 0
    curved = stencil(first, yc[...], near[...], far[...], left[...], right[...])
    halves(first, curved - pupil_mask[...].astype(f32), mine, other)


def primal_kernel(core, new_a, new_b, far_a, far_b, x, out, near, far, head, tail):
    first = core[0] == 0
    mine = jnp.transpose(jnp.concatenate([new_a[...], new_b[...]], axis=0))
    other = jnp.transpose(jnp.concatenate([far_a[...], far_b[...]], axis=0))
    new = jnp.concatenate([jnp.where(first, mine, other), jnp.where(first, other, mine)], axis=1)
    out[...] = new
    put_edges(first, 2.0 * new - x[...], near, far, head, tail)


def dual_kernel(core, new, x, yc, near, far, left, right, out, *edges):
    first = core[0] == 0
    extended = 2.0 * new[...] - x[...]
    curved = stencil(first, extended, near[...], far[...], left[...], right[...])
    moved = yc[...] + step_dual * curved
    result = moved - step_dual * jnp.clip(moved / step_dual, -curvature_limit, curvature_limit)
    out[...] = result
    if edges:
        put_edges(first, result, *edges)


def focal_kernel(parts, yf, dark, out, *spread):
    fields = parts[0]
    for other in range(1, COLS):
        fields = fields + parts[other]
    shifted = yf[...] + step_dual * fields
    result = dark[...] * (shifted - step_dual * jnp.clip(shifted / step_dual, -contrast, contrast))
    out[...] = result
    if spread:
        for other in range(COLS):
            spread[0][other] = result


def fetch(pairs, sems):
    copies = [pltpu.make_async_copy(src, dst, sems.at[i]) for i, (src, dst) in enumerate(pairs)]
    for copy in copies:
        copy.start()
    return copies


def carry_kernel(core, y, table, mine, other, held, sems):
    waves, rows = y.shape[1], y.shape[0] * y.shape[2]
    copies = fetch([(table.at[w], held.at[w]) for w in range(waves)], sems)
    for w in range(waves):
        copies[w].wait()
        carried = dot3(y[:, w].reshape(rows, y.shape[3]), held[w], ((1,), (0,)))
        at = pl.ds(w * rows, rows)
        halves(core[0] == 0, carried, mine.at[at], other.at[at], turn=False)


def found_kernel(core, own_a, own_b, far_a, far_b, table, out, held, sems):
    first = core[0] == 0
    waves, rows = out.shape[1], out.shape[0] * out.shape[2]
    copies = fetch([(table.at[w], held.at[w]) for w in range(waves)], sems)
    for w in range(waves):
        at = pl.ds(w * rows, rows)
        own = jnp.concatenate([own_a[at, :], own_b[at, :]], axis=1)
        far = jnp.concatenate([far_a[at, :], far_b[at, :]], axis=1)
        left = jnp.concatenate([jnp.where(first, own, far), jnp.where(first, far, own)], axis=1)
        copies[w].wait()
        found = dot3(left, held[w], ((1,), (1,)))
        out[:, w] = found.reshape(out.shape[0], out.shape[2], out.shape[3])


def table_kernel(where, mine, other, top, rest):
    rows = mine.shape[3]
    for at, block in ((0, mine), (rows, other)):
        a, b = split(block[:, 0].reshape(top.shape[1], rows))
        top[0, :, at : at + rows] = a
        rest[0, :, at : at + rows] = b


def fetch_table(top, rest, held_top, held_rest, sems):
    pairs = []
    for b in range(top.shape[0]):
        pairs += [(top.at[b], held_top.at[b]), (rest.at[b], held_rest.at[b])]
    return fetch(pairs, sems)


def back_kernel(t0, t1, t2, t3, top, rest, out, held_top, held_rest, sems):
    copies = fetch_table(top, rest, held_top, held_rest, sems)
    for step, t in enumerate((t0, t1, t2, t3)):
        depth, wide = t.shape
        a, b = split(jnp.transpose(t[...]))
        for copy in copies[4 * step : 4 * step + 4]:
            copy.wait()
        blocks = slice(2 * step, 2 * step + 2)
        both = jnp.dot(
            jnp.concatenate([a, b], axis=0),
            held_top[blocks].reshape(depth, out.shape[1]),
            preferred_element_type=f32,
        )
        more = jnp.dot(a, held_rest[blocks].reshape(depth, out.shape[1]), preferred_element_type=f32)
        part = both[:wide] + (both[wide:] + more)
        out[...] = part if step == 0 else out[...] + part


def update_kernel(
    back, far, x0, x1, s0, s1, k0, k1, top, rest, new0, new1, l0, l1, l2, l3, held_top, held_rest, sems
):
    copies = fetch_table(top, rest, held_top, held_rest, sems)
    rows = x0.shape[1]
    masked = []
    for i, (x, stop, known, new) in enumerate(((x0, s0, k0, new0), (x1, s1, k1, new1))):
        at = slice(i * rows, (i + 1) * rows)
        before = x[...]
        gradient = known[...] + stop[...] * (back[:, at] + far[:, at])
        after = jnp.clip(before - step_primal * gradient, 0.0, 1.0)
        new[...] = after
        masked.append(stop[...] * (2.0 * after - before))
    a, b = split(jnp.concatenate(masked, axis=1))
    both, wide = jnp.concatenate([a, b], axis=0), a.shape[0]
    dims = (((1,), (1,)), ((), ()))
    for step, left in enumerate((l0, l1, l2, l3)):
        for copy in copies[4 * step : 4 * step + 4]:
            copy.wait()
        depth = left.shape[0]
        blocks = slice(2 * step, 2 * step + 2)
        large = held_top[blocks].reshape(depth, both.shape[1])
        small = held_rest[blocks].reshape(depth, both.shape[1])
        one = lax.dot_general(large, both, dims, preferred_element_type=f32)
        two = lax.dot_general(small, a, dims, preferred_element_type=f32)
        left[...] = one[:, :wide] + (one[:, wide:] + two)


def whole(kernel, core, args, shapes):
    return pl.pallas_call(
        kernel,
        out_shape=[jax.ShapeDtypeStruct(shape, f32) for shape in shapes],
        in_specs=[in_smem] + [in_vmem] * len(args) if core is not None else [in_vmem] * len(args),
        out_specs=[in_vmem] * len(shapes),
        cost_estimate=cost(4 << 20),
        compiler_params=pltpu.CompilerParams(vmem_limit_bytes=LIMIT),
    )(*(([core] if core is not None else []) + list(args)))


def per_device(
    transmission,
    dual_focal,
    dual_curvature,
    pupil_mask,
    lyot_mask,
    dark_mask,
    focal_rows,
    focal_cols,
):
    z = lax.axis_index("z").astype(jnp.int32)
    core = lax.axis_index("core").astype(jnp.int32)
    where, core = jnp.stack([z, core]), core[None]
    waves, fields, rows = focal_rows.shape
    cols = focal_cols.shape[2]
    part = fields // (ZS * CORES)
    own = dual_focal.shape[0]
    count = waves * part
    half = cols // CORES
    wide = half // CHUNKS
    tile, line = (rows, cols), [(1, cols)] * 4
    piece = (half, rows)

    dark = jnp.transpose(dark_mask.astype(f32), (1, 0, 2))
    dual_f = jnp.transpose(dual_focal, (1, 0, 2)) * dark
    spread = jnp.broadcast_to(dual_f[None], (COLS,) + dual_f.shape)

    other_rows = swap_core(focal_rows)
    started = pl.pallas_call(
        start_kernel,
        out_shape=[jax.ShapeDtypeStruct(shape, f32) for shape in line + [piece] * 4],
        in_specs=[in_smem] + [in_hbm] * 4,
        out_specs=[in_vmem] * 8,
        scratch_shapes=[pltpu.VMEM(tile, f32)] * 2 + [pltpu.VMEM(tile, jnp.int32)] * 2 + [pltpu.SemaphoreType.DMA((4,))],
        cost_estimate=cost(6 << 20),
        compiler_params=pltpu.CompilerParams(vmem_limit_bytes=LIMIT),
    )(core, *(stay(cells) for cells in (dual_curvature, transmission, pupil_mask, lyot_mask)))
    edges, x_mine, x_other, stop_mine, stop_other = started[:4], *started[4:]

    def block_of(b, where):
        return (0, (where[0] + b // CORES) % ZS * CORES + (where[1] + b) % CORES, 0, 0)

    def table_of(mine, other):
        return pl.pallas_call(
            table_kernel,
            grid_spec=pltpu.PrefetchScalarGridSpec(
                num_scalar_prefetch=1,
                grid=(ZS * CORES,),
                in_specs=[pl.BlockSpec((waves, 1, part, rows), block_of)] * 2,
                out_specs=[pl.BlockSpec((1, count, 2 * rows), lambda b, where: (b, 0, 0))] * 2,
            ),
            out_shape=[pltpu.HBM((ZS * CORES, count, 2 * rows), bf16)] * 2,
            cost_estimate=cost(20 << 20),
            compiler_params=pltpu.CompilerParams(vmem_limit_bytes=LIMIT),
        )(where, *(stay(half.reshape(waves, ZS * CORES, part, rows)) for half in (mine, other)))

    table = [stay(half) for half in table_of(focal_rows, other_rows)]
    primal_half = (x_mine, swap_core(x_other))
    stop_half = (stop_mine, swap_core(stop_other))
    held_table = [pltpu.VMEM((ZS * CORES, count, 2 * rows), bf16)] * 2 + [
        pltpu.SemaphoreType.DMA((2 * ZS * CORES,))
    ]
    held_cols = [pltpu.VMEM((waves, fields, cols), f32), pltpu.SemaphoreType.DMA((waves,))]

    def known(yc, around):
        mine, other = whole(known_kernel, core, (yc, pupil_mask, *around), [piece] * 2)
        return mine, swap_core(other)

    def streamed(kernel, args, shapes, scratch, specs, moved):
        return pl.pallas_call(
            kernel,
            grid=(1,),
            in_specs=specs,
            out_specs=[in_vmem] * len(shapes),
            out_shape=[jax.ShapeDtypeStruct(shape, f32) for shape in shapes],
            scratch_shapes=scratch,
            cost_estimate=cost(moved << 20),
            compiler_params=pltpu.CompilerParams(vmem_limit_bytes=LIMIT),
        )(*args)

    def carry(gathered):
        specs = [in_smem, in_vmem, in_hbm]
        return streamed(carry_kernel, (core, gathered, stay(focal_cols)), [(count, half)] * 2, held_cols, specs, 6)

    def find(sums, fars):
        specs = [in_smem, in_vmem, in_vmem, in_vmem, in_vmem, in_hbm]
        args = (core, *sums, *fars, stay(focal_cols))
        return streamed(found_kernel, args, [(COLS, waves, own, fields)], held_cols, specs, 8)[0]

    def gather(block):
        return block, shift_z(block, -1), shift_z(block, -2), shift_z(block, -3)

    def backward(full):
        specs = [in_vmem] * 4 + [in_hbm] * 2
        back = streamed(back_kernel, (*full, *table), [(wide, CORES * rows)], held_table, specs, 12)[0]
        return back, lax.ppermute(back, "wave", [(0, 1), (1, 0)])

    def update(chunk, known_half, back, far):
        cut = pl.BlockSpec((wide, rows), lambda i: (chunk, 0))
        specs = [in_vmem] * 2 + [cut] * 6 + [in_hbm] * 2
        args = (back, far, *primal_half, *stop_half, *known_half, *table)
        shapes = [(wide, rows)] * 2 + [(CORES * count, wide)] * ZS
        new0, new1, *left = streamed(update_kernel, args, shapes, held_table, specs, 14)
        return (new0, new1), left

    def scatter(left):
        return left[0] + shift_z(left[1], 1) + shift_z(left[2], 2) + shift_z(left[3], 3)

    primal, dual_c = transmission, dual_curvature
    gathered = lax.all_to_all(spread, COL, 0, 0, tiled=True)
    gathered, *around = tie((gathered, *exchange(edges)))
    known_half = known(dual_c, around)
    for iteration in range(ITERS):
        last = iteration == ITERS - 1
        mine, other = carry(gathered)
        received = swap_core(other)
        pair = jnp.concatenate([mine, received], axis=0)
        full_a, full_b = gather(pair[:, :wide]), gather(pair[:, wide:])
        back_a, far_a = backward(full_a)
        back_b, far_b = backward(full_b)
        far_a, back_b = tie((far_a, back_b))
        new_a, left_a = update(0, known_half, back_a, far_a)
        sum_a = scatter(left_a)
        far_b, new_a = tie((far_b, new_a))
        new_b, left_b = update(1, known_half, back_b, far_b)
        sum_b = scatter(left_b)

        args = (new_a[0], new_b[0], swap_core(new_a[1]), swap_core(new_b[1]), primal)
        primal_new, *edges = whole(primal_kernel, core, args, [tile] + line)
        sum_a, sum_b, primal_new, *around = tie((sum_a, sum_b, primal_new, *exchange(edges)))

        fars = swap_core(sum_a[count:]), swap_core(sum_b[count:])
        found, *around = tie((find((sum_a[:count], sum_b[:count]), fars), *around))
        parts = lax.all_to_all(found, COL, 0, 0, tiled=True)
        args = (primal_new, primal, dual_c, *around)
        dual_c, *edges = whole(dual_kernel, core, args, [tile] + ([] if last else line))
        primal = primal_new
        parts, dual_c, *edges = tie((parts, dual_c, *edges))
        if last:
            dual_f = whole(focal_kernel, None, (parts, dual_f, dark), [dual_f.shape])[0]
            break
        primal_half = tuple(jnp.concatenate(pieces, axis=0) for pieces in zip(new_a, new_b))
        dual_f, spread = whole(focal_kernel, None, (parts, dual_f, dark), [dual_f.shape, spread.shape])
        gathered = lax.all_to_all(spread, COL, 0, 0, tiled=True)
        gathered, *around = tie((gathered, *exchange(edges)))
        known_half = known(dual_c, around)
    return (primal, jnp.transpose(dual_f, (1, 0, 2)), dual_c)


def solution(mesh):
    parts = Mesh(
        mesh.devices.reshape(ZS, CORES, 2, COLS // 2, WAVES),
        ("z", "core", "xl", "y", "wave"),
    )
    return jax.shard_map(
        per_device,
        mesh=parts,
        in_specs=(
            P(ROW, COL),
            P(ROW + COL, "wave", None),
            P(ROW, COL),
            P(ROW, COL),
            P(ROW, COL),
            P(ROW + COL, "wave", None),
            P("wave", None, ROW),
            P("wave", None, COL),
        ),
        out_specs=(P(ROW, COL), P(ROW + COL, "wave", None), P(ROW, COL)),
        check_vma=False,
    )
```

```python
import functools

import jax
import jax.numpy as jnp
from jax import lax
from jax.experimental import pallas as pl
from jax.experimental.pallas import tpu as pltpu
from jax.sharding import Mesh, PartitionSpec as P

ITERS = 2

step_primal = 0.12
step_dual = 0.2
contrast = 0.5
curvature_limit = 0.1

ROW = ("z", "core")
COL = ("xl", "y")
ZS, CORES, COLS, WAVES = 4, 2, 8, 2
CHUNKS = 2
LIMIT = 24 * 1024 * 1024
f32 = jnp.float32
tie = lax.optimization_barrier
in_vmem = pl.BlockSpec(memory_space=pltpu.VMEM)
in_smem = pl.BlockSpec(memory_space=pltpu.SMEM)
in_hbm = pl.BlockSpec(memory_space=pltpu.HBM)
bf16 = jnp.bfloat16


def hold(cells):
    return pltpu.with_memory_space_constraint(cells, pltpu.VMEM)


def stay(cells):
    return pltpu.with_memory_space_constraint(cells, pltpu.HBM)


def cost(moved):
    return pl.CostEstimate(flops=0, bytes_accessed=moved, transcendentals=0)


def swap_core(cells):
    return lax.ppermute(cells, "core", [(0, 1), (1, 0)])


def shift_z(cells, by):
    return lax.ppermute(cells, "z", [(i, (i + by) % ZS) for i in range(ZS)])


def split(values):
    top = values.astype(jnp.bfloat16)
    return top, (values - top.astype(f32)).astype(jnp.bfloat16)


def dot3(a, b, dims):
    (a1, a2), (b1, b2) = split(a), split(b)
    mul = functools.partial(lax.dot_general, dimension_numbers=(dims, ((), ())), preferred_element_type=f32)
    return mul(a1, b1) + (mul(a1, b2) + mul(a2, b1))


def exchange(edges):
    near, far, head, tail = edges
    pairs = [(i, i + 1) for i in range(1, ZS * CORES - 1, 2)]
    return (
        swap_core(near),
        lax.ppermute(far, ROW, pairs + [(b, a) for a, b in pairs]),
        lax.ppermute(tail, COL, [(i, i + 1) for i in range(COLS - 1)]),
        lax.ppermute(head, COL, [(i + 1, i) for i in range(COLS - 1)]),
    )


def put_edges(first, cells, near_ref, far_ref, head_ref, tail_ref):
    rows, cols = cells.shape
    top, bottom = cells[0:1, :], cells[rows - 1 : rows, :]
    near_ref[...] = jnp.where(first, bottom, top)
    far_ref[...] = jnp.where(first, top, bottom)
    head_ref[...] = jnp.transpose(cells[:, :128])[0:1, :]
    tail_ref[...] = jnp.transpose(cells[:, cols - 128 :])[127:128, :]


def stencil(first, cells, near, far, left, right):
    rows, cols = cells.shape
    above, below = jnp.where(first, far, near), jnp.where(first, near, far)
    row = lax.broadcasted_iota(jnp.int32, cells.shape, 0)
    col = lax.broadcasted_iota(jnp.int32, cells.shape, 1)
    left = jnp.transpose(jnp.broadcast_to(left, (128, rows)))[:, 0:1]
    right = jnp.transpose(jnp.broadcast_to(right, (128, rows)))[:, 0:1]
    down = jnp.where(row == 0, above, pltpu.roll(cells, 1, 0))
    up = jnp.where(row == rows - 1, below, pltpu.roll(cells, rows - 1, 0))
    after = jnp.where(col == 0, left, pltpu.roll(cells, 1, 1))
    before = jnp.where(col == cols - 1, right, pltpu.roll(cells, cols - 1, 1))
    return 0.25 * (down + up + after + before) - cells


def halves(first, cells, mine_ref, other_ref, turn=True):
    half = cells.shape[1] // 2
    a, b = cells[:, :half], cells[:, half:]
    mine, other = jnp.where(first, a, b), jnp.where(first, b, a)
    mine_ref[...] = jnp.transpose(mine) if turn else mine
    other_ref[...] = jnp.transpose(other) if turn else other


def start_kernel(core, yc, x, pupil_mask, lyot_mask, *refs):
    near, far, head, tail, x_mine, x_other, stop_mine, stop_other, *held, sems = refs
    first = core[0] == 0
    copies = fetch(list(zip((yc, x, pupil_mask, lyot_mask), held)), sems)
    copies[0].wait()
    put_edges(first, held[0][...], near, far, head, tail)
    copies[1].wait()
    halves(first, held[1][...], x_mine, x_other)
    copies[2].wait()
    copies[3].wait()
    halves(first, (held[2][...] * held[3][...]).astype(f32), stop_mine, stop_other)


def known_kernel(core, yc, pupil_mask, near, far, left, right, mine, other):
    first = core[0] == 0
    curved = stencil(first, yc[...], near[...], far[...], left[...], right[...])
    halves(first, curved - pupil_mask[...].astype(f32), mine, other)


def primal_kernel(core, new_a, new_b, far_a, far_b, x, out, near, far, head, tail):
    first = core[0] == 0
    mine = jnp.transpose(jnp.concatenate([new_a[...], new_b[...]], axis=0))
    other = jnp.transpose(jnp.concatenate([far_a[...], far_b[...]], axis=0))
    new = jnp.concatenate([jnp.where(first, mine, other), jnp.where(first, other, mine)], axis=1)
    out[...] = new
    put_edges(first, 2.0 * new - x[...], near, far, head, tail)


def dual_kernel(core, new, x, yc, near, far, left, right, out, *edges):
    first = core[0] == 0
    extended = 2.0 * new[...] - x[...]
    curved = stencil(first, extended, near[...], far[...], left[...], right[...])
    moved = yc[...] + step_dual * curved
    result = moved - step_dual * jnp.clip(moved / step_dual, -curvature_limit, curvature_limit)
    out[...] = result
    if edges:
        put_edges(first, result, *edges)


def focal_kernel(parts, yf, dark, out, *spread):
    fields = parts[0]
    for other in range(1, COLS):
        fields = fields + parts[other]
    shifted = yf[...] + step_dual * fields
    result = dark[...] * (shifted - step_dual * jnp.clip(shifted / step_dual, -contrast, contrast))
    out[...] = result
    if spread:
        for other in range(COLS):
            spread[0][other] = result


def fetch(pairs, sems):
    copies = [pltpu.make_async_copy(src, dst, sems.at[i]) for i, (src, dst) in enumerate(pairs)]
    for copy in copies:
        copy.start()
    return copies


def carry_kernel(core, y, table, mine, other):
    waves, rows = y.shape[1], y.shape[0] * y.shape[2]
    for w in range(waves):
        carried = dot3(y[:, w].reshape(rows, y.shape[3]), table[w], ((1,), (0,)))
        at = pl.ds(w * rows, rows)
        halves(core[0] == 0, carried, mine.at[at], other.at[at], turn=False)


def found_kernel(core, own_a, own_b, far_a, far_b, table, out):
    first = core[0] == 0
    waves, rows = out.shape[1], out.shape[0] * out.shape[2]
    for w in range(waves):
        at = pl.ds(w * rows, rows)
        own = jnp.concatenate([own_a[at, :], own_b[at, :]], axis=1)
        far = jnp.concatenate([far_a[at, :], far_b[at, :]], axis=1)
        left = jnp.concatenate([jnp.where(first, own, far), jnp.where(first, far, own)], axis=1)
        found = dot3(left, table[w], ((1,), (1,)))
        out[:, w] = found.reshape(out.shape[0], out.shape[2], out.shape[3])


def table_kernel(where, mine, other, top, rest):
    rows, b = mine.shape[3], pl.program_id(0)
    for at, block in ((0, mine), (rows, other)):
        large, small = split(block[:, 0].reshape(top.shape[1], rows))
        top[b, :, at : at + rows] = large
        rest[b, :, at : at + rows] = small


def cols_kernel(table, out, sems):
    fetch([(table, out)], sems)[0].wait()


def back_kernel(t0, t1, t2, t3, top, rest, out):
    for step, t in enumerate((t0, t1, t2, t3)):
        depth, wide = t.shape
        a, b = split(jnp.transpose(t[...]))
        blocks = slice(2 * step, 2 * step + 2)
        both = jnp.dot(
            jnp.concatenate([a, b], axis=0),
            top[blocks].reshape(depth, out.shape[1]),
            preferred_element_type=f32,
        )
        more = jnp.dot(a, rest[blocks].reshape(depth, out.shape[1]), preferred_element_type=f32)
        part = both[:wide] + (both[wide:] + more)
        out[...] = part if step == 0 else out[...] + part


def update_kernel(back, far, x0, x1, s0, s1, k0, k1, top, rest, new0, new1, l0, l1, l2, l3):
    rows = x0.shape[1]
    masked = []
    for i, (x, stop, known, new) in enumerate(((x0, s0, k0, new0), (x1, s1, k1, new1))):
        at = slice(i * rows, (i + 1) * rows)
        before = x[...]
        gradient = known[...] + stop[...] * (back[:, at] + far[:, at])
        after = jnp.clip(before - step_primal * gradient, 0.0, 1.0)
        new[...] = after
        masked.append(stop[...] * (2.0 * after - before))
    a, b = split(jnp.concatenate(masked, axis=1))
    both, wide = jnp.concatenate([a, b], axis=0), a.shape[0]
    dims = (((1,), (1,)), ((), ()))
    for step, left in enumerate((l0, l1, l2, l3)):
        depth = left.shape[0]
        blocks = slice(2 * step, 2 * step + 2)
        large = top[blocks].reshape(depth, both.shape[1])
        small = rest[blocks].reshape(depth, both.shape[1])
        one = lax.dot_general(large, both, dims, preferred_element_type=f32)
        two = lax.dot_general(small, a, dims, preferred_element_type=f32)
        left[...] = one[:, :wide] + (one[:, wide:] + two)


def whole(kernel, core, args, shapes):
    return pl.pallas_call(
        kernel,
        out_shape=[jax.ShapeDtypeStruct(shape, f32) for shape in shapes],
        in_specs=[in_smem] + [in_vmem] * len(args) if core is not None else [in_vmem] * len(args),
        out_specs=[in_vmem] * len(shapes),
        cost_estimate=cost(4 << 20),
        compiler_params=pltpu.CompilerParams(vmem_limit_bytes=LIMIT),
    )(*(([core] if core is not None else []) + list(args)))


def per_device(
    transmission,
    dual_focal,
    dual_curvature,
    pupil_mask,
    lyot_mask,
    dark_mask,
    focal_rows,
    focal_cols,
):
    z = lax.axis_index("z").astype(jnp.int32)
    core = lax.axis_index("core").astype(jnp.int32)
    where, core = jnp.stack([z, core]), core[None]
    waves, fields, rows = focal_rows.shape
    cols = focal_cols.shape[2]
    part = fields // (ZS * CORES)
    own = dual_focal.shape[0]
    count = waves * part
    half = cols // CORES
    wide = half // CHUNKS
    tile, line = (rows, cols), [(1, cols)] * 4
    piece = (half, rows)

    dark = jnp.transpose(dark_mask.astype(f32), (1, 0, 2))
    dual_f = jnp.transpose(dual_focal, (1, 0, 2)) * dark
    spread = jnp.broadcast_to(dual_f[None], (COLS,) + dual_f.shape)

    other_rows = swap_core(focal_rows)
    started = pl.pallas_call(
        start_kernel,
        out_shape=[jax.ShapeDtypeStruct(shape, f32) for shape in line + [piece] * 4],
        in_specs=[in_smem] + [in_hbm] * 4,
        out_specs=[in_vmem] * 8,
        scratch_shapes=[pltpu.VMEM(tile, f32)] * 2 + [pltpu.VMEM(tile, jnp.int32)] * 2 + [pltpu.SemaphoreType.DMA((4,))],
        cost_estimate=cost(6 << 20),
        compiler_params=pltpu.CompilerParams(vmem_limit_bytes=LIMIT),
    )(core, *(stay(cells) for cells in (dual_curvature, transmission, pupil_mask, lyot_mask)))
    edges, x_mine, x_other, stop_mine, stop_other = started[:4], *started[4:]

    def block_of(b, where):
        return (0, (where[0] + b // CORES) % ZS * CORES + (where[1] + b) % CORES, 0, 0)

    def table_of(mine, other):
        return pl.pallas_call(
            table_kernel,
            grid_spec=pltpu.PrefetchScalarGridSpec(
                num_scalar_prefetch=1,
                grid=(ZS * CORES,),
                in_specs=[pl.BlockSpec((waves, 1, part, rows), block_of)] * 2,
                out_specs=[in_vmem] * 2,
            ),
            out_shape=[pltpu.VMEM((ZS * CORES, count, 2 * rows), bf16)] * 2,
            cost_estimate=cost(20 << 20),
            compiler_params=pltpu.CompilerParams(vmem_limit_bytes=LIMIT),
        )(where, *(stay(half.reshape(waves, ZS * CORES, part, rows)) for half in (mine, other)))

    table = [hold(half) for half in table_of(focal_rows, other_rows)]
    columns = hold(
        pl.pallas_call(
            cols_kernel,
            out_shape=pltpu.VMEM(focal_cols.shape, f32),
            in_specs=[in_hbm],
            out_specs=in_vmem,
            scratch_shapes=[pltpu.SemaphoreType.DMA((1,))],
            cost_estimate=cost(4 << 20),
            compiler_params=pltpu.CompilerParams(vmem_limit_bytes=LIMIT),
        )(stay(focal_cols))
    )
    primal_half = (x_mine, swap_core(x_other))
    stop_half = (stop_mine, swap_core(stop_other))

    def known(yc, around):
        mine, other = whole(known_kernel, core, (yc, pupil_mask, *around), [piece] * 2)
        return mine, swap_core(other)

    def product(kernel, args, shapes, specs, moved):
        return pl.pallas_call(
            kernel,
            grid=(1,),
            in_specs=specs,
            out_specs=[in_vmem] * len(shapes),
            out_shape=[jax.ShapeDtypeStruct(shape, f32) for shape in shapes],
            cost_estimate=cost(moved << 20),
            compiler_params=pltpu.CompilerParams(vmem_limit_bytes=LIMIT),
        )(*args)

    def carry(gathered):
        specs = [in_smem, in_vmem, in_vmem]
        return product(carry_kernel, (core, gathered, columns), [(count, half)] * 2, specs, 6)

    def find(sums, fars):
        specs = [in_smem] + [in_vmem] * 5
        args = (core, *sums, *fars, columns)
        return product(found_kernel, args, [(COLS, waves, own, fields)], specs, 8)[0]

    def gather(block):
        return block, shift_z(block, -1), shift_z(block, -2), shift_z(block, -3)

    def backward(full):
        specs = [in_vmem] * 6
        back = product(back_kernel, (*full, *table), [(wide, CORES * rows)], specs, 12)[0]
        return back, lax.ppermute(back, "wave", [(0, 1), (1, 0)])

    def update(chunk, known_half, back, far):
        cut = pl.BlockSpec((wide, rows), lambda i: (chunk, 0))
        specs = [in_vmem] * 2 + [cut] * 6 + [in_vmem] * 2
        args = (back, far, *primal_half, *stop_half, *known_half, *table)
        shapes = [(wide, rows)] * 2 + [(CORES * count, wide)] * ZS
        new0, new1, *left = product(update_kernel, args, shapes, specs, 1)
        return (new0, new1), left

    def scatter(left):
        return left[0] + shift_z(left[1], 1) + shift_z(left[2], 2) + shift_z(left[3], 3)

    primal, dual_c = transmission, dual_curvature
    gathered = lax.all_to_all(spread, COL, 0, 0, tiled=True)
    gathered, *around = tie((gathered, *exchange(edges)))
    known_half = known(dual_c, around)
    for iteration in range(ITERS):
        last = iteration == ITERS - 1
        mine, other = carry(gathered)
        received = swap_core(other)
        pair = jnp.concatenate([mine, received], axis=0)
        full_a, full_b = gather(pair[:, :wide]), gather(pair[:, wide:])
        back_a, far_a = backward(full_a)
        back_b, far_b = backward(full_b)
        far_a, back_b = tie((far_a, back_b))
        new_a, left_a = update(0, known_half, back_a, far_a)
        sum_a = scatter(left_a)
        far_b, new_a = tie((far_b, new_a))
        new_b, left_b = update(1, known_half, back_b, far_b)
        sum_b = scatter(left_b)

        moved = swap_core(new_a[1]), swap_core(new_b[1])
        sum_a, *moved = tie((sum_a, *moved))
        args = (new_a[0], new_b[0], *moved, primal)
        primal_new, *edges = whole(primal_kernel, core, args, [tile] + line)
        sum_a, sum_b, primal_new, *around = tie((sum_a, sum_b, primal_new, *exchange(edges)))

        fars = swap_core(sum_a[count:]), swap_core(sum_b[count:])
        found, *around = tie((find((sum_a[:count], sum_b[:count]), fars), *around))
        parts = lax.all_to_all(found, COL, 0, 0, tiled=True)
        args = (primal_new, primal, dual_c, *around)
        dual_c, *edges = whole(dual_kernel, core, args, [tile] + ([] if last else line))
        primal = primal_new
        parts, dual_c, *edges = tie((parts, dual_c, *edges))
        if last:
            dual_f = whole(focal_kernel, None, (parts, dual_f, dark), [dual_f.shape])[0]
            break
        primal_half = tuple(jnp.concatenate(pieces, axis=0) for pieces in zip(new_a, new_b))
        dual_f, spread = whole(focal_kernel, None, (parts, dual_f, dark), [dual_f.shape, spread.shape])
        gathered = lax.all_to_all(spread, COL, 0, 0, tiled=True)
        gathered, *around = tie((gathered, *exchange(edges)))
        known_half = known(dual_c, around)
    return (primal, jnp.transpose(dual_f, (1, 0, 2)), dual_c)


def solution(mesh):
    parts = Mesh(
        mesh.devices.reshape(ZS, CORES, 2, COLS // 2, WAVES),
        ("z", "core", "xl", "y", "wave"),
    )
    return jax.shard_map(
        per_device,
        mesh=parts,
        in_specs=(
            P(ROW, COL),
            P(ROW + COL, "wave", None),
            P(ROW, COL),
            P(ROW, COL),
            P(ROW, COL),
            P(ROW + COL, "wave", None),
            P("wave", None, ROW),
            P("wave", None, COL),
        ),
        out_specs=(P(ROW, COL), P(ROW + COL, "wave", None), P(ROW, COL)),
        check_vma=False,
    )
```

```python
import functools

import jax
import jax.numpy as jnp
from jax import lax
from jax.experimental import pallas as pl
from jax.experimental.pallas import tpu as pltpu
from jax.sharding import Mesh, PartitionSpec as P

ITERS = 2

step_primal = 0.12
step_dual = 0.2
contrast = 0.5
curvature_limit = 0.1

ROW = ("z", "core")
COL = ("xl", "y")
ZS, CORES, COLS, WAVES = 4, 2, 8, 2
CHUNKS = 2
LIMIT = 16 * 1024 * 1024
f32 = jnp.float32
tie = lax.optimization_barrier
in_vmem = pl.BlockSpec(memory_space=pltpu.VMEM)
in_smem = pl.BlockSpec(memory_space=pltpu.SMEM)
in_hbm = pl.BlockSpec(memory_space=pltpu.HBM)
bf16 = jnp.bfloat16


def hold(cells):
    return pltpu.with_memory_space_constraint(cells, pltpu.VMEM)


def stay(cells):
    return pltpu.with_memory_space_constraint(cells, pltpu.HBM)


def cost(moved):
    return pl.CostEstimate(flops=0, bytes_accessed=moved, transcendentals=0)


def swap_core(cells):
    return lax.ppermute(cells, "core", [(0, 1), (1, 0)])


def shift_z(cells, by):
    return lax.ppermute(cells, "z", [(i, (i + by) % ZS) for i in range(ZS)])


def split(values):
    top = values.astype(jnp.bfloat16)
    return top, (values - top.astype(f32)).astype(jnp.bfloat16)


def dot3(a, b, dims):
    (a1, a2), (b1, b2) = split(a), split(b)
    mul = functools.partial(lax.dot_general, dimension_numbers=(dims, ((), ())), preferred_element_type=f32)
    return mul(a1, b1) + (mul(a1, b2) + mul(a2, b1))


def exchange(edges):
    near, far, head, tail = edges
    pairs = [(i, i + 1) for i in range(1, ZS * CORES - 1, 2)]
    return (
        swap_core(near),
        lax.ppermute(far, ROW, pairs + [(b, a) for a, b in pairs]),
        lax.ppermute(tail, COL, [(i, i + 1) for i in range(COLS - 1)]),
        lax.ppermute(head, COL, [(i + 1, i) for i in range(COLS - 1)]),
    )


def put_edges(first, cells, near_ref, far_ref, head_ref, tail_ref):
    rows, cols = cells.shape
    top, bottom = cells[0:1, :], cells[rows - 1 : rows, :]
    near_ref[...] = jnp.where(first, bottom, top)
    far_ref[...] = jnp.where(first, top, bottom)
    head_ref[...] = jnp.transpose(cells[:, :128])[0:1, :]
    tail_ref[...] = jnp.transpose(cells[:, cols - 128 :])[127:128, :]


def stencil(first, cells, near, far, left, right):
    rows, cols = cells.shape
    above, below = jnp.where(first, far, near), jnp.where(first, near, far)
    row = lax.broadcasted_iota(jnp.int32, cells.shape, 0)
    col = lax.broadcasted_iota(jnp.int32, cells.shape, 1)
    left = jnp.transpose(jnp.broadcast_to(left, (128, rows)))[:, 0:1]
    right = jnp.transpose(jnp.broadcast_to(right, (128, rows)))[:, 0:1]
    down = jnp.where(row == 0, above, pltpu.roll(cells, 1, 0))
    up = jnp.where(row == rows - 1, below, pltpu.roll(cells, rows - 1, 0))
    after = jnp.where(col == 0, left, pltpu.roll(cells, 1, 1))
    before = jnp.where(col == cols - 1, right, pltpu.roll(cells, cols - 1, 1))
    return 0.25 * (down + up + after + before) - cells


def halves(first, cells, mine_ref, other_ref, turn=True):
    half = cells.shape[1] // 2
    a, b = cells[:, :half], cells[:, half:]
    mine, other = jnp.where(first, a, b), jnp.where(first, b, a)
    mine_ref[...] = jnp.transpose(mine) if turn else mine
    other_ref[...] = jnp.transpose(other) if turn else other


def start_kernel(core, yc, x, pupil_mask, lyot_mask, *refs):
    near, far, head, tail, x_mine, x_other, stop_mine, stop_other, *held, sems = refs
    first = core[1] == 0
    copies = fetch(list(zip((yc, x, pupil_mask, lyot_mask), held)), sems)
    copies[0].wait()
    put_edges(first, held[0][...], near, far, head, tail)
    copies[1].wait()
    halves(first, held[1][...], x_mine, x_other)
    copies[2].wait()
    copies[3].wait()
    halves(first, (held[2][...] * held[3][...]).astype(f32), stop_mine, stop_other)


def known_kernel(core, yc, pupil_mask, near, far, left, right, mine, other):
    first = core[1] == 0
    curved = stencil(first, yc[...], near[...], far[...], left[...], right[...])
    halves(first, curved - pupil_mask[...].astype(f32), mine, other)


def primal_kernel(core, new_a, new_b, far_a, far_b, x, out, near, far, head, tail):
    first = core[1] == 0
    mine = jnp.transpose(jnp.concatenate([new_a[...], new_b[...]], axis=0))
    other = jnp.transpose(jnp.concatenate([far_a[...], far_b[...]], axis=0))
    new = jnp.concatenate([jnp.where(first, mine, other), jnp.where(first, other, mine)], axis=1)
    out[...] = new
    put_edges(first, 2.0 * new - x[...], near, far, head, tail)


def dual_kernel(core, new, x, yc, near, far, left, right, out, *edges):
    first = core[1] == 0
    extended = 2.0 * new[...] - x[...]
    curved = stencil(first, extended, near[...], far[...], left[...], right[...])
    moved = yc[...] + step_dual * curved
    result = moved - step_dual * jnp.clip(moved / step_dual, -curvature_limit, curvature_limit)
    out[...] = result
    if edges:
        put_edges(first, result, *edges)


def focal_kernel(parts, yf, dark, out, *spread):
    fields = parts[0]
    for other in range(1, COLS):
        fields = fields + parts[other]
    shifted = yf[...] + step_dual * fields
    result = dark[...] * (shifted - step_dual * jnp.clip(shifted / step_dual, -contrast, contrast))
    out[...] = result
    if spread:
        for other in range(COLS):
            spread[0][other] = result


def fetch(pairs, sems):
    copies = [pltpu.make_async_copy(src, dst, sems.at[i]) for i, (src, dst) in enumerate(pairs)]
    for copy in copies:
        copy.start()
    return copies


def carry_kernel(core, y, table, mine, other, held, sems):
    waves, rows = y.shape[1], y.shape[0] * y.shape[2]
    copies = fetch([(table.at[w], held.at[w]) for w in range(waves)], sems)
    for w in range(waves):
        copies[w].wait()
        carried = dot3(y[:, w].reshape(rows, y.shape[3]), held[w], ((1,), (0,)))
        at = pl.ds(w * rows, rows)
        halves(core[1] == 0, carried, mine.at[at], other.at[at], turn=False)


def found_kernel(core, own_a, own_b, far_a, far_b, table, out):
    first = core[1] == 0
    waves, rows = out.shape[1], out.shape[0] * out.shape[2]
    for w in range(waves):
        at = pl.ds(w * rows, rows)
        own = jnp.concatenate([own_a[at, :], own_b[at, :]], axis=1)
        far = jnp.concatenate([far_a[at, :], far_b[at, :]], axis=1)
        left = jnp.concatenate([jnp.where(first, own, far), jnp.where(first, far, own)], axis=1)
        found = dot3(left, table[w], ((1,), (1,)))
        out[:, w] = found.reshape(out.shape[0], out.shape[2], out.shape[3])


def table_kernel(where, mine, other, top, rest, ready):
    ready[...] = jnp.zeros_like(ready)
    rows, b = mine.shape[3], pl.program_id(0)
    for at, block in ((0, mine), (rows, other)):
        large, small = split(block[:, 0].reshape(top.shape[1], rows))
        top[b, :, at : at + rows] = large
        rest[b, :, at : at + rows] = small


def back_kernel(t0, t1, t2, t3, top, rest, out):
    for step, t in enumerate((t0, t1, t2, t3)):
        depth, wide = t.shape
        a, b = split(jnp.transpose(t[...]))
        blocks = slice(2 * step, 2 * step + 2)
        both = jnp.dot(
            jnp.concatenate([a, b], axis=0),
            top[blocks].reshape(depth, out.shape[1]),
            preferred_element_type=f32,
        )
        more = jnp.dot(a, rest[blocks].reshape(depth, out.shape[1]), preferred_element_type=f32)
        part = both[:wide] + (both[wide:] + more)
        out[...] = part if step == 0 else out[...] + part


def update_kernel(back, far, x0, x1, s0, s1, k0, k1, top, rest, new0, new1, l0, l1, l2, l3):
    rows = x0.shape[1]
    masked = []
    for i, (x, stop, known, new) in enumerate(((x0, s0, k0, new0), (x1, s1, k1, new1))):
        at = slice(i * rows, (i + 1) * rows)
        before = x[...]
        gradient = known[...] + stop[...] * (back[:, at] + far[:, at])
        after = jnp.clip(before - step_primal * gradient, 0.0, 1.0)
        new[...] = after
        masked.append(stop[...] * (2.0 * after - before))
    a, b = split(jnp.concatenate(masked, axis=1))
    both, wide = jnp.concatenate([a, b], axis=0), a.shape[0]
    dims = (((1,), (1,)), ((), ()))
    for step, left in enumerate((l0, l1, l2, l3)):
        depth = left.shape[0]
        blocks = slice(2 * step, 2 * step + 2)
        large = top[blocks].reshape(depth, both.shape[1])
        small = rest[blocks].reshape(depth, both.shape[1])
        one = lax.dot_general(large, both, dims, preferred_element_type=f32)
        two = lax.dot_general(small, a, dims, preferred_element_type=f32)
        left[...] = one[:, :wide] + (one[:, wide:] + two)


def results(shapes, far):
    kinds = [pltpu.HBM(shape, f32) if i in far else jax.ShapeDtypeStruct(shape, f32) for i, shape in enumerate(shapes)]
    places = [
        pl.BlockSpec(shape, lambda i, rank=len(shape): (0,) * rank) if i in far else in_vmem
        for i, shape in enumerate(shapes)
    ]
    return {"grid": (1,), "out_shape": kinds, "out_specs": places}


def whole(kernel, core, args, shapes, far=()):
    return pl.pallas_call(
        kernel,
        **results(shapes, far),
        in_specs=[in_smem] + [in_vmem] * len(args) if core is not None else [in_vmem] * len(args),
        cost_estimate=cost(4 << 20),
        compiler_params=pltpu.CompilerParams(vmem_limit_bytes=LIMIT),
    )(*(([core] if core is not None else []) + list(args)))


def per_device(
    transmission,
    dual_focal,
    dual_curvature,
    pupil_mask,
    lyot_mask,
    dark_mask,
    focal_rows,
    focal_cols,
):
    z = lax.axis_index("z").astype(jnp.int32)
    core = lax.axis_index("core").astype(jnp.int32)
    core = where = jnp.stack([z, core])
    waves, fields, rows = focal_rows.shape
    cols = focal_cols.shape[2]
    part = fields // (ZS * CORES)
    own = dual_focal.shape[0]
    count = waves * part
    half = cols // CORES
    wide = half // CHUNKS
    tile, line = (rows, cols), [(1, cols)] * 4
    piece = (half, rows)

    dark = jnp.transpose(dark_mask.astype(f32), (1, 0, 2))
    dual_f = jnp.transpose(dual_focal, (1, 0, 2)) * dark
    spread = jnp.broadcast_to(dual_f[None], (COLS,) + dual_f.shape)

    other_rows = swap_core(focal_rows)
    started = pl.pallas_call(
        start_kernel,
        out_shape=[jax.ShapeDtypeStruct(shape, f32) for shape in line + [piece] * 4],
        in_specs=[in_smem] + [in_hbm] * 4,
        out_specs=[in_vmem] * 8,
        scratch_shapes=[pltpu.VMEM(tile, f32)] * 2 + [pltpu.VMEM(tile, jnp.int32)] * 2 + [pltpu.SemaphoreType.DMA((4,))],
        cost_estimate=cost(6 << 20),
        compiler_params=pltpu.CompilerParams(vmem_limit_bytes=LIMIT),
    )(core, *(stay(cells) for cells in (dual_curvature, transmission, pupil_mask, lyot_mask)))
    edges, x_mine, x_other, stop_mine, stop_other = started[:4], *started[4:]

    def block_of(b, where):
        return (0, (where[0] + b // CORES) % ZS * CORES + (where[1] + b) % CORES, 0, 0)

    def table_of(mine, other):
        return pl.pallas_call(
            table_kernel,
            grid_spec=pltpu.PrefetchScalarGridSpec(
                num_scalar_prefetch=1,
                grid=(ZS * CORES,),
                in_specs=[pl.BlockSpec((waves, 1, part, rows), block_of)] * 2,
                out_specs=[in_vmem] * 3,
            ),
            out_shape=[pltpu.VMEM((ZS * CORES, count, 2 * rows), bf16)] * 2 + [jax.ShapeDtypeStruct((8, 128), f32)],
            cost_estimate=cost(20 << 20),
            compiler_params=pltpu.CompilerParams(vmem_limit_bytes=LIMIT),
        )(where, *(stay(half.reshape(waves, ZS * CORES, part, rows)) for half in (mine, other)))

    *table, ready = table_of(focal_rows, other_rows)
    table = [hold(half) for half in table]
    primal_half = (x_mine, swap_core(x_other))
    stop_half = (stop_mine, swap_core(stop_other))

    def known(yc, around):
        mine, other = whole(known_kernel, core, (yc, pupil_mask, *around), [piece] * 2)
        return mine, swap_core(other)

    def product(kernel, args, shapes, specs, moved, scratch=(), far=()):
        return pl.pallas_call(
            kernel,
            **results(shapes, far),
            in_specs=specs,
            scratch_shapes=list(scratch),
            cost_estimate=cost(moved << 20),
            compiler_params=pltpu.CompilerParams(vmem_limit_bytes=LIMIT),
        )(*args)

    def carry(gathered):
        specs = [in_smem, in_vmem, in_hbm]
        scratch = [pltpu.VMEM((waves, fields, cols), f32), pltpu.SemaphoreType.DMA((waves,))]
        args = (core, gathered, stay(focal_cols))
        return product(carry_kernel, args, [(count, half)] * 2, specs, 6, scratch)

    def find(sums, fars):
        specs = [in_smem] + [in_vmem] * 5
        args = (core, *sums, *fars, hold(focal_cols))
        return product(found_kernel, args, [(COLS, waves, own, fields)], specs, 8, far=(0,))[0]

    def gather(block):
        return block, shift_z(block, -1), shift_z(block, -2), shift_z(block, -3)

    def backward(full):
        specs = [in_vmem] * 6
        back = product(back_kernel, (*full, *table), [(wide, CORES * rows)], specs, 12)[0]
        return back, lax.ppermute(back, "wave", [(0, 1), (1, 0)])

    def update(chunk, known_half, back, far):
        cut = pl.BlockSpec((wide, rows), lambda i: (chunk, 0))
        specs = [in_vmem] * 2 + [cut] * 6 + [in_vmem] * 2
        args = (back, far, *primal_half, *stop_half, *known_half, *table)
        shapes = [(wide, rows)] * 2 + [(CORES * count, wide)] * ZS
        new0, new1, *left = product(update_kernel, args, shapes, specs, 1)
        return (new0, new1), left

    def scatter(left):
        return left[0] + shift_z(left[1], 1) + shift_z(left[2], 2) + shift_z(left[3], 3)

    primal, dual_c = transmission, dual_curvature
    gathered = lax.all_to_all(spread, COL, 0, 0, tiled=True)
    gathered, *around = tie((gathered, *exchange(edges)))
    known_half = known(dual_c, around)
    for iteration in range(ITERS):
        last = iteration == ITERS - 1
        mine, other = carry(gathered)
        received = swap_core(other)
        pair = jnp.concatenate([mine, received], axis=0)
        pair_a, pair_b = pair[:, :wide], pair[:, wide:]
        if iteration == 0:
            pair_b, ready = tie((pair_b, ready))
        full_a, full_b = gather(pair_a), gather(pair_b)
        back_a, far_a = backward(full_a)
        back_b, far_b = backward(full_b)
        far_a, back_b = tie((far_a, back_b))
        new_a, left_a = update(0, known_half, back_a, far_a)
        sum_a = scatter(left_a)
        far_b, new_a = tie((far_b, new_a))
        new_b, left_b = update(1, known_half, back_b, far_b)
        sum_b = scatter(left_b)

        moved = swap_core(new_a[1]), swap_core(new_b[1])
        sum_a, *moved = tie((sum_a, *moved))
        args = (new_a[0], new_b[0], *moved, primal)
        primal_new, *edges = whole(primal_kernel, core, args, [tile] + line)
        sum_a, sum_b, primal_new, *around = tie((sum_a, sum_b, primal_new, *exchange(edges)))

        fars = swap_core(sum_a[count:]), swap_core(sum_b[count:])
        found, *around = tie((find((sum_a[:count], sum_b[:count]), fars), *around))
        parts = lax.all_to_all(found, COL, 0, 0, tiled=True)
        args = (primal_new, primal, dual_c, *around)
        dual_c, *edges = whole(dual_kernel, core, args, [tile] + ([] if last else line), () if last else (0, 1, 2, 3, 4))
        primal = primal_new
        parts, dual_c, *edges = tie((parts, dual_c, *edges))
        if last:
            dual_f = whole(focal_kernel, None, (parts, dual_f, dark), [dual_f.shape])[0]
            break
        primal_half = tuple(jnp.concatenate(pieces, axis=0) for pieces in zip(new_a, new_b))
        dual_f, spread = whole(focal_kernel, None, (parts, dual_f, dark), [dual_f.shape, spread.shape], (1,))
        gathered = lax.all_to_all(spread, COL, 0, 0, tiled=True)
        gathered, *around = tie((gathered, *exchange(edges)))
        known_half = known(dual_c, around)
    return (primal, jnp.transpose(dual_f, (1, 0, 2)), dual_c)


def solution(mesh):
    parts = Mesh(
        mesh.devices.reshape(ZS, CORES, 2, COLS // 2, WAVES),
        ("z", "core", "xl", "y", "wave"),
    )
    return jax.shard_map(
        per_device,
        mesh=parts,
        in_specs=(
            P(ROW, COL),
            P(ROW + COL, "wave", None),
            P(ROW, COL),
            P(ROW, COL),
            P(ROW, COL),
            P(ROW + COL, "wave", None),
            P("wave", None, ROW),
            P("wave", None, COL),
        ),
        out_specs=(P(ROW, COL), P(ROW + COL, "wave", None), P(ROW, COL)),
        check_vma=False,
    )
```

```python
import functools

import jax
import jax.numpy as jnp
from jax import lax
from jax.experimental import pallas as pl
from jax.experimental.pallas import tpu as pltpu
from jax.sharding import Mesh, PartitionSpec as P

ITERS = 2

step_primal = 0.12
step_dual = 0.2
contrast = 0.5
curvature_limit = 0.1

ROW = ("z", "core")
COL = ("xl", "y")
ZS, CORES, COLS, WAVES = 4, 2, 8, 2
CHUNKS = 2
LIMIT = 16 * 1024 * 1024
f32 = jnp.float32
tie = lax.optimization_barrier
in_vmem = pl.BlockSpec(memory_space=pltpu.VMEM)
in_smem = pl.BlockSpec(memory_space=pltpu.SMEM)
in_hbm = pl.BlockSpec(memory_space=pltpu.HBM)
bf16 = jnp.bfloat16


def hold(cells):
    return pltpu.with_memory_space_constraint(cells, pltpu.VMEM)


def stay(cells):
    return pltpu.with_memory_space_constraint(cells, pltpu.HBM)


def cost(moved):
    return pl.CostEstimate(flops=0, bytes_accessed=moved, transcendentals=0)


def swap_core(cells):
    return lax.ppermute(cells, "core", [(0, 1), (1, 0)])


def shift_z(cells, by):
    return lax.ppermute(cells, "z", [(i, (i + by) % ZS) for i in range(ZS)])


def split(values):
    top = values.astype(jnp.bfloat16)
    return top, (values - top.astype(f32)).astype(jnp.bfloat16)


def dot3(a, b, dims):
    (a1, a2), (b1, b2) = split(a), split(b)
    mul = functools.partial(lax.dot_general, dimension_numbers=(dims, ((), ())), preferred_element_type=f32)
    both, rows = mul(jnp.concatenate([a1, a2], axis=0), b1), a.shape[0]
    return both[:rows] + (mul(a1, b2) + both[rows:])


def exchange(edges):
    return *exchange_rows(*edges[:2]), *exchange_cols(*edges[2:])


def exchange_rows(near, far):
    pairs = [(i, i + 1) for i in range(1, ZS * CORES - 1, 2)]
    return swap_core(near), lax.ppermute(far, ROW, pairs + [(b, a) for a, b in pairs])


def exchange_cols(head, tail):
    return (
        lax.ppermute(tail, COL, [(i, i + 1) for i in range(COLS - 1)]),
        lax.ppermute(head, COL, [(i + 1, i) for i in range(COLS - 1)]),
    )


def put_edges(first, cells, near_ref, far_ref, head_ref, tail_ref):
    rows, cols = cells.shape
    top, bottom = cells[0:1, :], cells[rows - 1 : rows, :]
    near_ref[...] = jnp.where(first, bottom, top)
    far_ref[...] = jnp.where(first, top, bottom)
    head_ref[...] = jnp.transpose(cells[:, :128])[0:1, :]
    tail_ref[...] = jnp.transpose(cells[:, cols - 128 :])[127:128, :]


def stencil(first, cells, near, far, left, right):
    rows, cols = cells.shape
    above, below = jnp.where(first, far, near), jnp.where(first, near, far)
    row = lax.broadcasted_iota(jnp.int32, cells.shape, 0)
    col = lax.broadcasted_iota(jnp.int32, cells.shape, 1)
    left = jnp.transpose(jnp.broadcast_to(left, (128, rows)))[:, 0:1]
    right = jnp.transpose(jnp.broadcast_to(right, (128, rows)))[:, 0:1]
    down = jnp.where(row == 0, above, pltpu.roll(cells, 1, 0))
    up = jnp.where(row == rows - 1, below, pltpu.roll(cells, rows - 1, 0))
    after = jnp.where(col == 0, left, pltpu.roll(cells, 1, 1))
    before = jnp.where(col == cols - 1, right, pltpu.roll(cells, cols - 1, 1))
    return 0.25 * (down + up + after + before) - cells


def halves(first, cells, mine_ref, other_ref, turn=True):
    half = cells.shape[1] // 2
    a, b = cells[:, :half], cells[:, half:]
    mine, other = jnp.where(first, a, b), jnp.where(first, b, a)
    mine_ref[...] = jnp.transpose(mine) if turn else mine
    other_ref[...] = jnp.transpose(other) if turn else other


def start_kernel(core, yc, x, pupil_mask, lyot_mask, *refs):
    near, far, head, tail, x_mine, x_other, stop_mine, stop_other, *held, sems = refs
    first = core[1] == 0
    copies = fetch(list(zip((yc, x, pupil_mask, lyot_mask), held)), sems)
    copies[0].wait()
    put_edges(first, held[0][...], near, far, head, tail)
    copies[1].wait()
    halves(first, held[1][...], x_mine, x_other)
    copies[2].wait()
    copies[3].wait()
    halves(first, (held[2][...] * held[3][...]).astype(f32), stop_mine, stop_other)


def known_kernel(core, yc, pupil_mask, near, far, left, right, mine, other):
    first = core[1] == 0
    curved = stencil(first, yc[...], near[...], far[...], left[...], right[...])
    halves(first, curved - pupil_mask[...].astype(f32), mine, other)


def primal_kernel(core, new_a, new_b, far_a, far_b, x, out, near, far, head, tail):
    first = core[1] == 0
    mine = jnp.transpose(jnp.concatenate([new_a[...], new_b[...]], axis=0))
    other = jnp.transpose(jnp.concatenate([far_a[...], far_b[...]], axis=0))
    new = jnp.concatenate([jnp.where(first, mine, other), jnp.where(first, other, mine)], axis=1)
    out[...] = new
    put_edges(first, 2.0 * new - x[...], near, far, head, tail)


def dual_kernel(core, new, x, yc, near, far, left, right, out, *edges):
    first = core[1] == 0
    extended = 2.0 * new[...] - x[...]
    curved = stencil(first, extended, near[...], far[...], left[...], right[...])
    moved = yc[...] + step_dual * curved
    result = moved - step_dual * jnp.clip(moved / step_dual, -curvature_limit, curvature_limit)
    out[...] = result
    if edges:
        put_edges(first, result, *edges)


def focal_kernel(parts, yf, dark, out, *spread):
    fields = parts[0]
    for other in range(1, COLS):
        fields = fields + parts[other]
    shifted = yf[...] + step_dual * fields
    result = dark[...] * (shifted - step_dual * jnp.clip(shifted / step_dual, -contrast, contrast))
    out[...] = result
    if spread:
        for other in range(COLS):
            spread[0][other] = result


def fetch(pairs, sems):
    copies = [pltpu.make_async_copy(src, dst, sems.at[i]) for i, (src, dst) in enumerate(pairs)]
    for copy in copies:
        copy.start()
    return copies


def carry_kernel(core, y, table, mine, other, held, sems):
    waves, rows = y.shape[1], y.shape[0] * y.shape[2]
    copies = fetch([(table.at[w], held.at[w]) for w in range(waves)], sems)
    for w in range(waves):
        copies[w].wait()
        carried = dot3(y[:, w].reshape(rows, y.shape[3]), held[w], ((1,), (0,)))
        at = pl.ds(w * rows, rows)
        halves(core[1] == 0, carried, mine.at[at], other.at[at], turn=False)


def found_kernel(core, own_a, own_b, far_a, far_b, table, out):
    first = core[1] == 0
    waves, rows = out.shape[1], out.shape[0] * out.shape[2]
    for w in range(waves):
        at = pl.ds(w * rows, rows)
        own = jnp.concatenate([own_a[at, :], own_b[at, :]], axis=1)
        far = jnp.concatenate([far_a[at, :], far_b[at, :]], axis=1)
        left = jnp.concatenate([jnp.where(first, own, far), jnp.where(first, far, own)], axis=1)
        found = dot3(left, table[w], ((1,), (1,)))
        out[:, w] = found.reshape(out.shape[0], out.shape[2], out.shape[3])


def table_kernel(where, mine, other, top, rest, ready):
    ready[...] = jnp.zeros_like(ready)
    rows, b = mine.shape[3], pl.program_id(0)
    for at, block in ((0, mine), (rows, other)):
        large, small = split(block[:, 0].reshape(top.shape[1], rows))
        top[b, :, at : at + rows] = large
        rest[b, :, at : at + rows] = small


def back_kernel(t0, t1, t2, t3, top, rest, ready, out):
    for step, t in enumerate((t0, t1, t2, t3)):
        depth, wide = t.shape
        a, b = split(jnp.transpose(t[...]))
        blocks = slice(2 * step, 2 * step + 2)
        both = jnp.dot(
            jnp.concatenate([a, b], axis=0),
            top[blocks].reshape(depth, out.shape[1]),
            preferred_element_type=f32,
        )
        more = jnp.dot(a, rest[blocks].reshape(depth, out.shape[1]), preferred_element_type=f32)
        part = both[:wide] + (both[wide:] + more)
        out[...] = part if step == 0 else out[...] + part


def update_kernel(back, far, x0, x1, s0, s1, k0, k1, top, rest, new0, new1, l0, l1, l2, l3):
    rows = x0.shape[1]
    masked = []
    for i, (x, stop, known, new) in enumerate(((x0, s0, k0, new0), (x1, s1, k1, new1))):
        at = slice(i * rows, (i + 1) * rows)
        before = x[...]
        gradient = known[...] + stop[...] * (back[:, at] + far[:, at])
        after = jnp.clip(before - step_primal * gradient, 0.0, 1.0)
        new[...] = after
        masked.append(stop[...] * (2.0 * after - before))
    a, b = split(jnp.concatenate(masked, axis=1))
    both, wide = jnp.concatenate([a, b], axis=0), a.shape[0]
    dims = (((1,), (1,)), ((), ()))
    for step, left in enumerate((l0, l1, l2, l3)):
        depth = left.shape[0]
        blocks = slice(2 * step, 2 * step + 2)
        large = top[blocks].reshape(depth, both.shape[1])
        small = rest[blocks].reshape(depth, both.shape[1])
        one = lax.dot_general(large, both, dims, preferred_element_type=f32)
        two = lax.dot_general(small, a, dims, preferred_element_type=f32)
        left[...] = one[:, :wide] + (one[:, wide:] + two)


def results(shapes, far):
    kinds = [pltpu.HBM(shape, f32) if i in far else jax.ShapeDtypeStruct(shape, f32) for i, shape in enumerate(shapes)]
    places = [
        pl.BlockSpec(shape, lambda i, rank=len(shape): (0,) * rank) if i in far else in_vmem
        for i, shape in enumerate(shapes)
    ]
    return {"grid": (1,), "out_shape": kinds, "out_specs": places}


def whole(kernel, core, args, shapes, far=()):
    return pl.pallas_call(
        kernel,
        **results(shapes, far),
        in_specs=[in_smem] + [in_vmem] * len(args) if core is not None else [in_vmem] * len(args),
        cost_estimate=cost(4 << 20),
        compiler_params=pltpu.CompilerParams(vmem_limit_bytes=LIMIT),
    )(*(([core] if core is not None else []) + list(args)))


def per_device(
    transmission,
    dual_focal,
    dual_curvature,
    pupil_mask,
    lyot_mask,
    dark_mask,
    focal_rows,
    focal_cols,
):
    z = lax.axis_index("z").astype(jnp.int32)
    core = lax.axis_index("core").astype(jnp.int32)
    core = where = jnp.stack([z, core])
    waves, fields, rows = focal_rows.shape
    cols = focal_cols.shape[2]
    part = fields // (ZS * CORES)
    own = dual_focal.shape[0]
    count = waves * part
    half = cols // CORES
    wide = half // CHUNKS
    tile, line = (rows, cols), [(1, cols)] * 4
    piece = (half, rows)

    dark = jnp.transpose(dark_mask.astype(f32), (1, 0, 2))
    dual_f = jnp.transpose(dual_focal, (1, 0, 2)) * dark
    spread = jnp.broadcast_to(dual_f[None], (COLS,) + dual_f.shape)

    other_rows = swap_core(focal_rows)
    started = pl.pallas_call(
        start_kernel,
        out_shape=[jax.ShapeDtypeStruct(shape, f32) for shape in line + [piece] * 4],
        in_specs=[in_smem] + [in_hbm] * 4,
        out_specs=[in_vmem] * 8,
        scratch_shapes=[pltpu.VMEM(tile, f32)] * 2 + [pltpu.VMEM(tile, jnp.int32)] * 2 + [pltpu.SemaphoreType.DMA((4,))],
        cost_estimate=cost(6 << 20),
        compiler_params=pltpu.CompilerParams(vmem_limit_bytes=LIMIT),
    )(core, *(stay(cells) for cells in (dual_curvature, transmission, pupil_mask, lyot_mask)))
    edges, x_mine, x_other, stop_mine, stop_other = started[:4], *started[4:]

    def block_of(b, where):
        return (0, (where[0] + b // CORES) % ZS * CORES + (where[1] + b) % CORES, 0, 0)

    def table_of(mine, other):
        return pl.pallas_call(
            table_kernel,
            grid_spec=pltpu.PrefetchScalarGridSpec(
                num_scalar_prefetch=1,
                grid=(ZS * CORES,),
                in_specs=[pl.BlockSpec((waves, 1, part, rows), block_of)] * 2,
                out_specs=[in_vmem] * 3,
            ),
            out_shape=[pltpu.VMEM((ZS * CORES, count, 2 * rows), bf16)] * 2 + [jax.ShapeDtypeStruct((8, 128), f32)],
            cost_estimate=cost(20 << 20),
            compiler_params=pltpu.CompilerParams(vmem_limit_bytes=LIMIT),
        )(where, *(stay(half.reshape(waves, ZS * CORES, part, rows)) for half in (mine, other)))

    *table, ready = table_of(focal_rows, other_rows)
    table = [hold(half) for half in table]
    primal_half = (x_mine, swap_core(x_other))
    stop_half = (stop_mine, swap_core(stop_other))

    def known(yc, around):
        mine, other = whole(known_kernel, core, (yc, pupil_mask, *around), [piece] * 2)
        return mine, swap_core(other)

    def product(kernel, args, shapes, specs, moved, scratch=(), far=()):
        return pl.pallas_call(
            kernel,
            **results(shapes, far),
            in_specs=specs,
            scratch_shapes=list(scratch),
            cost_estimate=cost(moved << 20),
            compiler_params=pltpu.CompilerParams(vmem_limit_bytes=LIMIT),
        )(*args)

    def carry(gathered):
        specs = [in_smem, in_vmem, in_hbm]
        scratch = [pltpu.VMEM((waves, fields, cols), f32), pltpu.SemaphoreType.DMA((waves,))]
        args = (core, gathered, stay(focal_cols))
        return product(carry_kernel, args, [(count, half)] * 2, specs, 6, scratch)

    def find(sums, fars):
        specs = [in_smem] + [in_vmem] * 5
        args = (core, *sums, *fars, hold(focal_cols))
        return product(found_kernel, args, [(COLS, waves, own, fields)], specs, 8, far=(0,))[0]

    def gather(block):
        return block, shift_z(block, -1), shift_z(block, -2), shift_z(block, -3)

    def backward(full):
        specs = [in_vmem] * 7
        back = product(back_kernel, (*full, *table, ready), [(wide, CORES * rows)], specs, 12)[0]
        return back, lax.ppermute(back, "wave", [(0, 1), (1, 0)])

    def update(chunk, known_half, back, far):
        cut = pl.BlockSpec((wide, rows), lambda i: (chunk, 0))
        specs = [in_vmem] * 2 + [cut] * 6 + [in_vmem] * 2
        args = (back, far, *primal_half, *stop_half, *known_half, *table)
        shapes = [(wide, rows)] * 2 + [(CORES * count, wide)] * ZS
        new0, new1, *left = product(update_kernel, args, shapes, specs, 1)
        return (new0, new1), left

    def scatter(left):
        return left[0] + shift_z(left[1], 1) + shift_z(left[2], 2) + shift_z(left[3], 3)

    primal, dual_c = transmission, dual_curvature
    gathered = lax.all_to_all(spread, COL, 0, 0, tiled=True)
    gathered, *around = tie((gathered, *exchange_rows(*edges[:2])))
    for iteration in range(ITERS):
        last = iteration == ITERS - 1
        mine, other = carry(gathered)
        received = swap_core(other)
        pair = jnp.concatenate([mine, received], axis=0)
        pair_a, pair_b = pair[:, :wide], pair[:, wide:]
        full_a = gather(pair_a)
        if iteration == 0:
            pair_b, ready = tie((pair_b, ready))
        else:
            pair_b, *near = tie((pair_b, full_a[1], full_a[3]))
            full_a = full_a[0], near[0], full_a[2], near[1]
        full_b = gather(pair_b)
        back_a, far_a = backward(full_a)
        if iteration == 0:
            back_a, *ends = tie((back_a, *edges[2:]))
            known_half = known(dual_c, (*around, *exchange_cols(*ends)))
        back_b, far_b = backward(full_b)
        far_a, back_b = tie((far_a, back_b))
        new_a, left_a = update(0, known_half, back_a, far_a)
        sum_a = scatter(left_a)
        far_b, new_a = tie((far_b, new_a))
        new_b, left_b = update(1, known_half, back_b, far_b)
        sum_b = scatter(left_b)

        moved = swap_core(new_a[1]), swap_core(new_b[1])
        sum_a, *moved = tie((sum_a, *moved))
        args = (new_a[0], new_b[0], *moved, primal)
        primal_new, *edges = whole(primal_kernel, core, args, [tile] + line)
        *around, late = exchange(edges)
        sum_a, sum_b, primal_new, *around = tie((sum_a, sum_b, primal_new, *around))

        fars = swap_core(sum_a[count:]), swap_core(sum_b[count:])
        found, *around = tie((find((sum_a[:count], sum_b[:count]), fars), *around))
        parts = lax.all_to_all(found, COL, 0, 0, tiled=True)
        args = (primal_new, primal, dual_c, *around, late)
        dual_c, *edges = whole(dual_kernel, core, args, [tile] + ([] if last else line), () if last else (0, 1, 2, 3, 4))
        primal = primal_new
        parts, dual_c, *edges = tie((parts, dual_c, *edges))
        if last:
            dual_f = whole(focal_kernel, None, (parts, dual_f, dark), [dual_f.shape])[0]
            break
        primal_half = tuple(jnp.concatenate(pieces, axis=0) for pieces in zip(new_a, new_b))
        dual_f, spread = whole(focal_kernel, None, (parts, dual_f, dark), [dual_f.shape, spread.shape], (1,))
        gathered = lax.all_to_all(spread, COL, 0, 0, tiled=True)
        gathered, *around = tie((gathered, *exchange(edges)))
        known_half = known(dual_c, around)
    return (primal, jnp.transpose(dual_f, (1, 0, 2)), dual_c)


def solution(mesh):
    parts = Mesh(
        mesh.devices.reshape(ZS, CORES, 2, COLS // 2, WAVES),
        ("z", "core", "xl", "y", "wave"),
    )
    return jax.shard_map(
        per_device,
        mesh=parts,
        in_specs=(
            P(ROW, COL),
            P(ROW + COL, "wave", None),
            P(ROW, COL),
            P(ROW, COL),
            P(ROW, COL),
            P(ROW + COL, "wave", None),
            P("wave", None, ROW),
            P("wave", None, COL),
        ),
        out_specs=(P(ROW, COL), P(ROW + COL, "wave", None), P(ROW, COL)),
        check_vma=False,
    )
```

```python
import functools

import jax
import jax.numpy as jnp
from jax import lax
from jax.experimental import pallas as pl
from jax.experimental.pallas import tpu as pltpu
from jax.sharding import Mesh, PartitionSpec as P

ITERS = 2

step_primal = 0.12
step_dual = 0.2
contrast = 0.5
curvature_limit = 0.1

ROW = ("z", "core")
COL = ("xl", "y")
ZS, CORES, COLS, WAVES = 4, 2, 8, 2
CHUNKS = 2
LIMIT = 16 * 1024 * 1024
f32 = jnp.float32
tie = lax.optimization_barrier
in_vmem = pl.BlockSpec(memory_space=pltpu.VMEM)
in_smem = pl.BlockSpec(memory_space=pltpu.SMEM)
in_hbm = pl.BlockSpec(memory_space=pltpu.HBM)
bf16 = jnp.bfloat16


def hold(cells):
    return pltpu.with_memory_space_constraint(cells, pltpu.VMEM)


def stay(cells):
    return pltpu.with_memory_space_constraint(cells, pltpu.HBM)


def cost(moved):
    return pl.CostEstimate(flops=0, bytes_accessed=moved, transcendentals=0)


def swap_core(cells):
    return lax.ppermute(cells, "core", [(0, 1), (1, 0)])


def shift_z(cells, by):
    return lax.ppermute(cells, "z", [(i, (i + by) % ZS) for i in range(ZS)])


def split(values):
    top = values.astype(jnp.bfloat16)
    return top, (values - top.astype(f32)).astype(jnp.bfloat16)


def dot3(a, b, dims):
    (a1, a2), (b1, b2) = split(a), split(b)
    mul = functools.partial(lax.dot_general, dimension_numbers=(dims, ((), ())), preferred_element_type=f32)
    both, rows = mul(jnp.concatenate([a1, a2], axis=0), b1), a.shape[0]
    return both[:rows] + (mul(a1, b2) + both[rows:])


def exchange(edges):
    return *exchange_rows(*edges[:2]), *exchange_cols(*edges[2:])


def exchange_rows(near, far):
    pairs = [(i, i + 1) for i in range(1, ZS * CORES - 1, 2)]
    return swap_core(near), lax.ppermute(far, ROW, pairs + [(b, a) for a, b in pairs])


def exchange_cols(head, tail):
    return (
        lax.ppermute(tail, COL, [(i, i + 1) for i in range(COLS - 1)]),
        lax.ppermute(head, COL, [(i + 1, i) for i in range(COLS - 1)]),
    )


def put_edges(first, cells, near_ref, far_ref, head_ref, tail_ref):
    rows, cols = cells.shape
    top, bottom = cells[0:1, :], cells[rows - 1 : rows, :]
    near_ref[...] = jnp.where(first, bottom, top)
    far_ref[...] = jnp.where(first, top, bottom)
    head_ref[...] = jnp.transpose(cells[:, :128])[0:1, :]
    tail_ref[...] = jnp.transpose(cells[:, cols - 128 :])[127:128, :]


def stencil(first, cells, near, far, left, right):
    rows, cols = cells.shape
    above, below = jnp.where(first, far, near), jnp.where(first, near, far)
    row = lax.broadcasted_iota(jnp.int32, cells.shape, 0)
    col = lax.broadcasted_iota(jnp.int32, cells.shape, 1)
    left = jnp.transpose(jnp.broadcast_to(left, (128, rows)))[:, 0:1]
    right = jnp.transpose(jnp.broadcast_to(right, (128, rows)))[:, 0:1]
    down = jnp.where(row == 0, above, pltpu.roll(cells, 1, 0))
    up = jnp.where(row == rows - 1, below, pltpu.roll(cells, rows - 1, 0))
    after = jnp.where(col == 0, left, pltpu.roll(cells, 1, 1))
    before = jnp.where(col == cols - 1, right, pltpu.roll(cells, cols - 1, 1))
    return 0.25 * (down + up + after + before) - cells


def halves(first, cells, mine_ref, other_ref, turn=True):
    half = cells.shape[1] // 2
    a, b = cells[:, :half], cells[:, half:]
    mine, other = jnp.where(first, a, b), jnp.where(first, b, a)
    mine_ref[...] = jnp.transpose(mine) if turn else mine
    other_ref[...] = jnp.transpose(other) if turn else other


def start_kernel(core, yc, x, pupil_mask, lyot_mask, *refs):
    near, far, head, tail, x_mine, x_other, stop_mine, stop_other, *held, sems = refs
    first = core[1] == 0
    copies = fetch(list(zip((yc, x, pupil_mask, lyot_mask), held)), sems)
    copies[0].wait()
    put_edges(first, held[0][...], near, far, head, tail)
    copies[1].wait()
    halves(first, held[1][...], x_mine, x_other)
    copies[2].wait()
    copies[3].wait()
    halves(first, (held[2][...] * held[3][...]).astype(f32), stop_mine, stop_other)


def known_kernel(core, yc, pupil_mask, near, far, left, right, mine, other):
    first = core[1] == 0
    curved = stencil(first, yc[...], near[...], far[...], left[...], right[...])
    halves(first, curved - pupil_mask[...].astype(f32), mine, other)


def primal_kernel(core, new_a, new_b, far_a, far_b, x, out, near, far, head, tail):
    first = core[1] == 0
    mine = jnp.transpose(jnp.concatenate([new_a[...], new_b[...]], axis=0))
    other = jnp.transpose(jnp.concatenate([far_a[...], far_b[...]], axis=0))
    new = jnp.concatenate([jnp.where(first, mine, other), jnp.where(first, other, mine)], axis=1)
    out[...] = new
    put_edges(first, 2.0 * new - x[...], near, far, head, tail)


def dual_kernel(core, new, x, yc, near, far, left, right, out, *edges):
    first = core[1] == 0
    extended = 2.0 * new[...] - x[...]
    curved = stencil(first, extended, near[...], far[...], left[...], right[...])
    moved = yc[...] + step_dual * curved
    result = moved - step_dual * jnp.clip(moved / step_dual, -curvature_limit, curvature_limit)
    out[...] = result
    if edges:
        put_edges(first, result, *edges)


def focal_kernel(parts, yf, dark, out, *spread):
    fields = parts[0]
    for other in range(1, COLS):
        fields = fields + parts[other]
    shifted = yf[...] + step_dual * fields
    result = dark[...] * (shifted - step_dual * jnp.clip(shifted / step_dual, -contrast, contrast))
    out[...] = result
    if spread:
        for other in range(COLS):
            spread[0][other] = result


def fetch(pairs, sems):
    copies = [pltpu.make_async_copy(src, dst, sems.at[i]) for i, (src, dst) in enumerate(pairs)]
    for copy in copies:
        copy.start()
    return copies


def carry_kernel(core, y, table, mine, other, held, sems):
    waves, rows = y.shape[1], y.shape[0] * y.shape[2]
    copies = fetch([(table.at[w], held.at[w]) for w in range(waves)], sems)
    for w in range(waves):
        copies[w].wait()
        carried = dot3(y[:, w].reshape(rows, y.shape[3]), held[w], ((1,), (0,)))
        at = pl.ds(w * rows, rows)
        halves(core[1] == 0, carried, mine.at[at], other.at[at], turn=False)


def found_kernel(core, own_a, own_b, far_a, far_b, table, out):
    first = core[1] == 0
    waves, rows = out.shape[1], out.shape[0] * out.shape[2]
    for w in range(waves):
        at = pl.ds(w * rows, rows)
        own = jnp.concatenate([own_a[at, :], own_b[at, :]], axis=1)
        far = jnp.concatenate([far_a[at, :], far_b[at, :]], axis=1)
        left = jnp.concatenate([jnp.where(first, own, far), jnp.where(first, far, own)], axis=1)
        found = dot3(left, table[w], ((1,), (1,)))
        out[:, w] = found.reshape(out.shape[0], out.shape[2], out.shape[3])


def table_kernel(where, mine, other, table, ready):
    ready[...] = jnp.zeros_like(ready)
    rows, b = mine.shape[3], pl.program_id(0)
    top, rest = table.at[0], table.at[1]
    for at, block in ((0, mine), (rows, other)):
        large, small = split(block[:, 0].reshape(top.shape[1], rows))
        top[b, :, at : at + rows] = large
        rest[b, :, at : at + rows] = small


def back_kernel(t0, t1, t2, t3, table, ready, out):
    top, rest = table.at[0], table.at[1]
    for step, t in enumerate((t0, t1, t2, t3)):
        depth, wide = t.shape
        a, b = split(jnp.transpose(t[...]))
        blocks = slice(2 * step, 2 * step + 2)
        both = jnp.dot(
            jnp.concatenate([a, b], axis=0),
            top[blocks].reshape(depth, out.shape[1]),
            preferred_element_type=f32,
        )
        more = jnp.dot(a, rest[blocks].reshape(depth, out.shape[1]), preferred_element_type=f32)
        part = both[:wide] + (both[wide:] + more)
        out[...] = part if step == 0 else out[...] + part


def update_kernel(back, far, x0, x1, s0, s1, k0, k1, table, new0, new1, l0, l1, l2, l3):
    top, rest = table.at[0], table.at[1]
    rows = x0.shape[1]
    masked = []
    for i, (x, stop, known, new) in enumerate(((x0, s0, k0, new0), (x1, s1, k1, new1))):
        at = slice(i * rows, (i + 1) * rows)
        before = x[...]
        gradient = known[...] + stop[...] * (back[:, at] + far[:, at])
        after = jnp.clip(before - step_primal * gradient, 0.0, 1.0)
        new[...] = after
        masked.append(stop[...] * (2.0 * after - before))
    a, b = split(jnp.concatenate(masked, axis=1))
    both, wide = jnp.concatenate([a, b], axis=0), a.shape[0]
    dims = (((1,), (1,)), ((), ()))
    for step, left in enumerate((l0, l1, l2, l3)):
        depth = left.shape[0]
        blocks = slice(2 * step, 2 * step + 2)
        large = top[blocks].reshape(depth, both.shape[1])
        small = rest[blocks].reshape(depth, both.shape[1])
        one = lax.dot_general(large, both, dims, preferred_element_type=f32)
        two = lax.dot_general(small, a, dims, preferred_element_type=f32)
        left[...] = one[:, :wide] + (one[:, wide:] + two)


def results(shapes, far):
    kinds = [pltpu.HBM(shape, f32) if i in far else jax.ShapeDtypeStruct(shape, f32) for i, shape in enumerate(shapes)]
    places = [
        pl.BlockSpec(shape, lambda i, rank=len(shape): (0,) * rank) if i in far else in_vmem
        for i, shape in enumerate(shapes)
    ]
    return {"grid": (1,), "out_shape": kinds, "out_specs": places}


def whole(kernel, core, args, shapes, far=()):
    return pl.pallas_call(
        kernel,
        **results(shapes, far),
        in_specs=[in_smem] + [in_vmem] * len(args) if core is not None else [in_vmem] * len(args),
        cost_estimate=cost(4 << 20),
        compiler_params=pltpu.CompilerParams(vmem_limit_bytes=LIMIT),
    )(*(([core] if core is not None else []) + list(args)))


def per_device(
    transmission,
    dual_focal,
    dual_curvature,
    pupil_mask,
    lyot_mask,
    dark_mask,
    focal_rows,
    focal_cols,
):
    z = lax.axis_index("z").astype(jnp.int32)
    core = lax.axis_index("core").astype(jnp.int32)
    core = where = jnp.stack([z, core])
    waves, fields, rows = focal_rows.shape
    cols = focal_cols.shape[2]
    part = fields // (ZS * CORES)
    own = dual_focal.shape[0]
    count = waves * part
    half = cols // CORES
    wide = half // CHUNKS
    tile, line = (rows, cols), [(1, cols)] * 4
    piece = (half, rows)

    dark = jnp.transpose(dark_mask.astype(f32), (1, 0, 2))
    dual_f = jnp.transpose(dual_focal, (1, 0, 2)) * dark
    spread = jnp.broadcast_to(dual_f[None], (COLS,) + dual_f.shape)

    other_rows = swap_core(focal_rows)
    started = pl.pallas_call(
        start_kernel,
        out_shape=[jax.ShapeDtypeStruct(shape, f32) for shape in line + [piece] * 4],
        in_specs=[in_smem] + [in_hbm] * 4,
        out_specs=[in_vmem] * 8,
        scratch_shapes=[pltpu.VMEM(tile, f32)] * 2 + [pltpu.VMEM(tile, jnp.int32)] * 2 + [pltpu.SemaphoreType.DMA((4,))],
        cost_estimate=cost(6 << 20),
        compiler_params=pltpu.CompilerParams(vmem_limit_bytes=LIMIT),
    )(core, *(stay(cells) for cells in (dual_curvature, transmission, pupil_mask, lyot_mask)))
    edges, x_mine, x_other, stop_mine, stop_other = started[:4], *started[4:]

    def block_of(b, where):
        return (0, (where[0] + b // CORES) % ZS * CORES + (where[1] + b) % CORES, 0, 0)

    def table_of(mine, other):
        return pl.pallas_call(
            table_kernel,
            grid_spec=pltpu.PrefetchScalarGridSpec(
                num_scalar_prefetch=1,
                grid=(ZS * CORES,),
                in_specs=[pl.BlockSpec((waves, 1, part, rows), block_of)] * 2,
                out_specs=[in_vmem] * 2,
            ),
            out_shape=[pltpu.VMEM((2, ZS * CORES, count, 2 * rows), bf16), jax.ShapeDtypeStruct((8, 128), f32)],
            cost_estimate=cost(20 << 20),
            compiler_params=pltpu.CompilerParams(vmem_limit_bytes=LIMIT),
        )(where, *(stay(half.reshape(waves, ZS * CORES, part, rows)) for half in (mine, other)))

    table, ready = table_of(focal_rows, other_rows)
    table = hold(table)
    primal_half = (x_mine, swap_core(x_other))
    stop_half = (stop_mine, swap_core(stop_other))

    def known(yc, around):
        mine, other = whole(known_kernel, core, (yc, pupil_mask, *around), [piece] * 2)
        return mine, swap_core(other)

    def product(kernel, args, shapes, specs, moved, scratch=(), far=()):
        return pl.pallas_call(
            kernel,
            **results(shapes, far),
            in_specs=specs,
            scratch_shapes=list(scratch),
            cost_estimate=cost(moved << 20),
            compiler_params=pltpu.CompilerParams(vmem_limit_bytes=LIMIT // 2),
        )(*args)

    def carry(gathered):
        specs = [in_smem, in_vmem, in_hbm]
        scratch = [pltpu.VMEM((waves, fields, cols), f32), pltpu.SemaphoreType.DMA((waves,))]
        args = (core, gathered, stay(focal_cols))
        return product(carry_kernel, args, [(count, half)] * 2, specs, 6, scratch)

    def find(sums, fars):
        specs = [in_smem] + [in_vmem] * 5
        args = (core, *sums, *fars, hold(focal_cols))
        return product(found_kernel, args, [(COLS, waves, own, fields)], specs, 8, far=(0,))[0]

    def gather(block):
        return block, shift_z(block, -1), shift_z(block, -2), shift_z(block, -3)

    def backward(full):
        specs = [in_vmem] * 6
        back = product(back_kernel, (*full, table, ready), [(wide, CORES * rows)], specs, 12)[0]
        return back, lax.ppermute(back, "wave", [(0, 1), (1, 0)])

    def update(chunk, known_half, back, far):
        cut = pl.BlockSpec((wide, rows), lambda i: (chunk, 0))
        specs = [in_vmem] * 2 + [cut] * 6 + [in_vmem]
        args = (back, far, *primal_half, *stop_half, *known_half, table)
        shapes = [(wide, rows)] * 2 + [(CORES * count, wide)] * ZS
        new0, new1, *left = product(update_kernel, args, shapes, specs, 1)
        return (new0, new1), left

    def scatter(left):
        return left[0] + shift_z(left[1], 1) + shift_z(left[2], 2) + shift_z(left[3], 3)

    primal, dual_c = transmission, dual_curvature
    gathered = lax.all_to_all(spread, COL, 0, 0, tiled=True)
    gathered, *around = tie((gathered, *exchange_rows(*edges[:2])))
    for iteration in range(ITERS):
        last = iteration == ITERS - 1
        mine, other = carry(gathered)
        received = swap_core(other)
        pair = jnp.concatenate([mine, received], axis=0)
        pair_a, pair_b = pair[:, :wide], pair[:, wide:]
        if iteration == 0:
            full_a = gather(pair_a)
            pair_b, ready = tie((pair_b, ready))
        else:
            pair_a, *ends = tie((pair_a, *edges[2:]))
            full_a = gather(pair_a)
            pair_b, *ends = tie((pair_b, *exchange_cols(*ends)))
            known_half = known(dual_c, (*around, *ends))
        full_b = gather(pair_b)
        back_a, far_a = backward(full_a)
        if iteration == 0:
            first_b, *ends = tie((full_b[1], *edges[2:]))
            full_b = full_b[0], first_b, *full_b[2:]
            known_half = known(dual_c, (*around, *exchange_cols(*ends)))
        back_b, far_b = backward(full_b)
        far_a, back_b = tie((far_a, back_b))
        new_a, left_a = update(0, known_half, back_a, far_a)
        sum_a = scatter(left_a)
        far_b, new_a = tie((far_b, new_a))
        new_b, left_b = update(1, known_half, back_b, far_b)
        sum_b = scatter(left_b)

        moved = swap_core(new_a[1]), swap_core(new_b[1])
        sum_a, *moved = tie((sum_a, *moved))
        args = (new_a[0], new_b[0], *moved, primal)
        primal_new, *edges = whole(primal_kernel, core, args, [tile] + line)
        *around, late = exchange(edges)
        sum_a, sum_b, primal_new, *around = tie((sum_a, sum_b, primal_new, *around))

        fars = swap_core(sum_a[count:]), swap_core(sum_b[count:])
        found, *around = tie((find((sum_a[:count], sum_b[:count]), fars), *around))
        parts = lax.all_to_all(found, COL, 0, 0, tiled=True)
        args = (primal_new, primal, dual_c, *around, late)
        dual_c, *edges = whole(dual_kernel, core, args, [tile] + ([] if last else line), () if last else (0, 1, 2, 3, 4))
        primal = primal_new
        parts, dual_c, *edges = tie((parts, dual_c, *edges))
        if last:
            dual_f = whole(focal_kernel, None, (parts, dual_f, dark), [dual_f.shape])[0]
            break
        primal_half = tuple(jnp.concatenate(pieces, axis=0) for pieces in zip(new_a, new_b))
        dual_f, spread = whole(focal_kernel, None, (parts, dual_f, dark), [dual_f.shape, spread.shape], (1,))
        gathered = lax.all_to_all(spread, COL, 0, 0, tiled=True)
        gathered, *around = tie((gathered, *exchange_rows(*edges[:2])))
    return (primal, jnp.transpose(dual_f, (1, 0, 2)), dual_c)


def solution(mesh):
    parts = Mesh(
        mesh.devices.reshape(ZS, CORES, 2, COLS // 2, WAVES),
        ("z", "core", "xl", "y", "wave"),
    )
    return jax.shard_map(
        per_device,
        mesh=parts,
        in_specs=(
            P(ROW, COL),
            P(ROW + COL, "wave", None),
            P(ROW, COL),
            P(ROW, COL),
            P(ROW, COL),
            P(ROW + COL, "wave", None),
            P("wave", None, ROW),
            P("wave", None, COL),
        ),
        out_specs=(P(ROW, COL), P(ROW + COL, "wave", None), P(ROW, COL)),
        check_vma=False,
    )
```

```python
import functools

import jax
import jax.numpy as jnp
from jax import lax
from jax.experimental import pallas as pl
from jax.experimental.pallas import tpu as pltpu
from jax.sharding import Mesh, PartitionSpec as P

ITERS = 2

step_primal = 0.12
step_dual = 0.2
contrast = 0.5
curvature_limit = 0.1

ROW = ("z", "core")
COL = ("xl", "y")
ZS, CORES, COLS, WAVES = 4, 2, 8, 2
CHUNKS = 2
LIMIT = 16 * 1024 * 1024
f32 = jnp.float32
tie = lax.optimization_barrier
in_vmem = pl.BlockSpec(memory_space=pltpu.VMEM)
in_smem = pl.BlockSpec(memory_space=pltpu.SMEM)
in_hbm = pl.BlockSpec(memory_space=pltpu.HBM)
bf16 = jnp.bfloat16


def hold(cells):
    return pltpu.with_memory_space_constraint(cells, pltpu.VMEM)


def stay(cells):
    return pltpu.with_memory_space_constraint(cells, pltpu.HBM)


def cost(moved):
    return pl.CostEstimate(flops=0, bytes_accessed=moved, transcendentals=0)


def swap_core(cells):
    return lax.ppermute(cells, "core", [(0, 1), (1, 0)])


def shift_z(cells, by):
    return lax.ppermute(cells, "z", [(i, (i + by) % ZS) for i in range(ZS)])


def split(values):
    top = values.astype(jnp.bfloat16)
    return top, (values - top.astype(f32)).astype(jnp.bfloat16)


def dot3(a, b, dims):
    (a1, a2), (b1, b2) = split(a), split(b)
    mul = functools.partial(lax.dot_general, dimension_numbers=(dims, ((), ())), preferred_element_type=f32)
    both, rows = mul(jnp.concatenate([a1, a2], axis=0), b1), a.shape[0]
    return both[:rows] + (mul(a1, b2) + both[rows:])


def exchange(edges):
    return *exchange_rows(*edges[:2]), *exchange_cols(*edges[2:])


def exchange_rows(near, far):
    pairs = [(i, i + 1) for i in range(1, ZS * CORES - 1, 2)]
    return swap_core(near), lax.ppermute(far, ROW, pairs + [(b, a) for a, b in pairs])


def exchange_cols(head, tail):
    return (
        lax.ppermute(tail, COL, [(i, i + 1) for i in range(COLS - 1)]),
        lax.ppermute(head, COL, [(i + 1, i) for i in range(COLS - 1)]),
    )


def put_edges(first, cells, near_ref, far_ref, head_ref, tail_ref):
    rows, cols = cells.shape
    top, bottom = cells[0:1, :], cells[rows - 1 : rows, :]
    near_ref[...] = jnp.where(first, bottom, top)
    far_ref[...] = jnp.where(first, top, bottom)
    head_ref[...] = jnp.transpose(cells[:, :128])[0:1, :]
    tail_ref[...] = jnp.transpose(cells[:, cols - 128 :])[127:128, :]


def stencil(first, cells, near, far, left, right):
    rows, cols = cells.shape
    above, below = jnp.where(first, far, near), jnp.where(first, near, far)
    row = lax.broadcasted_iota(jnp.int32, cells.shape, 0)
    col = lax.broadcasted_iota(jnp.int32, cells.shape, 1)
    left = jnp.transpose(jnp.broadcast_to(left, (128, rows)))[:, 0:1]
    right = jnp.transpose(jnp.broadcast_to(right, (128, rows)))[:, 0:1]
    down = jnp.where(row == 0, above, pltpu.roll(cells, 1, 0))
    up = jnp.where(row == rows - 1, below, pltpu.roll(cells, rows - 1, 0))
    after = jnp.where(col == 0, left, pltpu.roll(cells, 1, 1))
    before = jnp.where(col == cols - 1, right, pltpu.roll(cells, cols - 1, 1))
    return 0.25 * (down + up + after + before) - cells


def halves(first, cells, mine_ref, other_ref, turn=True):
    half = cells.shape[1] // 2
    a, b = cells[:, :half], cells[:, half:]
    mine, other = jnp.where(first, a, b), jnp.where(first, b, a)
    mine_ref[...] = jnp.transpose(mine) if turn else mine
    other_ref[...] = jnp.transpose(other) if turn else other


def start_kernel(core, yc, x, pupil_mask, lyot_mask, *refs):
    near, far, head, tail, x_mine, x_other, stop_mine, stop_other, *held, sems = refs
    first = core[1] == 0
    copies = fetch(list(zip((yc, x, pupil_mask, lyot_mask), held)), sems)
    copies[0].wait()
    put_edges(first, held[0][...], near, far, head, tail)
    copies[1].wait()
    halves(first, held[1][...], x_mine, x_other)
    copies[2].wait()
    copies[3].wait()
    halves(first, (held[2][...] * held[3][...]).astype(f32), stop_mine, stop_other)


def known_kernel(core, yc, pupil_mask, near, far, left, right, *refs):
    mine, other = refs[-2:]
    first = core[1] == 0
    curved = stencil(first, yc[...], near[...], far[...], left[...], right[...])
    halves(first, curved - pupil_mask[...].astype(f32), mine, other)


def primal_kernel(core, new_a, new_b, far_a, far_b, x, out, near, far, head, tail):
    first = core[1] == 0
    mine = jnp.transpose(jnp.concatenate([new_a[...], new_b[...]], axis=0))
    other = jnp.transpose(jnp.concatenate([far_a[...], far_b[...]], axis=0))
    new = jnp.concatenate([jnp.where(first, mine, other), jnp.where(first, other, mine)], axis=1)
    out[...] = new
    put_edges(first, 2.0 * new - x[...], near, far, head, tail)


def dual_kernel(core, new, x, yc, near, far, left, right, out, *edges):
    first = core[1] == 0
    extended = 2.0 * new[...] - x[...]
    curved = stencil(first, extended, near[...], far[...], left[...], right[...])
    moved = yc[...] + step_dual * curved
    result = moved - step_dual * jnp.clip(moved / step_dual, -curvature_limit, curvature_limit)
    out[...] = result
    if edges:
        put_edges(first, result, *edges)


def focal_kernel(parts, yf, dark, out, *spread):
    fields = parts[0]
    for other in range(1, COLS):
        fields = fields + parts[other]
    shifted = yf[...] + step_dual * fields
    result = dark[...] * (shifted - step_dual * jnp.clip(shifted / step_dual, -contrast, contrast))
    out[...] = result
    if spread:
        for other in range(COLS):
            spread[0][other] = result


def fetch(pairs, sems):
    copies = [pltpu.make_async_copy(src, dst, sems.at[i]) for i, (src, dst) in enumerate(pairs)]
    for copy in copies:
        copy.start()
    return copies


def carry_kernel(core, y, table, mine, other, held, sems):
    waves, rows = y.shape[1], y.shape[0] * y.shape[2]
    copies = fetch([(table.at[w], held.at[w]) for w in range(waves)], sems)
    for w in range(waves):
        copies[w].wait()
        carried = dot3(y[:, w].reshape(rows, y.shape[3]), held[w], ((1,), (0,)))
        at = pl.ds(w * rows, rows)
        halves(core[1] == 0, carried, mine.at[at], other.at[at], turn=False)


def found_kernel(core, own_a, own_b, far_a, far_b, table, out):
    first = core[1] == 0
    waves, rows = out.shape[1], out.shape[0] * out.shape[2]
    for w in range(waves):
        at = pl.ds(w * rows, rows)
        own = jnp.concatenate([own_a[at, :], own_b[at, :]], axis=1)
        far = jnp.concatenate([far_a[at, :], far_b[at, :]], axis=1)
        left = jnp.concatenate([jnp.where(first, own, far), jnp.where(first, far, own)], axis=1)
        found = dot3(left, table[w], ((1,), (1,)))
        out[:, w] = found.reshape(out.shape[0], out.shape[2], out.shape[3])


def table_kernel(where, mine, other, top, rest, ready):
    ready[...] = jnp.zeros_like(ready)
    rows, b = mine.shape[3], pl.program_id(0)
    for at, block in ((0, mine), (rows, other)):
        large, small = split(block[:, 0].reshape(top.shape[1], rows))
        top[b, :, at : at + rows] = large
        rest[b, :, at : at + rows] = small


def back_kernel(t0, t1, t2, t3, top, rest, ready, out):
    for step, t in enumerate((t0, t1, t2, t3)):
        depth, wide = t.shape
        a, b = split(jnp.transpose(t[...]))
        blocks = slice(2 * step, 2 * step + 2)
        both = jnp.dot(
            jnp.concatenate([a, b], axis=0),
            top[blocks].reshape(depth, out.shape[1]),
            preferred_element_type=f32,
        )
        more = jnp.dot(a, rest[blocks].reshape(depth, out.shape[1]), preferred_element_type=f32)
        part = both[:wide] + (both[wide:] + more)
        out[...] = part if step == 0 else out[...] + part


def update_kernel(back, far, x0, x1, s0, s1, k0, k1, top, rest, new0, new1, l0, l1, l2, l3):
    rows = x0.shape[1]
    masked = []
    for i, (x, stop, known, new) in enumerate(((x0, s0, k0, new0), (x1, s1, k1, new1))):
        at = slice(i * rows, (i + 1) * rows)
        before = x[...]
        gradient = known[...] + stop[...] * (back[:, at] + far[:, at])
        after = jnp.clip(before - step_primal * gradient, 0.0, 1.0)
        new[...] = after
        masked.append(stop[...] * (2.0 * after - before))
    a, b = split(jnp.concatenate(masked, axis=1))
    both, wide = jnp.concatenate([a, b], axis=0), a.shape[0]
    dims = (((1,), (1,)), ((), ()))
    for step, left in enumerate((l0, l1, l2, l3)):
        depth = left.shape[0]
        blocks = slice(2 * step, 2 * step + 2)
        large = top[blocks].reshape(depth, both.shape[1])
        small = rest[blocks].reshape(depth, both.shape[1])
        one = lax.dot_general(large, both, dims, preferred_element_type=f32)
        two = lax.dot_general(small, a, dims, preferred_element_type=f32)
        left[...] = one[:, :wide] + (one[:, wide:] + two)


def results(shapes, far):
    kinds = [pltpu.HBM(shape, f32) if i in far else jax.ShapeDtypeStruct(shape, f32) for i, shape in enumerate(shapes)]
    places = [
        pl.BlockSpec(shape, lambda i, rank=len(shape): (0,) * rank) if i in far else in_vmem
        for i, shape in enumerate(shapes)
    ]
    return {"grid": (1,), "out_shape": kinds, "out_specs": places}


def whole(kernel, core, args, shapes, far=()):
    return pl.pallas_call(
        kernel,
        **results(shapes, far),
        in_specs=[in_smem] + [in_vmem] * len(args) if core is not None else [in_vmem] * len(args),
        cost_estimate=cost(2 << 20),
        compiler_params=pltpu.CompilerParams(vmem_limit_bytes=LIMIT),
    )(*(([core] if core is not None else []) + list(args)))


def per_device(
    transmission,
    dual_focal,
    dual_curvature,
    pupil_mask,
    lyot_mask,
    dark_mask,
    focal_rows,
    focal_cols,
):
    z = lax.axis_index("z").astype(jnp.int32)
    core = lax.axis_index("core").astype(jnp.int32)
    core = where = jnp.stack([z, core])
    waves, fields, rows = focal_rows.shape
    cols = focal_cols.shape[2]
    part = fields // (ZS * CORES)
    own = dual_focal.shape[0]
    count = waves * part
    half = cols // CORES
    wide = half // CHUNKS
    tile, line = (rows, cols), [(1, cols)] * 4
    piece = (half, rows)

    dark = jnp.transpose(dark_mask.astype(f32), (1, 0, 2))
    dual_f = jnp.transpose(dual_focal, (1, 0, 2)) * dark
    spread = jnp.broadcast_to(dual_f[None], (COLS,) + dual_f.shape)

    other_rows = swap_core(focal_rows)
    started = pl.pallas_call(
        start_kernel,
        out_shape=[jax.ShapeDtypeStruct(shape, f32) for shape in line + [piece] * 4],
        in_specs=[in_smem] + [in_hbm] * 4,
        out_specs=[in_vmem] * 8,
        scratch_shapes=[pltpu.VMEM(tile, f32)] * 2 + [pltpu.VMEM(tile, jnp.int32)] * 2 + [pltpu.SemaphoreType.DMA((4,))],
        cost_estimate=cost(6 << 20),
        compiler_params=pltpu.CompilerParams(vmem_limit_bytes=LIMIT),
    )(core, *(stay(cells) for cells in (dual_curvature, transmission, pupil_mask, lyot_mask)))
    edges, x_mine, x_other, stop_mine, stop_other = started[:4], *started[4:]

    def block_of(b, where):
        return (0, (where[0] + b // CORES) % ZS * CORES + (where[1] + b) % CORES, 0, 0)

    def table_of(mine, other):
        return pl.pallas_call(
            table_kernel,
            grid_spec=pltpu.PrefetchScalarGridSpec(
                num_scalar_prefetch=1,
                grid=(ZS * CORES,),
                in_specs=[pl.BlockSpec((waves, 1, part, rows), block_of)] * 2,
                out_specs=[in_vmem] * 3,
            ),
            out_shape=[pltpu.VMEM((ZS * CORES, count, 2 * rows), bf16)] * 2 + [jax.ShapeDtypeStruct((8, 128), f32)],
            cost_estimate=cost(20 << 20),
            compiler_params=pltpu.CompilerParams(vmem_limit_bytes=LIMIT),
        )(where, *(stay(half.reshape(waves, ZS * CORES, part, rows)) for half in (mine, other)))

    *table, ready = table_of(focal_rows, other_rows)
    table = [hold(half) for half in table]
    primal_half = (x_mine, swap_core(x_other))
    stop_half = (stop_mine, swap_core(stop_other))

    def known(yc, around, held=()):
        return whole(known_kernel, core, (yc, pupil_mask, *around, *held), [piece] * 2)

    def product(kernel, args, shapes, specs, moved, scratch=(), far=()):
        return pl.pallas_call(
            kernel,
            **results(shapes, far),
            in_specs=specs,
            scratch_shapes=list(scratch),
            cost_estimate=cost(moved << 20),
            compiler_params=pltpu.CompilerParams(vmem_limit_bytes=LIMIT),
        )(*args)

    def carry(gathered):
        specs = [in_smem, in_vmem, in_hbm]
        scratch = [pltpu.VMEM((waves, fields, cols), f32), pltpu.SemaphoreType.DMA((waves,))]
        args = (core, gathered, stay(focal_cols))
        return product(carry_kernel, args, [(count, half)] * 2, specs, 6, scratch)

    def find(sums, fars):
        specs = [in_smem] + [in_vmem] * 5
        args = (core, *sums, *fars, hold(focal_cols))
        return product(found_kernel, args, [(COLS, waves, own, fields)], specs, 8, far=(0,))[0]

    def gather(block):
        return block, shift_z(block, -1), shift_z(block, -2), shift_z(block, -3)

    def backward(full):
        specs = [in_vmem] * 7
        back = product(back_kernel, (*full, *table, ready), [(wide, CORES * rows)], specs, 2)[0]
        return back, lax.ppermute(back, "wave", [(0, 1), (1, 0)])

    def update(chunk, known_half, back, far):
        cut = pl.BlockSpec((wide, rows), lambda i: (chunk, 0))
        specs = [in_vmem] * 2 + [cut] * 6 + [in_vmem] * 2
        args = (back, far, *primal_half, *stop_half, *known_half, *table)
        shapes = [(wide, rows)] * 2 + [(CORES * count, wide)] * ZS
        new0, new1, *left = product(update_kernel, args, shapes, specs, 1)
        return (new0, new1), left

    def scatter(left):
        return left[0] + shift_z(left[1], 1) + shift_z(left[2], 2) + shift_z(left[3], 3)

    primal, dual_c = transmission, dual_curvature
    gathered = lax.all_to_all(spread, COL, 0, 0, tiled=True)
    gathered, *around = tie((gathered, *exchange_rows(*edges[:2])))
    for iteration in range(ITERS):
        last = iteration == ITERS - 1
        mine, other = carry(gathered)
        received = swap_core(other)
        pair = jnp.concatenate([mine, received], axis=0)
        pair_a, pair_b = pair[:, :wide], pair[:, wide:]
        full_a = gather(pair_a)
        if iteration == 0:
            pair_b, ready = tie((pair_b, ready))
        else:
            mine, other = known(dual_c, around, table)
            last_a, mine, other = tie((full_a[3], mine, other))
            full_a = *full_a[:3], last_a
            known_half = mine, swap_core(other)
        full_b = gather(pair_b)
        back_a, far_a = backward(full_a)
        if iteration == 0:
            back_a, *ends = tie((back_a, *edges[2:]))
            mine, other = known(dual_c, (*around, *exchange_cols(*ends)))
            known_half = mine, swap_core(other)
        back_b, far_b = backward(full_b)
        far_a, back_b = tie((far_a, back_b))
        new_a, left_a = update(0, known_half, back_a, far_a)
        sum_a = scatter(left_a)
        far_b, new_a = tie((far_b, new_a))
        new_b, left_b = update(1, known_half, back_b, far_b)
        sum_b = scatter(left_b)

        moved = swap_core(new_a[1]), swap_core(new_b[1])
        sum_a, *moved = tie((sum_a, *moved))
        args = (new_a[0], new_b[0], *moved, primal)
        primal_new, *edges = whole(primal_kernel, core, args, [tile] + line)
        sum_a, sum_b, primal_new, *around = tie((sum_a, sum_b, primal_new, *exchange(edges)))

        fars = swap_core(sum_a[count:]), swap_core(sum_b[count:])
        found, *around = tie((find((sum_a[:count], sum_b[:count]), fars), *around))
        parts = lax.all_to_all(found, COL, 0, 0, tiled=True)
        args = (primal_new, primal, dual_c, *around)
        dual_c, *edges = whole(dual_kernel, core, args, [tile] + ([] if last else line), () if last else (0, 1, 2, 3, 4))
        primal = primal_new
        if last:
            parts, dual_c = tie((parts, dual_c))
            dual_f = whole(focal_kernel, None, (parts, dual_f, dark), [dual_f.shape])[0]
            break
        parts, dual_c, *around = tie((parts, dual_c, *exchange_rows(*edges[:2])))
        primal_half = tuple(jnp.concatenate(pieces, axis=0) for pieces in zip(new_a, new_b))
        dual_f, spread = whole(focal_kernel, None, (parts, dual_f, dark), [dual_f.shape, spread.shape], (1,))
        gathered = lax.all_to_all(spread, COL, 0, 0, tiled=True)
        gathered, *around = tie((gathered, *around, *exchange_cols(*edges[2:])))
    return (primal, jnp.transpose(dual_f, (1, 0, 2)), dual_c)


def solution(mesh):
    parts = Mesh(
        mesh.devices.reshape(ZS, CORES, 2, COLS // 2, WAVES),
        ("z", "core", "xl", "y", "wave"),
    )
    return jax.shard_map(
        per_device,
        mesh=parts,
        in_specs=(
            P(ROW, COL),
            P(ROW + COL, "wave", None),
            P(ROW, COL),
            P(ROW, COL),
            P(ROW, COL),
            P(ROW + COL, "wave", None),
            P("wave", None, ROW),
            P("wave", None, COL),
        ),
        out_specs=(P(ROW, COL), P(ROW + COL, "wave", None), P(ROW, COL)),
        check_vma=False,
    )
```

```python
import functools

import jax
import jax.numpy as jnp
from jax import lax
from jax.experimental import pallas as pl
from jax.experimental.pallas import tpu as pltpu
from jax.sharding import Mesh, PartitionSpec as P

ITERS = 2

step_primal = 0.12
step_dual = 0.2
contrast = 0.5
curvature_limit = 0.1

ROW = ("z", "core")
COL = ("xl", "y")
ZS, CORES, COLS, WAVES = 4, 2, 8, 2
CHUNKS = 2
LIMIT = 16 * 1024 * 1024
f32 = jnp.float32
tie = lax.optimization_barrier
in_vmem = pl.BlockSpec(memory_space=pltpu.VMEM)
in_smem = pl.BlockSpec(memory_space=pltpu.SMEM)
in_hbm = pl.BlockSpec(memory_space=pltpu.HBM)
bf16 = jnp.bfloat16


def hold(cells):
    return pltpu.with_memory_space_constraint(cells, pltpu.VMEM)


def stay(cells):
    return pltpu.with_memory_space_constraint(cells, pltpu.HBM)


def cost(moved):
    return pl.CostEstimate(flops=0, bytes_accessed=moved, transcendentals=0)


def swap_core(cells):
    return lax.ppermute(cells, "core", [(0, 1), (1, 0)])


def shift_z(cells, by):
    return lax.ppermute(cells, "z", [(i, (i + by) % ZS) for i in range(ZS)])


def split(values):
    top = values.astype(jnp.bfloat16)
    return top, (values - top.astype(f32)).astype(jnp.bfloat16)


def dot3(a, b, dims):
    (a1, a2), (b1, b2) = split(a), split(b)
    mul = functools.partial(lax.dot_general, dimension_numbers=(dims, ((), ())), preferred_element_type=f32)
    both, rows = mul(jnp.concatenate([a1, a2], axis=0), b1), a.shape[0]
    return both[:rows] + (mul(a1, b2) + both[rows:])


def exchange(edges):
    return *exchange_rows(*edges[:2]), *exchange_cols(*edges[2:])


def exchange_rows(near, far):
    pairs = [(i, i + 1) for i in range(1, ZS * CORES - 1, 2)]
    return swap_core(near), lax.ppermute(far, ROW, pairs + [(b, a) for a, b in pairs])


def exchange_cols(head, tail):
    return (
        lax.ppermute(tail, COL, [(i, i + 1) for i in range(COLS - 1)]),
        lax.ppermute(head, COL, [(i + 1, i) for i in range(COLS - 1)]),
    )


def put_edges(first, cells, near_ref, far_ref, head_ref, tail_ref):
    rows, cols = cells.shape
    top, bottom = cells[0:1, :], cells[rows - 1 : rows, :]
    near_ref[...] = jnp.where(first, bottom, top)
    far_ref[...] = jnp.where(first, top, bottom)
    head_ref[...] = jnp.transpose(cells[:, :128])[0:1, :]
    tail_ref[...] = jnp.transpose(cells[:, cols - 128 :])[127:128, :]


def stencil(first, cells, near, far, left, right):
    rows, cols = cells.shape
    above, below = jnp.where(first, far, near), jnp.where(first, near, far)
    row = lax.broadcasted_iota(jnp.int32, cells.shape, 0)
    col = lax.broadcasted_iota(jnp.int32, cells.shape, 1)
    left = jnp.transpose(jnp.broadcast_to(left, (128, rows)))[:, 0:1]
    right = jnp.transpose(jnp.broadcast_to(right, (128, rows)))[:, 0:1]
    down = jnp.where(row == 0, above, pltpu.roll(cells, 1, 0))
    up = jnp.where(row == rows - 1, below, pltpu.roll(cells, rows - 1, 0))
    after = jnp.where(col == 0, left, pltpu.roll(cells, 1, 1))
    before = jnp.where(col == cols - 1, right, pltpu.roll(cells, cols - 1, 1))
    return 0.25 * (down + up + after + before) - cells


def halves(first, cells, mine_ref, other_ref, turn=True):
    half = cells.shape[1] // 2
    a, b = cells[:, :half], cells[:, half:]
    mine, other = jnp.where(first, a, b), jnp.where(first, b, a)
    mine_ref[...] = jnp.transpose(mine) if turn else mine
    other_ref[...] = jnp.transpose(other) if turn else other


def start_kernel(core, yc, x, pupil_mask, lyot_mask, *refs):
    near, far, head, tail, x_mine, x_other, stop_mine, stop_other, *held, sems = refs
    first = core[1] == 0
    copies = fetch(list(zip((yc, x, pupil_mask, lyot_mask), held)), sems)
    copies[0].wait()
    put_edges(first, held[0][...], near, far, head, tail)
    copies[1].wait()
    halves(first, held[1][...], x_mine, x_other)
    copies[2].wait()
    copies[3].wait()
    halves(first, (held[2][...] * held[3][...]).astype(f32), stop_mine, stop_other)


def known_kernel(core, yc, pupil_mask, near, far, left, right, *refs):
    mine, other = refs[-2:]
    first = core[1] == 0
    curved = stencil(first, yc[...], near[...], far[...], left[...], right[...])
    halves(first, curved - pupil_mask[...].astype(f32), mine, other)


def primal_kernel(core, new_a, new_b, far_a, far_b, x, out, near, far, head, tail):
    first = core[1] == 0
    mine = jnp.transpose(jnp.concatenate([new_a[...], new_b[...]], axis=0))
    other = jnp.transpose(jnp.concatenate([far_a[...], far_b[...]], axis=0))
    new = jnp.concatenate([jnp.where(first, mine, other), jnp.where(first, other, mine)], axis=1)
    out[...] = new
    put_edges(first, 2.0 * new - x[...], near, far, head, tail)


def dual_kernel(core, new, x, yc, near, far, left, right, out, *edges):
    first = core[1] == 0
    extended = 2.0 * new[...] - x[...]
    curved = stencil(first, extended, near[...], far[...], left[...], right[...])
    moved = yc[...] + step_dual * curved
    result = moved - step_dual * jnp.clip(moved / step_dual, -curvature_limit, curvature_limit)
    out[...] = result
    if edges:
        put_edges(first, result, *edges)


def focal_kernel(parts, yf, dark, out, *spread):
    fields = parts[0]
    for other in range(1, COLS):
        fields = fields + parts[other]
    shifted = yf[...] + step_dual * fields
    result = dark[...] * (shifted - step_dual * jnp.clip(shifted / step_dual, -contrast, contrast))
    out[...] = result
    if spread:
        for other in range(COLS):
            spread[0][other] = result


def fetch(pairs, sems):
    copies = [pltpu.make_async_copy(src, dst, sems.at[i]) for i, (src, dst) in enumerate(pairs)]
    for copy in copies:
        copy.start()
    return copies


def carry_kernel(core, y, table, mine, other, held, sems):
    waves, rows = table.shape[0], y.shape[0] * y.shape[2]
    copies = fetch([(table.at[w], held.at[w]) for w in range(waves)], sems)
    for w in range(waves):
        copies[w].wait()
        carried = dot3(y[:, w].reshape(rows, y.shape[3]), held[w], ((1,), (0,)))
        at = pl.ds(w * rows, rows)
        halves(core[1] == 0, carried, mine.at[at], other.at[at], turn=False)


def found_kernel(core, own_a, own_b, far_a, far_b, table, out):
    first = core[1] == 0
    waves, rows = out.shape[1], out.shape[0] * out.shape[2]
    for w in range(waves):
        at = pl.ds(w * rows, rows)
        own = jnp.concatenate([own_a[at, :], own_b[at, :]], axis=1)
        far = jnp.concatenate([far_a[at, :], far_b[at, :]], axis=1)
        left = jnp.concatenate([jnp.where(first, own, far), jnp.where(first, far, own)], axis=1)
        found = dot3(left, table[w], ((1,), (1,)))
        out[:, w] = found.reshape(out.shape[0], out.shape[2], out.shape[3])


def table_kernel(where, mine, other, top, rest, ready):
    ready[...] = jnp.zeros_like(ready)
    rows, b = mine.shape[3], pl.program_id(0)
    for at, block in ((0, mine), (rows, other)):
        large, small = split(block[:, 0].reshape(top.shape[1], rows))
        top[b, :, at : at + rows] = large
        rest[b, :, at : at + rows] = small


def back_kernel(t0, t1, t2, t3, top, rest, ready, out):
    for step, t in enumerate((t0, t1, t2, t3)):
        depth, wide = t.shape
        a, b = split(jnp.transpose(t[...]))
        blocks = slice(2 * step, 2 * step + 2)
        both = jnp.dot(
            jnp.concatenate([a, b], axis=0),
            top[blocks].reshape(depth, out.shape[1]),
            preferred_element_type=f32,
        )
        more = jnp.dot(a, rest[blocks].reshape(depth, out.shape[1]), preferred_element_type=f32)
        part = both[:wide] + (both[wide:] + more)
        out[...] = part if step == 0 else out[...] + part


def update_kernel(back, far, x0, x1, s0, s1, k0, k1, top, rest, new0, new1, l0, l1, l2, l3):
    rows = x0.shape[1]
    masked = []
    for i, (x, stop, known, new) in enumerate(((x0, s0, k0, new0), (x1, s1, k1, new1))):
        at = slice(i * rows, (i + 1) * rows)
        before = x[...]
        gradient = known[...] + stop[...] * (back[:, at] + far[:, at])
        after = jnp.clip(before - step_primal * gradient, 0.0, 1.0)
        new[...] = after
        masked.append(stop[...] * (2.0 * after - before))
    a, b = split(jnp.concatenate(masked, axis=1))
    both, wide = jnp.concatenate([a, b], axis=0), a.shape[0]
    dims = (((1,), (1,)), ((), ()))
    for step, left in enumerate((l0, l1, l2, l3)):
        depth = left.shape[0]
        blocks = slice(2 * step, 2 * step + 2)
        large = top[blocks].reshape(depth, both.shape[1])
        small = rest[blocks].reshape(depth, both.shape[1])
        one = lax.dot_general(large, both, dims, preferred_element_type=f32)
        two = lax.dot_general(small, a, dims, preferred_element_type=f32)
        left[...] = one[:, :wide] + (one[:, wide:] + two)


def results(shapes, far):
    kinds = [pltpu.HBM(shape, f32) if i in far else jax.ShapeDtypeStruct(shape, f32) for i, shape in enumerate(shapes)]
    places = [
        pl.BlockSpec(shape, lambda i, rank=len(shape): (0,) * rank) if i in far else in_vmem
        for i, shape in enumerate(shapes)
    ]
    return {"grid": (1,), "out_shape": kinds, "out_specs": places}


def whole(kernel, core, args, shapes, far=()):
    return pl.pallas_call(
        kernel,
        **results(shapes, far),
        in_specs=[in_smem] + [in_vmem] * len(args) if core is not None else [in_vmem] * len(args),
        cost_estimate=cost(2 << 20),
        compiler_params=pltpu.CompilerParams(vmem_limit_bytes=LIMIT),
    )(*(([core] if core is not None else []) + list(args)))


def per_device(
    transmission,
    dual_focal,
    dual_curvature,
    pupil_mask,
    lyot_mask,
    dark_mask,
    focal_rows,
    focal_cols,
):
    z = lax.axis_index("z").astype(jnp.int32)
    core = lax.axis_index("core").astype(jnp.int32)
    core = where = jnp.stack([z, core])
    waves, fields, rows = focal_rows.shape
    cols = focal_cols.shape[2]
    part = fields // (ZS * CORES)
    own = dual_focal.shape[0]
    count = waves * part
    half = cols // CORES
    wide = half // CHUNKS
    tile, line = (rows, cols), [(1, cols)] * 4
    piece = (half, rows)

    dark = jnp.transpose(dark_mask.astype(f32), (1, 0, 2))
    dual_f = jnp.transpose(dual_focal, (1, 0, 2)) * dark

    other_rows = swap_core(focal_rows)
    started = pl.pallas_call(
        start_kernel,
        out_shape=[jax.ShapeDtypeStruct(shape, f32) for shape in line + [piece] * 4],
        in_specs=[in_smem] + [in_hbm] * 4,
        out_specs=[in_vmem] * 8,
        scratch_shapes=[pltpu.VMEM(tile, f32)] * 2 + [pltpu.VMEM(tile, jnp.int32)] * 2 + [pltpu.SemaphoreType.DMA((4,))],
        cost_estimate=cost(6 << 20),
        compiler_params=pltpu.CompilerParams(vmem_limit_bytes=LIMIT),
    )(core, *(stay(cells) for cells in (dual_curvature, transmission, pupil_mask, lyot_mask)))
    edges, x_mine, x_other, stop_mine, stop_other = started[:4], *started[4:]

    def block_of(b, where):
        return (0, (where[0] + b // CORES) % ZS * CORES + (where[1] + b) % CORES, 0, 0)

    def table_of(mine, other):
        return pl.pallas_call(
            table_kernel,
            grid_spec=pltpu.PrefetchScalarGridSpec(
                num_scalar_prefetch=1,
                grid=(ZS * CORES,),
                in_specs=[pl.BlockSpec((waves, 1, part, rows), block_of)] * 2,
                out_specs=[in_vmem] * 3,
            ),
            out_shape=[pltpu.VMEM((ZS * CORES, count, 2 * rows), bf16)] * 2 + [jax.ShapeDtypeStruct((8, 128), f32)],
            cost_estimate=cost(20 << 20),
            compiler_params=pltpu.CompilerParams(vmem_limit_bytes=LIMIT),
        )(where, *(stay(half.reshape(waves, ZS * CORES, part, rows)) for half in (mine, other)))

    *table, ready = table_of(focal_rows, other_rows)
    table = [hold(half) for half in table]
    primal_half = (x_mine, swap_core(x_other))
    stop_half = (stop_mine, swap_core(stop_other))

    def known(yc, around, held=()):
        return whole(known_kernel, core, (yc, pupil_mask, *around, *held), [piece] * 2)

    def product(kernel, args, shapes, specs, moved, scratch=(), far=()):
        return pl.pallas_call(
            kernel,
            **results(shapes, far),
            in_specs=specs,
            scratch_shapes=list(scratch),
            cost_estimate=cost(moved << 20),
            compiler_params=pltpu.CompilerParams(vmem_limit_bytes=LIMIT),
        )(*args)

    def carry(gathered):
        specs = [in_smem, in_vmem, in_hbm]
        scratch = [pltpu.VMEM((waves, fields, cols), f32), pltpu.SemaphoreType.DMA((waves,))]
        args = (core, gathered, stay(focal_cols))
        return product(carry_kernel, args, [(count, half)] * 2, specs, 6, scratch)

    def find(sums, fars):
        specs = [in_smem] + [in_vmem] * 5
        args = (core, *sums, *fars, hold(focal_cols))
        return product(found_kernel, args, [(COLS, waves, own, fields)], specs, 8, far=(0,))[0]

    def gather(block):
        return block, shift_z(block, -1), shift_z(block, -2), shift_z(block, -3)

    def backward(full):
        specs = [in_vmem] * 7
        back = product(back_kernel, (*full, *table, ready), [(wide, CORES * rows)], specs, 2)[0]
        return back, lax.ppermute(back, "wave", [(0, 1), (1, 0)])

    def update(chunk, known_half, back, far):
        cut = pl.BlockSpec((wide, rows), lambda i: (chunk, 0))
        specs = [in_vmem] * 2 + [cut] * 6 + [in_vmem] * 2
        args = (back, far, *primal_half, *stop_half, *known_half, *table)
        shapes = [(wide, rows)] * 2 + [(CORES * count, wide)] * ZS
        new0, new1, *left = product(update_kernel, args, shapes, specs, 1)
        return (new0, new1), left

    def scatter(left):
        return left[0] + shift_z(left[1], 1) + shift_z(left[2], 2) + shift_z(left[3], 3)

    primal, dual_c = transmission, dual_curvature
    lines = jnp.concatenate([edges[3], edges[2], jnp.zeros((own - 2, fields), f32)], axis=0)
    spread = jnp.concatenate([dual_f, lines[None]], axis=0)
    spread = jnp.broadcast_to(spread[None], (COLS,) + spread.shape)
    gathered = lax.all_to_all(spread, COL, 0, 0, tiled=True)
    gathered, *around = tie((gathered, *exchange_rows(*edges[:2])))
    place = lax.axis_index(COL)
    lines = gathered[:, waves]
    left = lax.dynamic_index_in_dim(lines, jnp.maximum(place - 1, 0), 0, keepdims=False)[0:1]
    right = lax.dynamic_index_in_dim(lines, jnp.minimum(place + 1, COLS - 1), 0, keepdims=False)[1:2]
    around += [jnp.where(place > 0, left, 0.0), jnp.where(place < COLS - 1, right, 0.0)]
    for iteration in range(ITERS):
        last = iteration == ITERS - 1
        mine, other = carry(gathered)
        received = swap_core(other)
        pair = jnp.concatenate([mine, received], axis=0)
        pair_a, pair_b = pair[:, :wide], pair[:, wide:]
        full_a = gather(pair_a)
        if iteration == 0:
            pair_b, ready = tie((pair_b, ready))
        else:
            mine, other = known(dual_c, around, table)
            last_a, mine, other = tie((full_a[3], mine, other))
            full_a = *full_a[:3], last_a
            known_half = mine, swap_core(other)
        full_b = gather(pair_b)
        back_a, far_a = backward(full_a)
        if iteration == 0:
            mine, other = known(dual_c, around)
            known_half = mine, swap_core(other)
        back_b, far_b = backward(full_b)
        far_a, back_b = tie((far_a, back_b))
        new_a, left_a = update(0, known_half, back_a, far_a)
        sum_a = scatter(left_a)
        far_b, new_a = tie((far_b, new_a))
        new_b, left_b = update(1, known_half, back_b, far_b)
        sum_b = scatter(left_b)

        moved = swap_core(new_a[1]), swap_core(new_b[1])
        sum_a, *moved = tie((sum_a, *moved))
        args = (new_a[0], new_b[0], *moved, primal)
        primal_new, *edges = whole(primal_kernel, core, args, [tile] + line)
        sum_a, sum_b, primal_new, *around = tie((sum_a, sum_b, primal_new, *exchange(edges)))

        fars = swap_core(sum_a[count:]), swap_core(sum_b[count:])
        found, *around = tie((find((sum_a[:count], sum_b[:count]), fars), *around))
        parts = lax.all_to_all(found, COL, 0, 0, tiled=True)
        args = (primal_new, primal, dual_c, *around)
        dual_c, *edges = whole(dual_kernel, core, args, [tile] + ([] if last else line), () if last else (0, 1, 2, 3, 4))
        primal = primal_new
        if last:
            parts, dual_c = tie((parts, dual_c))
            dual_f = whole(focal_kernel, None, (parts, dual_f, dark), [dual_f.shape])[0]
            break
        parts, dual_c, *around = tie((parts, dual_c, *exchange_rows(*edges[:2])))
        primal_half = tuple(jnp.concatenate(pieces, axis=0) for pieces in zip(new_a, new_b))
        dual_f, spread = whole(focal_kernel, None, (parts, dual_f, dark), [dual_f.shape, (COLS,) + dual_f.shape], (1,))
        gathered = lax.all_to_all(spread, COL, 0, 0, tiled=True)
        gathered, *around = tie((gathered, *around, *exchange_cols(*edges[2:])))
    return (primal, jnp.transpose(dual_f, (1, 0, 2)), dual_c)


def solution(mesh):
    parts = Mesh(
        mesh.devices.reshape(ZS, CORES, 2, COLS // 2, WAVES),
        ("z", "core", "xl", "y", "wave"),
    )
    return jax.shard_map(
        per_device,
        mesh=parts,
        in_specs=(
            P(ROW, COL),
            P(ROW + COL, "wave", None),
            P(ROW, COL),
            P(ROW, COL),
            P(ROW, COL),
            P(ROW + COL, "wave", None),
            P("wave", None, ROW),
            P("wave", None, COL),
        ),
        out_specs=(P(ROW, COL), P(ROW + COL, "wave", None), P(ROW, COL)),
        check_vma=False,
    )
```

```python
import functools

import jax
import jax.numpy as jnp
from jax import lax
from jax.experimental import pallas as pl
from jax.experimental.pallas import tpu as pltpu
from jax.sharding import Mesh, PartitionSpec as P

ITERS = 2

step_primal = 0.12
step_dual = 0.2
contrast = 0.5
curvature_limit = 0.1

ROW = ("z", "core")
COL = ("xl", "y")
ZS, CORES, COLS, WAVES = 4, 2, 8, 2
CHUNKS = 2
LIMIT = 16 * 1024 * 1024
f32 = jnp.float32
tie = lax.optimization_barrier
in_vmem = pl.BlockSpec(memory_space=pltpu.VMEM)
in_smem = pl.BlockSpec(memory_space=pltpu.SMEM)
in_hbm = pl.BlockSpec(memory_space=pltpu.HBM)
bf16 = jnp.bfloat16


def hold(cells):
    return pltpu.with_memory_space_constraint(cells, pltpu.VMEM)


def stay(cells):
    return pltpu.with_memory_space_constraint(cells, pltpu.HBM)


def cost(moved):
    return pl.CostEstimate(flops=0, bytes_accessed=moved, transcendentals=0)


def swap_core(cells):
    return lax.ppermute(cells, "core", [(0, 1), (1, 0)])


def shift_z(cells, by):
    return lax.ppermute(cells, "z", [(i, (i + by) % ZS) for i in range(ZS)])


def split(values):
    top = values.astype(jnp.bfloat16)
    return top, (values - top.astype(f32)).astype(jnp.bfloat16)


def dot3(a, b, dims):
    (a1, a2), (b1, b2) = split(a), split(b)
    mul = functools.partial(lax.dot_general, dimension_numbers=(dims, ((), ())), preferred_element_type=f32)
    both, rows = mul(jnp.concatenate([a1, a2], axis=0), b1), a.shape[0]
    return both[:rows] + (mul(a1, b2) + both[rows:])


def exchange(edges):
    return *exchange_rows(*edges[:2]), *exchange_cols(*edges[2:])


def exchange_rows(near, far):
    pairs = [(i, i + 1) for i in range(1, ZS * CORES - 1, 2)]
    return swap_core(near), lax.ppermute(far, ROW, pairs + [(b, a) for a, b in pairs])


def exchange_cols(head, tail):
    return (
        lax.ppermute(tail, COL, [(i, i + 1) for i in range(COLS - 1)]),
        lax.ppermute(head, COL, [(i + 1, i) for i in range(COLS - 1)]),
    )


def put_edges(first, cells, near_ref, far_ref, head_ref, tail_ref):
    rows, cols = cells.shape
    top, bottom = cells[0:1, :], cells[rows - 1 : rows, :]
    near_ref[...] = jnp.where(first, bottom, top)
    far_ref[...] = jnp.where(first, top, bottom)
    head_ref[...] = jnp.transpose(cells[:, :128])[0:1, :]
    tail_ref[...] = jnp.transpose(cells[:, cols - 128 :])[127:128, :]


def stencil(first, cells, near, far, left, right):
    rows, cols = cells.shape
    above, below = jnp.where(first, far, near), jnp.where(first, near, far)
    row = lax.broadcasted_iota(jnp.int32, cells.shape, 0)
    col = lax.broadcasted_iota(jnp.int32, cells.shape, 1)
    left = jnp.transpose(jnp.broadcast_to(left, (128, rows)))[:, 0:1]
    right = jnp.transpose(jnp.broadcast_to(right, (128, rows)))[:, 0:1]
    down = jnp.where(row == 0, above, pltpu.roll(cells, 1, 0))
    up = jnp.where(row == rows - 1, below, pltpu.roll(cells, rows - 1, 0))
    after = jnp.where(col == 0, left, pltpu.roll(cells, 1, 1))
    before = jnp.where(col == cols - 1, right, pltpu.roll(cells, cols - 1, 1))
    return 0.25 * (down + up + after + before) - cells


def halves(first, cells, mine_ref, other_ref, turn=True):
    half = cells.shape[1] // 2
    a, b = cells[:, :half], cells[:, half:]
    mine, other = jnp.where(first, a, b), jnp.where(first, b, a)
    mine_ref[...] = jnp.transpose(mine) if turn else mine
    other_ref[...] = jnp.transpose(other) if turn else other


def edge_kernel(core, yc, near, far, head, tail, held, sems):
    fetch([(yc, held)], sems)[0].wait()
    put_edges(core[1] == 0, held[...], near, far, head, tail)


def start_kernel(core, x, pupil_mask, lyot_mask, *refs):
    x_mine, x_other, stop_mine, stop_other, *held, sems = refs
    first = core[1] == 0
    copies = fetch(list(zip((x, pupil_mask, lyot_mask), held)), sems)
    copies[0].wait()
    halves(first, held[0][...], x_mine, x_other)
    copies[1].wait()
    copies[2].wait()
    halves(first, (held[1][...] * held[2][...]).astype(f32), stop_mine, stop_other)


def first_known_kernel(core, yc, pupil_mask, near, far, gathered, mine, other):
    place, slab = core[2], gathered.shape[1] - 1
    left = gathered[jnp.maximum(place - 1, 0), slab, 0:1]
    right = gathered[jnp.minimum(place + 1, COLS - 1), slab, 1:2]
    left = jnp.where(place > 0, left, 0.0)
    right = jnp.where(place < COLS - 1, right, 0.0)
    known_kernel(core, yc, pupil_mask, near, far, left, right, mine, other)


def known_kernel(core, yc, pupil_mask, near, far, left, right, *refs):
    mine, other = refs[-2:]
    first = core[1] == 0
    curved = stencil(first, yc[...], near[...], far[...], left[...], right[...])
    halves(first, curved - pupil_mask[...].astype(f32), mine, other)


def primal_kernel(core, new_a, new_b, far_a, far_b, x, out, near, far, head, tail):
    first = core[1] == 0
    mine = jnp.transpose(jnp.concatenate([new_a[...], new_b[...]], axis=0))
    other = jnp.transpose(jnp.concatenate([far_a[...], far_b[...]], axis=0))
    new = jnp.concatenate([jnp.where(first, mine, other), jnp.where(first, other, mine)], axis=1)
    out[...] = new
    put_edges(first, 2.0 * new - x[...], near, far, head, tail)


def dual_kernel(core, new, x, yc, near, far, left, right, out, *edges):
    first = core[1] == 0
    extended = 2.0 * new[...] - x[...]
    curved = stencil(first, extended, near[...], far[...], left[...], right[...])
    moved = yc[...] + step_dual * curved
    result = moved - step_dual * jnp.clip(moved / step_dual, -curvature_limit, curvature_limit)
    out[...] = result
    if edges:
        put_edges(first, result, *edges)


def focal_kernel(parts, yf, dark, out, *spread):
    fields = parts[0]
    for other in range(1, COLS):
        fields = fields + parts[other]
    shifted = yf[...] + step_dual * fields
    result = dark[...] * (shifted - step_dual * jnp.clip(shifted / step_dual, -contrast, contrast))
    out[...] = result
    if spread:
        for other in range(COLS):
            spread[0][other] = result


def fetch(pairs, sems):
    copies = [pltpu.make_async_copy(src, dst, sems.at[i]) for i, (src, dst) in enumerate(pairs)]
    for copy in copies:
        copy.start()
    return copies


def carry_kernel(core, y, table, mine, other, held, sems):
    waves, rows = table.shape[0], y.shape[0] * y.shape[2]
    copies = fetch([(table.at[w], held.at[w]) for w in range(waves)], sems)
    for w in range(waves):
        copies[w].wait()
        carried = dot3(y[:, w].reshape(rows, y.shape[3]), held[w], ((1,), (0,)))
        at = pl.ds(w * rows, rows)
        halves(core[1] == 0, carried, mine.at[at], other.at[at], turn=False)


def found_kernel(core, own_a, own_b, far_a, far_b, table, out):
    first = core[1] == 0
    waves, rows = out.shape[1], out.shape[0] * out.shape[2]
    for w in range(waves):
        at = pl.ds(w * rows, rows)
        own = jnp.concatenate([own_a[at, :], own_b[at, :]], axis=1)
        far = jnp.concatenate([far_a[at, :], far_b[at, :]], axis=1)
        left = jnp.concatenate([jnp.where(first, own, far), jnp.where(first, far, own)], axis=1)
        found = dot3(left, table[w], ((1,), (1,)))
        out[:, w] = found.reshape(out.shape[0], out.shape[2], out.shape[3])


def table_kernel(where, mine, other, top, rest, ready):
    ready[...] = jnp.zeros_like(ready)
    rows, b = mine.shape[3], pl.program_id(0)
    for at, block in ((0, mine), (rows, other)):
        large, small = split(block[:, 0].reshape(top.shape[1], rows))
        top[b, :, at : at + rows] = large
        rest[b, :, at : at + rows] = small


def back_kernel(t0, t1, t2, t3, top, rest, ready, out):
    for step, t in enumerate((t0, t1, t2, t3)):
        depth, wide = t.shape
        a, b = split(jnp.transpose(t[...]))
        blocks = slice(2 * step, 2 * step + 2)
        both = jnp.dot(
            jnp.concatenate([a, b], axis=0),
            top[blocks].reshape(depth, out.shape[1]),
            preferred_element_type=f32,
        )
        more = jnp.dot(a, rest[blocks].reshape(depth, out.shape[1]), preferred_element_type=f32)
        part = both[:wide] + (both[wide:] + more)
        out[...] = part if step == 0 else out[...] + part


def update_kernel(back, far, x0, x1, s0, s1, k0, k1, top, rest, new0, new1, l0, l1, l2, l3):
    rows = x0.shape[1]
    masked = []
    for i, (x, stop, known, new) in enumerate(((x0, s0, k0, new0), (x1, s1, k1, new1))):
        at = slice(i * rows, (i + 1) * rows)
        before = x[...]
        gradient = known[...] + stop[...] * (back[:, at] + far[:, at])
        after = jnp.clip(before - step_primal * gradient, 0.0, 1.0)
        new[...] = after
        masked.append(stop[...] * (2.0 * after - before))
    a, b = split(jnp.concatenate(masked, axis=1))
    both, wide = jnp.concatenate([a, b], axis=0), a.shape[0]
    dims = (((1,), (1,)), ((), ()))
    for step, left in enumerate((l0, l1, l2, l3)):
        depth = left.shape[0]
        blocks = slice(2 * step, 2 * step + 2)
        large = top[blocks].reshape(depth, both.shape[1])
        small = rest[blocks].reshape(depth, both.shape[1])
        one = lax.dot_general(large, both, dims, preferred_element_type=f32)
        two = lax.dot_general(small, a, dims, preferred_element_type=f32)
        left[...] = one[:, :wide] + (one[:, wide:] + two)


def results(shapes, far):
    kinds = [pltpu.HBM(shape, f32) if i in far else jax.ShapeDtypeStruct(shape, f32) for i, shape in enumerate(shapes)]
    places = [
        pl.BlockSpec(shape, lambda i, rank=len(shape): (0,) * rank) if i in far else in_vmem
        for i, shape in enumerate(shapes)
    ]
    return {"grid": (1,), "out_shape": kinds, "out_specs": places}


def whole(kernel, core, args, shapes, far=()):
    return pl.pallas_call(
        kernel,
        **results(shapes, far),
        in_specs=[in_smem] + [in_vmem] * len(args) if core is not None else [in_vmem] * len(args),
        cost_estimate=cost(2 << 20),
        compiler_params=pltpu.CompilerParams(vmem_limit_bytes=LIMIT),
    )(*(([core] if core is not None else []) + list(args)))


def per_device(
    transmission,
    dual_focal,
    dual_curvature,
    pupil_mask,
    lyot_mask,
    dark_mask,
    focal_rows,
    focal_cols,
):
    z = lax.axis_index("z").astype(jnp.int32)
    core = lax.axis_index("core").astype(jnp.int32)
    core = where = jnp.stack([z, core, lax.axis_index(COL).astype(jnp.int32)])
    waves, fields, rows = focal_rows.shape
    cols = focal_cols.shape[2]
    part = fields // (ZS * CORES)
    own = dual_focal.shape[0]
    count = waves * part
    half = cols // CORES
    wide = half // CHUNKS
    tile, line = (rows, cols), [(1, cols)] * 4
    piece = (half, rows)

    dark = jnp.transpose(dark_mask.astype(f32), (1, 0, 2))
    dual_f = jnp.transpose(dual_focal, (1, 0, 2)) * dark

    other_rows = swap_core(focal_rows)
    def started(kernel, inputs, shapes):
        return pl.pallas_call(
            kernel,
            out_shape=[jax.ShapeDtypeStruct(shape, f32) for shape in shapes],
            in_specs=[in_smem] + [in_hbm] * len(inputs),
            out_specs=[in_vmem] * len(shapes),
            scratch_shapes=[pltpu.VMEM(tile, cells.dtype) for cells in inputs]
            + [pltpu.SemaphoreType.DMA((len(inputs),))],
            cost_estimate=cost(2 << 20),
            compiler_params=pltpu.CompilerParams(vmem_limit_bytes=LIMIT),
        )(core, *(stay(cells) for cells in inputs))

    edges = started(edge_kernel, (dual_curvature,), line)
    inputs = (transmission, pupil_mask, lyot_mask)
    x_mine, x_other, stop_mine, stop_other = started(start_kernel, inputs, [piece] * 4)

    def block_of(b, where):
        return (0, (where[0] + b // CORES) % ZS * CORES + (where[1] + b) % CORES, 0, 0)

    def table_of(mine, other):
        return pl.pallas_call(
            table_kernel,
            grid_spec=pltpu.PrefetchScalarGridSpec(
                num_scalar_prefetch=1,
                grid=(ZS * CORES,),
                in_specs=[pl.BlockSpec((waves, 1, part, rows), block_of)] * 2,
                out_specs=[in_vmem] * 3,
            ),
            out_shape=[pltpu.VMEM((ZS * CORES, count, 2 * rows), bf16)] * 2 + [jax.ShapeDtypeStruct((8, 128), f32)],
            cost_estimate=cost(20 << 20),
            compiler_params=pltpu.CompilerParams(vmem_limit_bytes=LIMIT),
        )(where, *(stay(half.reshape(waves, ZS * CORES, part, rows)) for half in (mine, other)))

    *table, ready = table_of(focal_rows, other_rows)
    table = [hold(half) for half in table]
    primal_half = (x_mine, swap_core(x_other))
    stop_half = (stop_mine, swap_core(stop_other))

    def known(yc, around, held=()):
        return whole(known_kernel, core, (yc, pupil_mask, *around, *held), [piece] * 2)

    def product(kernel, args, shapes, specs, moved, scratch=(), far=()):
        return pl.pallas_call(
            kernel,
            **results(shapes, far),
            in_specs=specs,
            scratch_shapes=list(scratch),
            cost_estimate=cost(moved << 20),
            compiler_params=pltpu.CompilerParams(vmem_limit_bytes=LIMIT),
        )(*args)

    def carry(gathered):
        specs = [in_smem, in_vmem, in_hbm]
        scratch = [pltpu.VMEM((waves, fields, cols), f32), pltpu.SemaphoreType.DMA((waves,))]
        args = (core, gathered, stay(focal_cols))
        return product(carry_kernel, args, [(count, half)] * 2, specs, 6, scratch)

    def find(sums, fars):
        specs = [in_smem] + [in_vmem] * 5
        args = (core, *sums, *fars, hold(focal_cols))
        return product(found_kernel, args, [(COLS, waves, own, fields)], specs, 8, far=(0,))[0]

    def gather(block):
        return block, shift_z(block, -1), shift_z(block, -2), shift_z(block, -3)

    def backward(full):
        specs = [in_vmem] * 7
        back = product(back_kernel, (*full, *table, ready), [(wide, CORES * rows)], specs, 2)[0]
        return back, lax.ppermute(back, "wave", [(0, 1), (1, 0)])

    def update(chunk, known_half, back, far):
        cut = pl.BlockSpec((wide, rows), lambda i: (chunk, 0))
        specs = [in_vmem] * 2 + [cut] * 6 + [in_vmem] * 2
        args = (back, far, *primal_half, *stop_half, *known_half, *table)
        shapes = [(wide, rows)] * 2 + [(CORES * count, wide)] * ZS
        new0, new1, *left = product(update_kernel, args, shapes, specs, 1)
        return (new0, new1), left

    def scatter(left):
        return left[0] + shift_z(left[1], 1) + shift_z(left[2], 2) + shift_z(left[3], 3)

    primal, dual_c = transmission, dual_curvature
    lines = jnp.concatenate([edges[3], edges[2], jnp.zeros((own - 2, fields), f32)], axis=0)
    spread = jnp.concatenate([dual_f, lines[None]], axis=0)
    spread = jnp.broadcast_to(spread[None], (COLS,) + spread.shape)
    gathered = lax.all_to_all(spread, COL, 0, 0, tiled=True)
    gathered, *around = tie((gathered, *exchange_rows(*edges[:2])))
    for iteration in range(ITERS):
        last = iteration == ITERS - 1
        mine, other = carry(gathered)
        received = swap_core(other)
        pair = jnp.concatenate([mine, received], axis=0)
        pair_a, pair_b = pair[:, :wide], pair[:, wide:]
        full_a = gather(pair_a)
        if iteration == 0:
            pair_b, ready = tie((pair_b, ready))
        else:
            mine, other = known(dual_c, around, table)
            last_a, mine, other = tie((full_a[3], mine, other))
            full_a = *full_a[:3], last_a
            known_half = mine, swap_core(other)
        full_b = gather(pair_b)
        back_a, far_a = backward(full_a)
        if iteration == 0:
            mine, other = whole(first_known_kernel, core, (dual_c, pupil_mask, *around, gathered), [piece] * 2)
            known_half = mine, swap_core(other)
        back_b, far_b = backward(full_b)
        far_a, back_b = tie((far_a, back_b))
        new_a, left_a = update(0, known_half, back_a, far_a)
        sum_a = scatter(left_a)
        far_b, new_a = tie((far_b, new_a))
        new_b, left_b = update(1, known_half, back_b, far_b)
        sum_b = scatter(left_b)

        moved = swap_core(new_a[1]), swap_core(new_b[1])
        sum_a, *moved = tie((sum_a, *moved))
        args = (new_a[0], new_b[0], *moved, primal)
        primal_new, *edges = whole(primal_kernel, core, args, [tile] + line)
        sum_a, sum_b, primal_new, *around = tie((sum_a, sum_b, primal_new, *exchange(edges)))

        fars = swap_core(sum_a[count:]), swap_core(sum_b[count:])
        found, *around = tie((find((sum_a[:count], sum_b[:count]), fars), *around))
        parts = lax.all_to_all(found, COL, 0, 0, tiled=True)
        args = (primal_new, primal, dual_c, *around)
        dual_c, *edges = whole(dual_kernel, core, args, [tile] + ([] if last else line), () if last else (0, 1, 2, 3, 4))
        primal = primal_new
        if last:
            parts, dual_c = tie((parts, dual_c))
            dual_f = whole(focal_kernel, None, (parts, dual_f, dark), [dual_f.shape])[0]
            break
        parts, dual_c, *around = tie((parts, dual_c, *exchange_rows(*edges[:2])))
        primal_half = tuple(jnp.concatenate(pieces, axis=0) for pieces in zip(new_a, new_b))
        dual_f, spread = whole(focal_kernel, None, (parts, dual_f, dark), [dual_f.shape, (COLS,) + dual_f.shape], (1,))
        gathered = lax.all_to_all(spread, COL, 0, 0, tiled=True)
        gathered, *around = tie((gathered, *around, *exchange_cols(*edges[2:])))
    return (primal, jnp.transpose(dual_f, (1, 0, 2)), dual_c)


def solution(mesh):
    parts = Mesh(
        mesh.devices.reshape(ZS, CORES, 2, COLS // 2, WAVES),
        ("z", "core", "xl", "y", "wave"),
    )
    return jax.shard_map(
        per_device,
        mesh=parts,
        in_specs=(
            P(ROW, COL),
            P(ROW + COL, "wave", None),
            P(ROW, COL),
            P(ROW, COL),
            P(ROW, COL),
            P(ROW + COL, "wave", None),
            P("wave", None, ROW),
            P("wave", None, COL),
        ),
        out_specs=(P(ROW, COL), P(ROW + COL, "wave", None), P(ROW, COL)),
        check_vma=False,
    )
```

```python
import functools

import jax
import jax.numpy as jnp
from jax import lax
from jax.experimental import pallas as pl
from jax.experimental.pallas import tpu as pltpu
from jax.sharding import Mesh, PartitionSpec as P

ITERS = 2

step_primal = 0.12
step_dual = 0.2
contrast = 0.5
curvature_limit = 0.1

ROW = ("z", "core")
COL = ("xl", "y")
ZS, CORES, COLS, WAVES = 4, 2, 8, 2
CHUNKS = 2
LIMIT = 16 * 1024 * 1024
f32 = jnp.float32
tie = lax.optimization_barrier
in_vmem = pl.BlockSpec(memory_space=pltpu.VMEM)
in_smem = pl.BlockSpec(memory_space=pltpu.SMEM)
in_hbm = pl.BlockSpec(memory_space=pltpu.HBM)
bf16 = jnp.bfloat16


def hold(cells):
    return pltpu.with_memory_space_constraint(cells, pltpu.VMEM)


def stay(cells):
    return pltpu.with_memory_space_constraint(cells, pltpu.HBM)


def cost(moved):
    return pl.CostEstimate(flops=0, bytes_accessed=moved, transcendentals=0)


def swap_core(cells):
    return lax.ppermute(cells, "core", [(0, 1), (1, 0)])


def shift_z(cells, by):
    return lax.ppermute(cells, "z", [(i, (i + by) % ZS) for i in range(ZS)])


def split(values):
    top = values.astype(jnp.bfloat16)
    return top, (values - top.astype(f32)).astype(jnp.bfloat16)


def dot3(a, b, dims):
    (a1, a2), (b1, b2) = split(a), split(b)
    mul = functools.partial(lax.dot_general, dimension_numbers=(dims, ((), ())), preferred_element_type=f32)
    both, rows = mul(jnp.concatenate([a1, a2], axis=0), b1), a.shape[0]
    return both[:rows] + (mul(a1, b2) + both[rows:])


def exchange(edges):
    return *exchange_rows(*edges[:2]), *exchange_cols(*edges[2:])


def exchange_rows(near, far):
    pairs = [(i, i + 1) for i in range(1, ZS * CORES - 1, 2)]
    return swap_core(near), lax.ppermute(far, ROW, pairs + [(b, a) for a, b in pairs])


def exchange_cols(head, tail):
    return (
        lax.ppermute(tail, COL, [(i, i + 1) for i in range(COLS - 1)]),
        lax.ppermute(head, COL, [(i + 1, i) for i in range(COLS - 1)]),
    )


def put_edges(first, cells, near_ref, far_ref, head_ref, tail_ref):
    rows, cols = cells.shape
    top, bottom = cells[0:1, :], cells[rows - 1 : rows, :]
    near_ref[...] = jnp.where(first, bottom, top)
    far_ref[...] = jnp.where(first, top, bottom)
    head_ref[...] = jnp.transpose(cells[:, :128])[0:1, :]
    tail_ref[...] = jnp.transpose(cells[:, cols - 128 :])[127:128, :]


def stencil(first, cells, near, far, left, right):
    rows, cols = cells.shape
    above, below = jnp.where(first, far, near), jnp.where(first, near, far)
    row = lax.broadcasted_iota(jnp.int32, cells.shape, 0)
    col = lax.broadcasted_iota(jnp.int32, cells.shape, 1)
    left = jnp.transpose(jnp.broadcast_to(left, (128, rows)))[:, 0:1]
    right = jnp.transpose(jnp.broadcast_to(right, (128, rows)))[:, 0:1]
    down = jnp.where(row == 0, above, pltpu.roll(cells, 1, 0))
    up = jnp.where(row == rows - 1, below, pltpu.roll(cells, rows - 1, 0))
    after = jnp.where(col == 0, left, pltpu.roll(cells, 1, 1))
    before = jnp.where(col == cols - 1, right, pltpu.roll(cells, cols - 1, 1))
    return 0.25 * (down + up + after + before) - cells


def halves(first, cells, mine_ref, other_ref, turn=True):
    half = cells.shape[1] // 2
    a, b = cells[:, :half], cells[:, half:]
    mine, other = jnp.where(first, a, b), jnp.where(first, b, a)
    mine_ref[...] = jnp.transpose(mine) if turn else mine
    other_ref[...] = jnp.transpose(other) if turn else other


def edge_kernel(core, yc, near, far, head, tail, held, sems):
    fetch([(yc, held)], sems)[0].wait()
    put_edges(core[1] == 0, held[...], near, far, head, tail)


def start_kernel(core, x, pupil_mask, lyot_mask, *refs):
    x_mine, x_other, stop_mine, stop_other, *held, sems = refs
    first = core[1] == 0
    copies = fetch(list(zip((x, pupil_mask, lyot_mask), held)), sems)
    copies[0].wait()
    halves(first, held[0][...], x_mine, x_other)
    copies[1].wait()
    copies[2].wait()
    halves(first, (held[1][...] * held[2][...]).astype(f32), stop_mine, stop_other)


def first_known_kernel(core, yc, pupil_mask, near, far, gathered, mine, other):
    place, slab = core[2], gathered.shape[1] - 1
    left = gathered[jnp.maximum(place - 1, 0), slab, 0:1]
    right = gathered[jnp.minimum(place + 1, COLS - 1), slab, 1:2]
    left = jnp.where(place > 0, left, 0.0)
    right = jnp.where(place < COLS - 1, right, 0.0)
    known_kernel(core, yc, pupil_mask, near, far, left, right, mine, other)


def known_kernel(core, yc, pupil_mask, near, far, left, right, *refs):
    mine, other = refs[-2:]
    first = core[1] == 0
    curved = stencil(first, yc[...], near[...], far[...], left[...], right[...])
    halves(first, curved - pupil_mask[...].astype(f32), mine, other)


def primal_kernel(core, new_a, new_b, far_a, far_b, x, out, near, far, head, tail):
    first = core[1] == 0
    mine = jnp.transpose(jnp.concatenate([new_a[...], new_b[...]], axis=0))
    other = jnp.transpose(jnp.concatenate([far_a[...], far_b[...]], axis=0))
    new = jnp.concatenate([jnp.where(first, mine, other), jnp.where(first, other, mine)], axis=1)
    out[...] = new
    put_edges(first, 2.0 * new - x[...], near, far, head, tail)


def dual_kernel(core, new, x, yc, near, far, left, right, out, *edges):
    first = core[1] == 0
    extended = 2.0 * new[...] - x[...]
    curved = stencil(first, extended, near[...], far[...], left[...], right[...])
    moved = yc[...] + step_dual * curved
    result = moved - step_dual * jnp.clip(moved / step_dual, -curvature_limit, curvature_limit)
    out[...] = result
    if edges:
        put_edges(first, result, *edges)


def focal_kernel(parts, yf, dark, out, *spread):
    fields = parts[0]
    for other in range(1, COLS):
        fields = fields + parts[other]
    shifted = yf[...] + step_dual * fields
    result = dark[...] * (shifted - step_dual * jnp.clip(shifted / step_dual, -contrast, contrast))
    out[...] = result
    if spread:
        for other in range(COLS):
            spread[0][other] = result


def fetch(pairs, sems):
    copies = [pltpu.make_async_copy(src, dst, sems.at[i]) for i, (src, dst) in enumerate(pairs)]
    for copy in copies:
        copy.start()
    return copies


def carry_kernel(core, y, table, mine, other, held, sems):
    waves, rows = table.shape[0], y.shape[0] * y.shape[2]
    copies = fetch([(table.at[w], held.at[w]) for w in range(waves)], sems)
    for w in range(waves):
        copies[w].wait()
        carried = dot3(y[:, w].reshape(rows, y.shape[3]), held[w], ((1,), (0,)))
        at = pl.ds(w * rows, rows)
        halves(core[1] == 0, carried, mine.at[at], other.at[at], turn=False)


def found_kernel(core, own_a, own_b, far_a, far_b, table, out):
    first = core[1] == 0
    waves, rows = out.shape[1], out.shape[0] * out.shape[2]
    for w in range(waves):
        at = pl.ds(w * rows, rows)
        own = jnp.concatenate([own_a[at, :], own_b[at, :]], axis=1)
        far = jnp.concatenate([far_a[at, :], far_b[at, :]], axis=1)
        left = jnp.concatenate([jnp.where(first, own, far), jnp.where(first, far, own)], axis=1)
        found = dot3(left, table[w], ((1,), (1,)))
        out[:, w] = found.reshape(out.shape[0], out.shape[2], out.shape[3])


def table_kernel(where, mine, other, top, rest, ready):
    ready[...] = jnp.zeros_like(ready)
    rows, b = mine.shape[3], pl.program_id(0)
    for at, block in ((0, mine), (rows, other)):
        large, small = split(block[:, 0].reshape(top.shape[1], rows))
        top[b, :, at : at + rows] = large
        rest[b, :, at : at + rows] = small


def back_kernel(t0, t1, t2, t3, top, rest, ready, out):
    for step, t in enumerate((t0, t1, t2, t3)):
        depth, wide = t.shape
        a, b = split(jnp.transpose(t[...]))
        blocks = slice(2 * step, 2 * step + 2)
        both = jnp.dot(
            jnp.concatenate([a, b], axis=0),
            top[blocks].reshape(depth, out.shape[1]),
            preferred_element_type=f32,
        )
        more = jnp.dot(a, rest[blocks].reshape(depth, out.shape[1]), preferred_element_type=f32)
        part = both[:wide] + (both[wide:] + more)
        out[...] = part if step == 0 else out[...] + part


def update_kernel(back, far, x0, x1, s0, s1, k0, k1, top, rest, new0, new1, l0, l1, l2, l3):
    rows = x0.shape[1]
    masked = []
    for i, (x, stop, known, new) in enumerate(((x0, s0, k0, new0), (x1, s1, k1, new1))):
        at = slice(i * rows, (i + 1) * rows)
        before = x[...]
        gradient = known[...] + stop[...] * (back[:, at] + far[:, at])
        after = jnp.clip(before - step_primal * gradient, 0.0, 1.0)
        new[...] = after
        masked.append(stop[...] * (2.0 * after - before))
    a, b = split(jnp.concatenate(masked, axis=1))
    both, wide = jnp.concatenate([a, b], axis=0), a.shape[0]
    dims = (((1,), (1,)), ((), ()))
    for step, left in enumerate((l0, l1, l2, l3)):
        depth = left.shape[0]
        blocks = slice(2 * step, 2 * step + 2)
        large = top[blocks].reshape(depth, both.shape[1])
        small = rest[blocks].reshape(depth, both.shape[1])
        one = lax.dot_general(large, both, dims, preferred_element_type=f32)
        two = lax.dot_general(small, a, dims, preferred_element_type=f32)
        left[...] = one[:, :wide] + (one[:, wide:] + two)


def results(shapes, far):
    kinds = [pltpu.HBM(shape, f32) if i in far else jax.ShapeDtypeStruct(shape, f32) for i, shape in enumerate(shapes)]
    places = [
        pl.BlockSpec(shape, lambda i, rank=len(shape): (0,) * rank) if i in far else in_vmem
        for i, shape in enumerate(shapes)
    ]
    return {"grid": (1,), "out_shape": kinds, "out_specs": places}


def whole(kernel, core, args, shapes, far=()):
    return pl.pallas_call(
        kernel,
        **results(shapes, far),
        in_specs=[in_smem] + [in_vmem] * len(args) if core is not None else [in_vmem] * len(args),
        cost_estimate=cost(2 << 20),
        compiler_params=pltpu.CompilerParams(vmem_limit_bytes=LIMIT),
    )(*(([core] if core is not None else []) + list(args)))


def per_device(
    transmission,
    dual_focal,
    dual_curvature,
    pupil_mask,
    lyot_mask,
    dark_mask,
    focal_rows,
    focal_cols,
):
    z = lax.axis_index("z").astype(jnp.int32)
    core = lax.axis_index("core").astype(jnp.int32)
    core = where = jnp.stack([z, core, lax.axis_index(COL).astype(jnp.int32)])
    waves, fields, rows = focal_rows.shape
    cols = focal_cols.shape[2]
    part = fields // (ZS * CORES)
    own = dual_focal.shape[0]
    count = waves * part
    half = cols // CORES
    wide = half // CHUNKS
    tile, line = (rows, cols), [(1, cols)] * 4
    piece = (half, rows)

    dark = jnp.transpose(dark_mask.astype(f32), (1, 0, 2))
    dual_f = jnp.transpose(dual_focal, (1, 0, 2)) * dark

    other_rows = swap_core(focal_rows)
    def started(kernel, inputs, shapes):
        return pl.pallas_call(
            kernel,
            out_shape=[jax.ShapeDtypeStruct(shape, f32) for shape in shapes],
            in_specs=[in_smem] + [in_hbm] * len(inputs),
            out_specs=[in_vmem] * len(shapes),
            scratch_shapes=[pltpu.VMEM(tile, cells.dtype) for cells in inputs]
            + [pltpu.SemaphoreType.DMA((len(inputs),))],
            cost_estimate=cost(2 << 20),
            compiler_params=pltpu.CompilerParams(vmem_limit_bytes=LIMIT),
        )(core, *(stay(cells) for cells in inputs))

    edges = started(edge_kernel, (dual_curvature,), line)

    def block_of(b, where):
        return (0, (where[0] + b // CORES) % ZS * CORES + (where[1] + b) % CORES, 0, 0)

    def table_of(mine, other):
        return pl.pallas_call(
            table_kernel,
            grid_spec=pltpu.PrefetchScalarGridSpec(
                num_scalar_prefetch=1,
                grid=(ZS * CORES,),
                in_specs=[pl.BlockSpec((waves, 1, part, rows), block_of)] * 2,
                out_specs=[in_vmem] * 3,
            ),
            out_shape=[pltpu.VMEM((ZS * CORES, count, 2 * rows), bf16)] * 2 + [jax.ShapeDtypeStruct((8, 128), f32)],
            cost_estimate=cost(20 << 20),
            compiler_params=pltpu.CompilerParams(vmem_limit_bytes=LIMIT),
        )(where, *(stay(half.reshape(waves, ZS * CORES, part, rows)) for half in (mine, other)))

    *table, ready = table_of(focal_rows, other_rows)
    table = [hold(half) for half in table]

    def known(yc, around, held=()):
        return whole(known_kernel, core, (yc, pupil_mask, *around, *held), [piece] * 2)

    def product(kernel, args, shapes, specs, moved, scratch=(), far=()):
        return pl.pallas_call(
            kernel,
            **results(shapes, far),
            in_specs=specs,
            scratch_shapes=list(scratch),
            cost_estimate=cost(moved << 20),
            compiler_params=pltpu.CompilerParams(vmem_limit_bytes=LIMIT),
        )(*args)

    def carry(gathered):
        specs = [in_smem, in_vmem, in_hbm]
        scratch = [pltpu.VMEM((waves, fields, cols), f32), pltpu.SemaphoreType.DMA((waves,))]
        args = (core, gathered, stay(focal_cols))
        return product(carry_kernel, args, [(count, half)] * 2, specs, 6, scratch)

    def find(sums, fars):
        specs = [in_smem] + [in_vmem] * 5
        args = (core, *sums, *fars, hold(focal_cols))
        return product(found_kernel, args, [(COLS, waves, own, fields)], specs, 8, far=(0,))[0]

    def gather(block):
        return block, shift_z(block, -1), shift_z(block, -2), shift_z(block, -3)

    def backward(full):
        specs = [in_vmem] * 7
        back = product(back_kernel, (*full, *table, ready), [(wide, CORES * rows)], specs, 2)[0]
        return back, lax.ppermute(back, "wave", [(0, 1), (1, 0)])

    def update(chunk, known_half, primal_half, stop_half, back, far):
        cut = pl.BlockSpec((wide, rows), lambda i: (chunk, 0))
        specs = [in_vmem] * 2 + [cut] * 6 + [in_vmem] * 2
        args = (back, far, *primal_half, *stop_half, *known_half, *table)
        shapes = [(wide, rows)] * 2 + [(CORES * count, wide)] * ZS
        new0, new1, *left = product(update_kernel, args, shapes, specs, 1)
        return (new0, new1), left

    def scatter(left):
        return left[0] + shift_z(left[1], 1) + shift_z(left[2], 2) + shift_z(left[3], 3)

    primal, dual_c = transmission, dual_curvature
    lines = jnp.concatenate([edges[3], edges[2], jnp.zeros((own - 2, fields), f32)], axis=0)
    spread = jnp.concatenate([dual_f, lines[None]], axis=0)
    spread = jnp.broadcast_to(spread[None], (COLS,) + spread.shape)
    gathered = lax.all_to_all(spread, COL, 0, 0, tiled=True)
    gathered, *around = tie((gathered, *exchange_rows(*edges[:2])))
    for iteration in range(ITERS):
        last = iteration == ITERS - 1
        mine, other = carry(gathered)
        received = swap_core(other)
        pair = jnp.concatenate([mine, received], axis=0)
        pair_a, pair_b = pair[:, :wide], pair[:, wide:]
        full_a = gather(pair_a)
        if iteration == 0:
            pair_b, ready = tie((pair_b, ready))
        else:
            mine, other = known(dual_c, around, table)
            last_a, mine, other = tie((full_a[3], mine, other))
            full_a = *full_a[:3], last_a
            known_half = mine, swap_core(other)
        full_b = gather(pair_b)
        back_a, far_a = backward(full_a)
        if iteration == 0:
            mine, other = whole(first_known_kernel, core, (dual_c, pupil_mask, *around, gathered), [piece] * 2)
            known_half = mine, swap_core(other)
        back_b, far_b = backward(full_b)
        if iteration == 0:
            back_b, shown = tie((back_b, transmission))
            inputs = (shown, pupil_mask, lyot_mask)
            x_mine, x_other, stop_mine, stop_other = started(start_kernel, inputs, [piece] * 4)
            primal_half = (x_mine, swap_core(x_other))
            stop_half = (stop_mine, swap_core(stop_other))
        far_a, back_b = tie((far_a, back_b))
        new_a, left_a = update(0, known_half, primal_half, stop_half, back_a, far_a)
        sum_a = scatter(left_a)
        far_b, new_a = tie((far_b, new_a))
        new_b, left_b = update(1, known_half, primal_half, stop_half, back_b, far_b)
        sum_b = scatter(left_b)

        moved = swap_core(new_a[1]), swap_core(new_b[1])
        sum_a, *moved = tie((sum_a, *moved))
        args = (new_a[0], new_b[0], *moved, primal)
        primal_new, *edges = whole(primal_kernel, core, args, [tile] + line)
        sum_a, sum_b, primal_new, *around = tie((sum_a, sum_b, primal_new, *exchange(edges)))

        fars = swap_core(sum_a[count:]), swap_core(sum_b[count:])
        found, *around = tie((find((sum_a[:count], sum_b[:count]), fars), *around))
        parts = lax.all_to_all(found, COL, 0, 0, tiled=True)
        args = (primal_new, primal, dual_c, *around)
        dual_c, *edges = whole(dual_kernel, core, args, [tile] + ([] if last else line), () if last else (0, 1, 2, 3, 4))
        primal = primal_new
        if last:
            parts, dual_c = tie((parts, dual_c))
            dual_f = whole(focal_kernel, None, (parts, dual_f, dark), [dual_f.shape])[0]
            break
        parts, dual_c, *around = tie((parts, dual_c, *exchange_rows(*edges[:2])))
        primal_half = tuple(jnp.concatenate(pieces, axis=0) for pieces in zip(new_a, new_b))
        dual_f, spread = whole(focal_kernel, None, (parts, dual_f, dark), [dual_f.shape, (COLS,) + dual_f.shape], (1,))
        gathered = lax.all_to_all(spread, COL, 0, 0, tiled=True)
        gathered, *around = tie((gathered, *around, *exchange_cols(*edges[2:])))
    return (primal, jnp.transpose(dual_f, (1, 0, 2)), dual_c)


def solution(mesh):
    parts = Mesh(
        mesh.devices.reshape(ZS, CORES, 2, COLS // 2, WAVES),
        ("z", "core", "xl", "y", "wave"),
    )
    return jax.shard_map(
        per_device,
        mesh=parts,
        in_specs=(
            P(ROW, COL),
            P(ROW + COL, "wave", None),
            P(ROW, COL),
            P(ROW, COL),
            P(ROW, COL),
            P(ROW + COL, "wave", None),
            P("wave", None, ROW),
            P("wave", None, COL),
        ),
        out_specs=(P(ROW, COL), P(ROW + COL, "wave", None), P(ROW, COL)),
        check_vma=False,
    )
```

```python
import functools

import jax
import jax.numpy as jnp
from jax import lax
from jax.experimental import pallas as pl
from jax.experimental.pallas import tpu as pltpu
from jax.sharding import Mesh, PartitionSpec as P

ITERS = 2

step_primal = 0.12
step_dual = 0.2
contrast = 0.5
curvature_limit = 0.1

ROW = ("z", "core")
COL = ("xl", "y")
ZS, CORES, COLS, WAVES = 4, 2, 8, 2
CHUNKS = 2
LIMIT = 16 * 1024 * 1024
f32 = jnp.float32
tie = lax.optimization_barrier
in_vmem = pl.BlockSpec(memory_space=pltpu.VMEM)
in_smem = pl.BlockSpec(memory_space=pltpu.SMEM)
in_hbm = pl.BlockSpec(memory_space=pltpu.HBM)
bf16 = jnp.bfloat16


def hold(cells):
    return pltpu.with_memory_space_constraint(cells, pltpu.VMEM)


def stay(cells):
    return pltpu.with_memory_space_constraint(cells, pltpu.HBM)


def cost(moved):
    return pl.CostEstimate(flops=0, bytes_accessed=moved, transcendentals=0)


def swap_core(cells):
    return lax.ppermute(cells, "core", [(0, 1), (1, 0)])


def shift_z(cells, by):
    return lax.ppermute(cells, "z", [(i, (i + by) % ZS) for i in range(ZS)])


def split(values):
    top = values.astype(jnp.bfloat16)
    return top, (values - top.astype(f32)).astype(jnp.bfloat16)


def dot3(a, b, dims):
    (a1, a2), (b1, b2) = split(a), split(b)
    mul = functools.partial(lax.dot_general, dimension_numbers=(dims, ((), ())), preferred_element_type=f32)
    both, rows = mul(jnp.concatenate([a1, a2], axis=0), b1), a.shape[0]
    return both[:rows] + (mul(a1, b2) + both[rows:])


def exchange(edges):
    return *exchange_rows(*edges[:2]), *exchange_cols(*edges[2:])


def exchange_rows(near, far):
    pairs = [(i, i + 1) for i in range(1, ZS * CORES - 1, 2)]
    return swap_core(near), lax.ppermute(far, ROW, pairs + [(b, a) for a, b in pairs])


def exchange_cols(head, tail):
    return (
        lax.ppermute(tail, COL, [(i, i + 1) for i in range(COLS - 1)]),
        lax.ppermute(head, COL, [(i + 1, i) for i in range(COLS - 1)]),
    )


def put_edges(first, cells, near_ref, far_ref, head_ref, tail_ref):
    rows, cols = cells.shape
    top, bottom = cells[0:1, :], cells[rows - 1 : rows, :]
    near_ref[...] = jnp.where(first, bottom, top)
    far_ref[...] = jnp.where(first, top, bottom)
    head_ref[...] = jnp.transpose(cells[:, :128])[0:1, :]
    tail_ref[...] = jnp.transpose(cells[:, cols - 128 :])[127:128, :]


def stencil(first, cells, near, far, left, right):
    rows, cols = cells.shape
    above, below = jnp.where(first, far, near), jnp.where(first, near, far)
    row = lax.broadcasted_iota(jnp.int32, cells.shape, 0)
    col = lax.broadcasted_iota(jnp.int32, cells.shape, 1)
    left = jnp.transpose(jnp.broadcast_to(left, (128, rows)))[:, 0:1]
    right = jnp.transpose(jnp.broadcast_to(right, (128, rows)))[:, 0:1]
    down = jnp.where(row == 0, above, pltpu.roll(cells, 1, 0))
    up = jnp.where(row == rows - 1, below, pltpu.roll(cells, rows - 1, 0))
    after = jnp.where(col == 0, left, pltpu.roll(cells, 1, 1))
    before = jnp.where(col == cols - 1, right, pltpu.roll(cells, cols - 1, 1))
    return 0.25 * (down + up + after + before) - cells


def halves(first, cells, mine_ref, other_ref, turn=True):
    half = cells.shape[1] // 2
    a, b = cells[:, :half], cells[:, half:]
    mine, other = jnp.where(first, a, b), jnp.where(first, b, a)
    mine_ref[...] = jnp.transpose(mine) if turn else mine
    other_ref[...] = jnp.transpose(other) if turn else other


def edge_kernel(core, yc, near, far, head, tail, held, sems):
    fetch([(yc, held)], sems)[0].wait()
    put_edges(core[1] == 0, held[...], near, far, head, tail)


def start_kernel(core, x, pupil_mask, lyot_mask, *refs):
    x_mine, x_other, stop_mine, stop_other, *held, sems = refs
    first = core[1] == 0
    copies = fetch(list(zip((x, pupil_mask, lyot_mask), held)), sems)
    copies[0].wait()
    halves(first, held[0][...], x_mine, x_other)
    copies[1].wait()
    copies[2].wait()
    halves(first, (held[1][...] * held[2][...]).astype(f32), stop_mine, stop_other)


def first_known_kernel(core, yc, pupil_mask, near, far, gathered, mine, other):
    place, slab = core[2], gathered.shape[1] - 1
    left = gathered[jnp.maximum(place - 1, 0), slab, 0:1]
    right = gathered[jnp.minimum(place + 1, COLS - 1), slab, 1:2]
    left = jnp.where(place > 0, left, 0.0)
    right = jnp.where(place < COLS - 1, right, 0.0)
    known_kernel(core, yc, pupil_mask, near, far, left, right, mine, other)


def known_kernel(core, yc, pupil_mask, near, far, left, right, *refs):
    mine, other = refs[-2:]
    first = core[1] == 0
    curved = stencil(first, yc[...], near[...], far[...], left[...], right[...])
    halves(first, curved - pupil_mask[...].astype(f32), mine, other)


def primal_kernel(core, new_a, new_b, far_a, far_b, x, out, near, far, head, tail):
    first = core[1] == 0
    mine = jnp.transpose(jnp.concatenate([new_a[...], new_b[...]], axis=0))
    other = jnp.transpose(jnp.concatenate([far_a[...], far_b[...]], axis=0))
    new = jnp.concatenate([jnp.where(first, mine, other), jnp.where(first, other, mine)], axis=1)
    out[...] = new
    put_edges(first, 2.0 * new - x[...], near, far, head, tail)


def dual_kernel(core, new, x, yc, near, far, left, right, out, *edges):
    first = core[1] == 0
    extended = 2.0 * new[...] - x[...]
    curved = stencil(first, extended, near[...], far[...], left[...], right[...])
    moved = yc[...] + step_dual * curved
    result = moved - step_dual * jnp.clip(moved / step_dual, -curvature_limit, curvature_limit)
    out[...] = result
    if edges:
        put_edges(first, result, *edges)


def focal_kernel(parts, yf, dark, out, *spread):
    fields = parts[0]
    for other in range(1, COLS):
        fields = fields + parts[other]
    shifted = yf[...] + step_dual * fields
    result = dark[...] * (shifted - step_dual * jnp.clip(shifted / step_dual, -contrast, contrast))
    out[...] = result
    if spread:
        for other in range(COLS):
            spread[0][other] = result


def fetch(pairs, sems):
    copies = [pltpu.make_async_copy(src, dst, sems.at[i]) for i, (src, dst) in enumerate(pairs)]
    for copy in copies:
        copy.start()
    return copies


def carry_kernel(core, y, table, mine, other, held, sems):
    waves, rows = table.shape[0], y.shape[0] * y.shape[2]
    copies = fetch([(table.at[w], held.at[w]) for w in range(waves)], sems)
    for w in range(waves):
        copies[w].wait()
        carried = dot3(y[:, w].reshape(rows, y.shape[3]), held[w], ((1,), (0,)))
        at = pl.ds(w * rows, rows)
        halves(core[1] == 0, carried, mine.at[at], other.at[at], turn=False)


def found_kernel(core, own_a, own_b, far_a, far_b, table, out):
    first = core[1] == 0
    waves, rows = out.shape[1], out.shape[0] * out.shape[2]
    for w in range(waves):
        at = pl.ds(w * rows, rows)
        own = jnp.concatenate([own_a[at, :], own_b[at, :]], axis=1)
        far = jnp.concatenate([far_a[at, :], far_b[at, :]], axis=1)
        left = jnp.concatenate([jnp.where(first, own, far), jnp.where(first, far, own)], axis=1)
        found = dot3(left, table[w], ((1,), (1,)))
        out[:, w] = found.reshape(out.shape[0], out.shape[2], out.shape[3])


def table_kernel(where, mine, other, top, rest, ready):
    ready[...] = jnp.zeros_like(ready)
    rows, b = mine.shape[3], pl.program_id(0)
    for at, block in ((0, mine), (rows, other)):
        large, small = split(block[:, 0].reshape(top.shape[1], rows))
        top[b, :, at : at + rows] = large
        rest[b, :, at : at + rows] = small


def back_kernel(t0, t1, t2, t3, top, rest, ready, out):
    for step, t in enumerate((t0, t1, t2, t3)):
        depth, wide = t.shape
        a, b = split(jnp.transpose(t[...]))
        blocks = slice(2 * step, 2 * step + 2)
        both = jnp.dot(
            jnp.concatenate([a, b], axis=0),
            top[blocks].reshape(depth, out.shape[1]),
            preferred_element_type=f32,
        )
        more = jnp.dot(a, rest[blocks].reshape(depth, out.shape[1]), preferred_element_type=f32)
        part = both[:wide] + (both[wide:] + more)
        out[...] = part if step == 0 else out[...] + part


def update_kernel(back, far, x0, x1, s0, s1, k0, k1, top, rest, new0, new1, l0, l1, l2, l3):
    rows = x0.shape[1]
    masked = []
    for i, (x, stop, known, new) in enumerate(((x0, s0, k0, new0), (x1, s1, k1, new1))):
        at = slice(i * rows, (i + 1) * rows)
        before = x[...]
        gradient = known[...] + stop[...] * (back[:, at] + far[:, at])
        after = jnp.clip(before - step_primal * gradient, 0.0, 1.0)
        new[...] = after
        masked.append(stop[...] * (2.0 * after - before))
    a, b = split(jnp.concatenate(masked, axis=1))
    both, wide = jnp.concatenate([a, b], axis=0), a.shape[0]
    dims = (((1,), (1,)), ((), ()))
    for step, left in enumerate((l0, l1, l2, l3)):
        depth = left.shape[0]
        blocks = slice(2 * step, 2 * step + 2)
        large = top[blocks].reshape(depth, both.shape[1])
        small = rest[blocks].reshape(depth, both.shape[1])
        one = lax.dot_general(large, both, dims, preferred_element_type=f32)
        two = lax.dot_general(small, a, dims, preferred_element_type=f32)
        left[...] = one[:, :wide] + (one[:, wide:] + two)


def results(shapes, far):
    kinds = [pltpu.HBM(shape, f32) if i in far else jax.ShapeDtypeStruct(shape, f32) for i, shape in enumerate(shapes)]
    places = [
        pl.BlockSpec(shape, lambda i, rank=len(shape): (0,) * rank) if i in far else in_vmem
        for i, shape in enumerate(shapes)
    ]
    return {"grid": (1,), "out_shape": kinds, "out_specs": places}


def whole(kernel, core, args, shapes, far=()):
    return pl.pallas_call(
        kernel,
        **results(shapes, far),
        in_specs=[in_smem] + [in_vmem] * len(args) if core is not None else [in_vmem] * len(args),
        cost_estimate=cost(2 << 20),
        compiler_params=pltpu.CompilerParams(vmem_limit_bytes=LIMIT),
    )(*(([core] if core is not None else []) + list(args)))


def per_device(
    transmission,
    dual_focal,
    dual_curvature,
    pupil_mask,
    lyot_mask,
    dark_mask,
    focal_rows,
    focal_cols,
):
    z = lax.axis_index("z").astype(jnp.int32)
    core = lax.axis_index("core").astype(jnp.int32)
    core = where = jnp.stack([z, core, lax.axis_index(COL).astype(jnp.int32)])
    waves, fields, rows = focal_rows.shape
    cols = focal_cols.shape[2]
    part = fields // (ZS * CORES)
    own = dual_focal.shape[0]
    count = waves * part
    half = cols // CORES
    wide = half // CHUNKS
    tile, line = (rows, cols), [(1, cols)] * 4
    piece = (half, rows)

    dark = jnp.transpose(dark_mask.astype(f32), (1, 0, 2))
    dual_f = jnp.transpose(dual_focal, (1, 0, 2)) * dark

    other_rows = swap_core(focal_rows)
    def started(kernel, inputs, shapes):
        return pl.pallas_call(
            kernel,
            out_shape=[jax.ShapeDtypeStruct(shape, f32) for shape in shapes],
            in_specs=[in_smem] + [in_hbm] * len(inputs),
            out_specs=[in_vmem] * len(shapes),
            scratch_shapes=[pltpu.VMEM(tile, cells.dtype) for cells in inputs]
            + [pltpu.SemaphoreType.DMA((len(inputs),))],
            cost_estimate=cost(2 << 20),
            compiler_params=pltpu.CompilerParams(vmem_limit_bytes=LIMIT),
        )(core, *(stay(cells) for cells in inputs))

    edges = started(edge_kernel, (dual_curvature,), line)

    def block_of(b, where):
        return (0, (where[0] + b // CORES) % ZS * CORES + (where[1] + b) % CORES, 0, 0)

    def table_of(mine, other):
        return pl.pallas_call(
            table_kernel,
            grid_spec=pltpu.PrefetchScalarGridSpec(
                num_scalar_prefetch=1,
                grid=(ZS * CORES,),
                in_specs=[pl.BlockSpec((waves, 1, part, rows), block_of)] * 2,
                out_specs=[in_vmem] * 3,
            ),
            out_shape=[pltpu.VMEM((ZS * CORES, count, 2 * rows), bf16)] * 2 + [jax.ShapeDtypeStruct((8, 128), f32)],
            cost_estimate=cost(20 << 20),
            compiler_params=pltpu.CompilerParams(vmem_limit_bytes=LIMIT),
        )(where, *(stay(half.reshape(waves, ZS * CORES, part, rows)) for half in (mine, other)))

    *table, ready = table_of(focal_rows, other_rows)
    table = [hold(half) for half in table]

    def known(yc, around, held=()):
        return whole(known_kernel, core, (yc, pupil_mask, *around, *held), [piece] * 2)

    def product(kernel, args, shapes, specs, moved, scratch=(), far=()):
        return pl.pallas_call(
            kernel,
            **results(shapes, far),
            in_specs=specs,
            scratch_shapes=list(scratch),
            cost_estimate=cost(moved << 20),
            compiler_params=pltpu.CompilerParams(vmem_limit_bytes=LIMIT),
        )(*args)

    def carry(gathered):
        specs = [in_smem, in_vmem, in_hbm]
        scratch = [pltpu.VMEM((waves, fields, cols), f32), pltpu.SemaphoreType.DMA((waves,))]
        args = (core, gathered, stay(focal_cols))
        return product(carry_kernel, args, [(count, half)] * 2, specs, 6, scratch)

    def find(sums, fars):
        specs = [in_smem] + [in_vmem] * 5
        args = (core, *sums, *fars, hold(focal_cols))
        return product(found_kernel, args, [(COLS, waves, own, fields)], specs, 8, far=(0,))[0]

    def gather(block):
        return block, shift_z(block, -1), shift_z(block, -2), shift_z(block, -3)

    def backward(full):
        specs = [in_vmem] * 7
        back = product(back_kernel, (*full, *table, ready), [(wide, CORES * rows)], specs, 2)[0]
        return back, lax.ppermute(back, "wave", [(0, 1), (1, 0)])

    def update(chunk, known_half, primal_half, stop_half, back, far):
        cut = pl.BlockSpec((wide, rows), lambda i: (chunk, 0))
        specs = [in_vmem] * 2 + [cut] * 6 + [in_vmem] * 2
        args = (back, far, *primal_half, *stop_half, *known_half, *table)
        shapes = [(wide, rows)] * 2 + [(CORES * count, wide)] * ZS
        new0, new1, *left = product(update_kernel, args, shapes, specs, 1)
        return (new0, new1), left

    def scatter(left):
        return left[0] + shift_z(left[1], 1) + shift_z(left[2], 2) + shift_z(left[3], 3)

    primal, dual_c = transmission, dual_curvature
    lines = jnp.concatenate([edges[3], edges[2], jnp.zeros((own - 2, fields), f32)], axis=0)
    spread = jnp.concatenate([dual_f, lines[None]], axis=0)
    spread = jnp.broadcast_to(spread[None], (COLS,) + spread.shape)
    gathered = lax.all_to_all(spread, COL, 0, 0, tiled=True)
    gathered, *around = tie((gathered, *exchange_rows(*edges[:2])))
    for iteration in range(ITERS):
        last = iteration == ITERS - 1
        mine, other = carry(gathered)
        received = swap_core(other)
        pair = jnp.concatenate([mine, received], axis=0)
        pair_a, pair_b = pair[:, :wide], pair[:, wide:]
        full_a = gather(pair_a)
        if iteration == 0:
            pair_b, ready = tie((pair_b, ready))
        else:
            mine, other = known(dual_c, around, table)
            last_a, mine, other = tie((full_a[3], mine, other))
            full_a = *full_a[:3], last_a
            known_half = mine, swap_core(other)
        full_b = gather(pair_b)
        back_a, far_a = backward(full_a)
        if iteration == 0:
            back_a, shown = tie((back_a, dual_c))
            mine, other = whole(first_known_kernel, core, (shown, pupil_mask, *around, gathered), [piece] * 2)
            known_half = mine, swap_core(other)
        back_b, far_b = backward(full_b)
        if iteration == 0:
            back_b, shown = tie((back_b, transmission))
            inputs = (shown, pupil_mask, lyot_mask)
            x_mine, x_other, stop_mine, stop_other = started(start_kernel, inputs, [piece] * 4)
            primal_half = (x_mine, swap_core(x_other))
            stop_half = (stop_mine, swap_core(stop_other))
        far_a, back_b = tie((far_a, back_b))
        new_a, left_a = update(0, known_half, primal_half, stop_half, back_a, far_a)
        sum_a = scatter(left_a)
        far_b, new_a = tie((far_b, new_a))
        new_b, left_b = update(1, known_half, primal_half, stop_half, back_b, far_b)
        sum_b = scatter(left_b)

        moved = swap_core(new_a[1]), swap_core(new_b[1])
        sum_a, *moved = tie((sum_a, *moved))
        args = (new_a[0], new_b[0], *moved, primal)
        primal_new, *edges = whole(primal_kernel, core, args, [tile] + line)
        sum_a, sum_b, primal_new, *around = tie((sum_a, sum_b, primal_new, *exchange(edges)))

        fars = swap_core(sum_a[count:]), swap_core(sum_b[count:])
        found, *around = tie((find((sum_a[:count], sum_b[:count]), fars), *around))
        parts = lax.all_to_all(found, COL, 0, 0, tiled=True)
        args = (primal_new, primal, dual_c, *around)
        dual_c, *edges = whole(dual_kernel, core, args, [tile] + ([] if last else line), () if last else (0, 1, 2, 3, 4))
        primal = primal_new
        if last:
            parts, dual_c = tie((parts, dual_c))
            dual_f = whole(focal_kernel, None, (parts, dual_f, dark), [dual_f.shape])[0]
            break
        parts, dual_c, *around = tie((parts, dual_c, *exchange_rows(*edges[:2])))
        primal_half = tuple(jnp.concatenate(pieces, axis=0) for pieces in zip(new_a, new_b))
        dual_f, spread = whole(focal_kernel, None, (parts, dual_f, dark), [dual_f.shape, (COLS,) + dual_f.shape], (1,))
        gathered = lax.all_to_all(spread, COL, 0, 0, tiled=True)
        gathered, *around = tie((gathered, *around, *exchange_cols(*edges[2:])))
    return (primal, jnp.transpose(dual_f, (1, 0, 2)), dual_c)


def solution(mesh):
    parts = Mesh(
        mesh.devices.reshape(ZS, CORES, 2, COLS // 2, WAVES),
        ("z", "core", "xl", "y", "wave"),
    )
    return jax.shard_map(
        per_device,
        mesh=parts,
        in_specs=(
            P(ROW, COL),
            P(ROW + COL, "wave", None),
            P(ROW, COL),
            P(ROW, COL),
            P(ROW, COL),
            P(ROW + COL, "wave", None),
            P("wave", None, ROW),
            P("wave", None, COL),
        ),
        out_specs=(P(ROW, COL), P(ROW + COL, "wave", None), P(ROW, COL)),
        check_vma=False,
    )
```
